32 devices in a mesh: img: 4 (over y, x), txt: 8 (over z, core).
Axes of the slice: x: 2, y: 2, z: 4, core: 2. Of those that a mesh axis runs over, the one named last changes fastest.
Arguments:
- images: float32 [2048, 1152], P('txt'), may hold values from -520 to 520, as said below
- texts: float32 [2048, 1152], P(('img', 'txt')), may hold values from -520 to 520, as said below
- perm: int32 [2048], P('txt'), may hold values from 0 to 2047, each once
- scale: float32 [1], replicated, may hold values from 6 to 12
- shift: float32 [1], replicated, may hold values from -3 to -1
Outputs:
- grad_images: float32 [2048, 1152], P('txt')
- grad_texts: float32 [2048, 1152], P(('img', 'txt'))
The draws below stay inside these ranges and needn't reach their ends.
Inputs may be any that keep to these rules, and one draw needn't show every extreme that they name: `images`: every row has nonzero entries. `texts`: every row has nonzero entries.
All inputs are finite; a program needn't handle non-finite values.
Results may differ from the reference program's by a relative error of at most 0.0043.
Values may be sent and summed in bfloat16 or wider, within the bound.
No kernel may reach another device: no remote copies, remote signals or barrier semaphores. Data moves between devices by JAX's collectives and lax.ppermute only.
A program may use at most 64 MiB of HBM per device.

```python
import math
import jax
import jax.numpy as jnp
from jax import lax

D = 1152
PAIRS = 2048


def spread_scales(entries, key_rows, key_cols, top):
    rows = entries.shape[0]
    width = entries.shape[1]
    row_scale = jnp.exp(jax.random.uniform(key_rows, (rows, 1), jnp.float32) * math.log(top))
    col_scale = jnp.exp(jax.random.uniform(key_cols, (1, width), jnp.float32) * math.log(10.0))
    return entries * row_scale * col_scale


def draw_images(key, part):
    key = jax.random.fold_in(key, 1)
    first, second, third = jax.random.split(key, 3)
    entries = jnp.clip(jax.random.normal(first, (PAIRS, D), jnp.float32), -4.0, 4.0)
    top = 10.0
    return spread_scales(entries, second, third, top)


def draw_texts(key, part):
    key = jax.random.fold_in(key, 2)
    first, second, third = jax.random.split(key, 3)
    entries = jnp.clip(jax.random.normal(first, (PAIRS, D), jnp.float32), -4.0, 4.0)
    top = 10.0
    return spread_scales(entries, second, third, top)


def setup_inputs(seed: int = 0) -> dict:
    arg_keys = jax.random.split(jax.random.key(seed), 6)
    return {
        "images": draw_images(jax.random.fold_in(arg_keys[5], 71), 0),
        "texts": draw_texts(jax.random.fold_in(arg_keys[5], 71), 0),
        "perm": jax.random.permutation(arg_keys[2], PAIRS).astype(jnp.int32),
        "scale": jnp.clip(jax.random.uniform(arg_keys[3], (1,), jnp.float32, 6.0, 12.0), 6.0, 12.0),
        "shift": jnp.clip(jax.random.uniform(arg_keys[4], (1,), jnp.float32, -3.0, -1.0), -3.0, -1.0),
    }


EPSILON = 1e-06

def unit_rows(values):
    inverse = lax.rsqrt(lax.optimization_barrier(jnp.sum(values * values, axis=1, keepdims=True)) + EPSILON)
    return (values * inverse, inverse)

def backward_unit(unit, inverse, upstream):
    return inverse * (upstream - unit * lax.optimization_barrier(jnp.sum(unit * upstream, axis=1, keepdims=True)))

def reference(images, texts, perm, scale, shift):
    factor = scale[0]
    offset = shift[0]
    img_unit, img_inv = unit_rows(images)
    txt_unit, txt_inv = unit_rows(texts)
    img_bf = img_unit.astype(jnp.bfloat16)
    txt_wide = txt_unit.astype(jnp.bfloat16).astype(jnp.float32)
    block = math.gcd(PAIRS, 512)
    count = PAIRS // block
    image_blocks = img_bf.reshape(count, block, D)
    pair_blocks = perm.reshape(count, block)
    text_ids = jnp.arange(PAIRS, dtype=jnp.int32)

    def step(text_acc, item):
        rows_bf, paired = item
        rows_wide = rows_bf.astype(jnp.float32)
        logits = factor * jnp.dot(rows_wide, txt_wide.T) + offset
        positive = (paired[:, None] == text_ids[None, :]).astype(jnp.float32)
        weights = (jax.nn.sigmoid(logits) - positive).astype(jnp.bfloat16).astype(jnp.float32)
        to_images = jnp.dot(weights, txt_wide)
        return (text_acc + jnp.dot(weights.T, rows_wide), to_images)
    text_acc, image_parts = lax.scan(step, jnp.zeros((PAIRS, D), jnp.float32), (image_blocks, pair_blocks))
    image_acc = image_parts.reshape(PAIRS, D)
    grad_images = backward_unit(img_unit, img_inv, factor * image_acc)
    grad_texts = backward_unit(txt_unit, txt_inv, factor * text_acc)
    return (grad_images, grad_texts)
```

```python
import functools

import jax
import jax.numpy as jnp
from jax import lax
from jax.experimental import pallas as pl
from jax.experimental.pallas import tpu as pltpu
from jax.sharding import PartitionSpec as P

EPSILON = 1e-06
F32 = jnp.float32
BF16 = jnp.bfloat16
VMEM = pl.BlockSpec(memory_space=pltpu.VMEM)
SMEM = pl.BlockSpec(memory_space=pltpu.SMEM)


def call(body, outs, args, specs, limit, flops):
    size = sum(a.size * a.dtype.itemsize for a in args)
    size += sum(o.size * o.dtype.itemsize for o in outs)
    return pl.pallas_call(
        body,
        out_shape=outs,
        in_specs=specs,
        out_specs=[VMEM] * len(outs),
        compiler_params=pltpu.CompilerParams(vmem_limit_bytes=limit),
        cost_estimate=pl.CostEstimate(flops=flops, bytes_accessed=size, transcendentals=0),
    )(*args)


def struct(rows, cols, dtype):
    return jax.ShapeDtypeStruct((rows, cols), dtype)


def inverse_norm(values):
    return lax.rsqrt(jnp.sum(values * values, axis=1, keepdims=True) + EPSILON)


def backward_unit(values, upstream):
    inverse = inverse_norm(values)
    unit = values * inverse
    return inverse * (upstream - unit * jnp.sum(unit * upstream, axis=1, keepdims=True))


def unit_body(img_ref, txt_ref, img_out, txt_out):
    txt = txt_ref[...]
    txt_out[...] = (txt * inverse_norm(txt)).astype(BF16)
    img = img_ref[...]
    img_out[...] = (img * inverse_norm(img)).astype(BF16)


def pair_body(blocks, scalars, factors, perm_own, perm_other, img_own, img_other, *refs):
    txt = refs[:blocks]
    own_img, other_img, own_txt = refs[blocks : blocks + 3]
    other_txt = refs[blocks + 3 :]
    factor = factors[0]
    offset = factors[1]
    rows = txt[0].shape[0]
    tile = jnp.concatenate([t[...] for t in txt], axis=0)
    row = lax.broadcasted_iota(jnp.int32, (rows, 1), 0)
    ids = jnp.concatenate([row + scalars[k] for k in range(blocks)], axis=0)

    def weights(img, perm):
        logits = (
            factor
            * lax.dot_general(tile, img[...], (((1,), (1,)), ((), ())), preferred_element_type=F32)
            + offset
        )
        positive = (ids == perm[...]).astype(F32)
        return (jax.nn.sigmoid(logits) - positive).astype(BF16)

    w_other = weights(img_other, perm_other)
    other_img[...] = lax.dot_general(
        w_other, tile, (((0,), (0,)), ((), ())), preferred_element_type=F32
    ).astype(BF16)
    w_own = weights(img_own, perm_own)
    own_img[...] = lax.dot_general(
        w_own, tile, (((0,), (0,)), ((), ())), preferred_element_type=F32
    )
    to_txt = jnp.dot(w_own, img_own[...], preferred_element_type=F32) + jnp.dot(
        w_other, img_other[...], preferred_element_type=F32
    )
    own_txt[...] = to_txt[:rows]
    for k in range(1, blocks):
        other_txt[k - 1][...] = to_txt[k * rows : (k + 1) * rows].astype(BF16)


def split_body(count, position, own, other, keep, *send):
    rows = keep.shape[0]
    for k in range(count):
        start = pl.multiple_of(lax.rem(position[0] + k, count) * rows, rows)
        part = own[pl.ds(start, rows), :] + other[pl.ds(start, rows), :].astype(F32)
        if k == 0:
            keep[...] = part
        else:
            send[k - 1][...] = part.astype(BF16)


def total_of(own, parts):
    total = own[...]
    for part in parts:
        total = total + part[...].astype(F32)
    return total


def finish_img_body(position, factors, img_ref, own, *refs):
    *parts, out = refs
    rows = own.shape[0]
    start = pl.multiple_of(position[0] * rows, rows)
    upstream = factors[0] * total_of(own, parts)
    out[...] = backward_unit(img_ref[pl.ds(start, rows), :], upstream).astype(BF16)


def finish_txt_body(factors, txt_ref, own, *refs):
    *parts, out = refs
    out[...] = backward_unit(txt_ref[...], factors[0] * total_of(own, parts))


def join_body(count, position, *refs):
    *parts, out = refs
    rows = parts[0].shape[0]
    for k in range(count):
        start = pl.multiple_of(lax.rem(position[0] + count - k, count) * rows, rows)
        out[pl.ds(start, rows), :] = parts[k][...].astype(F32)


def shifted(value, axis, steps):
    count = lax.axis_size(axis)
    return lax.ppermute(value, axis, [(s, (s + steps) % count) for s in range(count)])


def swapped(value):
    count = lax.axis_size("txt")
    return lax.ppermute(value, "txt", [(s, s ^ 1) for s in range(count)])


def local(images, texts, perm, scale, shift):
    rows, width = images.shape
    txt_rows = texts.shape[0]
    line = lax.axis_size("txt")
    blocks = line // 2
    count = lax.axis_size("img")
    part = rows // count
    column = lax.axis_index("txt")
    place = lax.axis_index("img")
    position = place.reshape(1).astype(jnp.int32)
    factors = jnp.concatenate([scale, shift])
    perm_row = perm.reshape(1, rows)

    img_bf, txt_bf = call(
        unit_body,
        [struct(rows, width, BF16), struct(txt_rows, width, BF16)],
        [images, texts],
        [VMEM] * 2,
        16 << 20,
        4 * rows * width,
    )
    tiles = [txt_bf] + [shifted(txt_bf, "txt", 2 * k) for k in range(1, blocks)]
    img_other = swapped(img_bf)
    perm_other = swapped(perm_row)
    firsts = jnp.stack(
        [(place * line + (column - 2 * k) % line) * txt_rows for k in range(blocks)]
    ).astype(jnp.int32)
    own_img, other_img, own_txt, *other_txt = call(
        functools.partial(pair_body, blocks),
        [struct(rows, width, F32), struct(rows, width, BF16), struct(txt_rows, width, F32)]
        + [struct(txt_rows, width, BF16)] * (blocks - 1),
        [firsts, factors, perm_row, perm_other, img_bf, img_other, *tiles],
        [SMEM] * 2 + [VMEM] * (4 + blocks),
        48 << 20,
        12 * rows * blocks * txt_rows * width,
    )
    from_other = swapped(other_img)
    back = [shifted(other_txt[k - 1], "txt", -2 * k) for k in range(1, blocks)]

    keep, *send = call(
        functools.partial(split_body, count),
        [struct(part, width, F32)] + [struct(part, width, BF16)] * (count - 1),
        [position, own_img, from_other],
        [SMEM, VMEM, VMEM],
        24 << 20,
        rows * width,
    )
    got = [shifted(send[k - 1], "img", k) for k in range(1, count)]
    (grad_part,) = call(
        finish_img_body,
        [struct(part, width, BF16)],
        [position, factors, images, keep, *got],
        [SMEM] * 2 + [VMEM] * (1 + count),
        24 << 20,
        10 * part * width,
    )
    grads = [grad_part] + [shifted(grad_part, "img", k) for k in range(1, count)]
    (grad_images,) = call(
        functools.partial(join_body, count),
        [struct(rows, width, F32)],
        [position, *grads],
        [SMEM] + [VMEM] * count,
        24 << 20,
        rows * width,
    )
    (grad_texts,) = call(
        finish_txt_body,
        [struct(txt_rows, width, F32)],
        [factors, texts, own_txt, *back],
        [SMEM] + [VMEM] * (1 + blocks),
        24 << 20,
        10 * txt_rows * width,
    )
    return (grad_images, grad_texts)


def solution(mesh):
    placed = (P("txt", None), P(("img", "txt"), None), P("txt"), P(), P())
    return jax.shard_map(
        local,
        mesh=mesh,
        in_specs=placed,
        out_specs=(P("txt", None), P(("img", "txt"), None)),
        check_vma=False,
    )
```

```python
import functools

import jax
import jax.numpy as jnp
from jax import lax
from jax.experimental import pallas as pl
from jax.experimental.pallas import tpu as pltpu
from jax.sharding import PartitionSpec as P

EPSILON = 1e-06
F32 = jnp.float32
BF16 = jnp.bfloat16
VMEM = pl.BlockSpec(memory_space=pltpu.VMEM)
SMEM = pl.BlockSpec(memory_space=pltpu.SMEM)


def unit_rows(texts, images):
    sizes = [texts.shape, images.shape]
    total = texts.size + images.size
    return pl.pallas_call(
        unit_body,
        out_shape=[struct(*size, BF16) for size in sizes],
        in_specs=[pl.BlockSpec(memory_space=pltpu.HBM)] * 2,
        out_specs=[VMEM] * 2,
        scratch_shapes=[pltpu.VMEM(size, F32) for size in sizes] + [pltpu.SemaphoreType.DMA((2,))],
        compiler_params=pltpu.CompilerParams(vmem_limit_bytes=16 << 20),
        cost_estimate=pl.CostEstimate(flops=4 * total, bytes_accessed=6 * total, transcendentals=0),
    )(*[pltpu.with_memory_space_constraint(v, pltpu.HBM) for v in (texts, images)])


def call(body, outs, args, specs, limit, flops):
    size = sum(a.size * a.dtype.itemsize for a in args)
    size += sum(o.size * o.dtype.itemsize for o in outs)
    return pl.pallas_call(
        body,
        out_shape=outs,
        in_specs=specs,
        out_specs=[VMEM] * len(outs),
        compiler_params=pltpu.CompilerParams(vmem_limit_bytes=limit),
        cost_estimate=pl.CostEstimate(flops=flops, bytes_accessed=size, transcendentals=0),
    )(*args)


def struct(rows, cols, dtype):
    return jax.ShapeDtypeStruct((rows, cols), dtype)


def inverse_norm(values):
    return lax.rsqrt(jnp.sum(values * values, axis=1, keepdims=True) + EPSILON)


def backward_unit(values, upstream):
    inverse = inverse_norm(values)
    unit = values * inverse
    return inverse * (upstream - unit * jnp.sum(unit * upstream, axis=1, keepdims=True))


def unit_body(txt, img, txt_out, img_out, txt_held, img_held, sems):
    txt_copy = pltpu.make_async_copy(txt, txt_held, sems.at[0])
    img_copy = pltpu.make_async_copy(img, img_held, sems.at[1])
    txt_copy.start()
    img_copy.start()
    txt_copy.wait()
    values = txt_held[...]
    txt_out[...] = (values * inverse_norm(values)).astype(BF16)
    img_copy.wait()
    values = img_held[...]
    img_out[...] = (values * inverse_norm(values)).astype(BF16)


def weights_of(tile, scalars, factors, perm, img):
    rows = tile.shape[0] // scalars.shape[0]
    row = lax.broadcasted_iota(jnp.int32, (rows, 1), 0)
    ids = jnp.concatenate([row + scalars[k] for k in range(scalars.shape[0])], axis=0)
    products = lax.dot_general(tile, img, (((1,), (1,)), ((), ())), preferred_element_type=F32)
    positive = (ids == perm).astype(F32)
    return (jax.nn.sigmoid(factors[0] * products + factors[1]) - positive).astype(BF16)


def to_images(weights, tile):
    return lax.dot_general(weights, tile, (((0,), (0,)), ((), ())), preferred_element_type=F32)


def other_body(blocks, scalars, factors, perm, img, *refs):
    *txt, kept, out = refs
    tile = jnp.concatenate([t[...] for t in txt], axis=0)
    weights = weights_of(tile, scalars, factors, perm[...], img[...])
    kept[...] = weights
    out[...] = to_images(weights, tile).astype(BF16)


def own_body(blocks, scalars, factors, perm, img_own, img_other, kept, *refs):
    txt = refs[:blocks]
    own_img, own_txt, *other_txt = refs[blocks:]
    rows = own_txt.shape[0]
    tile = jnp.concatenate([t[...] for t in txt], axis=0)
    weights = weights_of(tile, scalars, factors, perm[...], img_own[...])
    own_img[...] = to_images(weights, tile)
    to_txt = jnp.dot(weights, img_own[...], preferred_element_type=F32) + jnp.dot(
        kept[...], img_other[...], preferred_element_type=F32
    )
    own_txt[...] = to_txt[:rows]
    for k in range(1, blocks):
        other_txt[k - 1][...] = to_txt[k * rows : (k + 1) * rows].astype(BF16)


def split_body(count, position, own, other, keep, *send):
    rows = keep.shape[0]
    for k in range(count):
        start = pl.multiple_of(lax.rem(position[0] + k, count) * rows, rows)
        part = own[pl.ds(start, rows), :] + other[pl.ds(start, rows), :].astype(F32)
        if k == 0:
            keep[...] = part
        else:
            send[k - 1][...] = part.astype(BF16)


def total_of(own, parts):
    total = own[...]
    for part in parts:
        total = total + part[...].astype(F32)
    return total


def finish_img_body(position, factors, img_ref, own, *refs):
    *parts, out = refs
    rows = own.shape[0]
    start = pl.multiple_of(position[0] * rows, rows)
    upstream = factors[0] * total_of(own, parts)
    out[...] = backward_unit(img_ref[pl.ds(start, rows), :], upstream).astype(BF16)


def finish_txt_body(factors, txt_ref, own, *refs):
    *parts, out = refs
    out[...] = backward_unit(txt_ref[...], factors[0] * total_of(own, parts))


def join_body(count, position, *refs):
    *parts, out = refs
    rows = parts[0].shape[0]
    for k in range(count):
        start = pl.multiple_of(lax.rem(position[0] + count - k, count) * rows, rows)
        out[pl.ds(start, rows), :] = parts[k][...].astype(F32)


def shifted(value, axis, steps):
    count = lax.axis_size(axis)
    return lax.ppermute(value, axis, [(s, (s + steps) % count) for s in range(count)])


def swapped(value):
    count = lax.axis_size("txt")
    return lax.ppermute(value, "txt", [(s, s ^ 1) for s in range(count)])


def local(images, texts, perm, scale, shift):
    rows, width = images.shape
    txt_rows = texts.shape[0]
    line = lax.axis_size("txt")
    blocks = line // 2
    count = lax.axis_size("img")
    part = rows // count
    column = lax.axis_index("txt")
    place = lax.axis_index("img")
    position = place.reshape(1).astype(jnp.int32)
    factors = jnp.concatenate([scale, shift])
    perm_row = perm.reshape(1, rows)

    txt_bf, img_bf = unit_rows(texts, images)
    tiles = [txt_bf] + [shifted(txt_bf, "txt", 2 * k) for k in range(1, blocks)]
    perm_other = swapped(perm_row)
    img_other = swapped(img_bf)
    firsts = jnp.stack(
        [(place * line + (column - 2 * k) % line) * txt_rows for k in range(blocks)]
    ).astype(jnp.int32)
    pairs = 2 * rows * blocks * txt_rows * width
    kept, other_img = call(
        functools.partial(other_body, blocks),
        [struct(blocks * txt_rows, rows, BF16), struct(rows, width, BF16)],
        [firsts, factors, perm_other, img_other, *tiles],
        [SMEM] * 2 + [VMEM] * (2 + blocks),
        40 << 20,
        2 * pairs,
    )
    from_other = swapped(other_img)
    own_img, own_txt, *other_txt = call(
        functools.partial(own_body, blocks),
        [struct(rows, width, F32), struct(txt_rows, width, F32)]
        + [struct(txt_rows, width, BF16)] * (blocks - 1),
        [firsts, factors, perm_row, img_bf, img_other, kept, *tiles],
        [SMEM] * 2 + [VMEM] * (4 + blocks),
        40 << 20,
        4 * pairs,
    )
    back = [shifted(other_txt[k - 1], "txt", -2 * k) for k in range(1, blocks)]

    keep, *send = call(
        functools.partial(split_body, count),
        [struct(part, width, F32)] + [struct(part, width, BF16)] * (count - 1),
        [position, own_img, from_other],
        [SMEM, VMEM, VMEM],
        24 << 20,
        rows * width,
    )
    got = [shifted(send[k - 1], "img", k) for k in range(1, count)]
    (grad_part,) = call(
        finish_img_body,
        [struct(part, width, BF16)],
        [position, factors, images, keep, *got],
        [SMEM] * 2 + [VMEM] * (1 + count),
        24 << 20,
        10 * part * width,
    )
    grads = [grad_part] + [shifted(grad_part, "img", k) for k in range(1, count)]
    (grad_images,) = call(
        functools.partial(join_body, count),
        [struct(rows, width, F32)],
        [position, *grads],
        [SMEM] + [VMEM] * count,
        24 << 20,
        rows * width,
    )
    (grad_texts,) = call(
        finish_txt_body,
        [struct(txt_rows, width, F32)],
        [factors, texts, own_txt, *back],
        [SMEM] + [VMEM] * (1 + blocks),
        24 << 20,
        10 * txt_rows * width,
    )
    return (grad_images, grad_texts)


def solution(mesh):
    placed = (P("txt", None), P(("img", "txt"), None), P("txt"), P(), P())
    return jax.shard_map(
        local,
        mesh=mesh,
        in_specs=placed,
        out_specs=(P("txt", None), P(("img", "txt"), None)),
        check_vma=False,
    )
```

```python
import functools

import jax
import jax.numpy as jnp
from jax import lax
from jax.experimental import pallas as pl
from jax.experimental.pallas import tpu as pltpu
from jax.sharding import PartitionSpec as P

EPSILON = 1e-06
F32 = jnp.float32
BF16 = jnp.bfloat16
VMEM = pl.BlockSpec(memory_space=pltpu.VMEM)
SMEM = pl.BlockSpec(memory_space=pltpu.SMEM)


def unit_rows(texts, images):
    sizes = [texts.shape, images.shape]
    total = texts.size + images.size
    return pl.pallas_call(
        unit_body,
        out_shape=[struct(*size, BF16) for size in sizes],
        in_specs=[pl.BlockSpec(memory_space=pltpu.HBM)] * 2,
        out_specs=[VMEM] * 2,
        scratch_shapes=[pltpu.VMEM(size, F32) for size in sizes] + [pltpu.SemaphoreType.DMA((2,))],
        compiler_params=pltpu.CompilerParams(vmem_limit_bytes=16 << 20),
        cost_estimate=pl.CostEstimate(flops=4 * total, bytes_accessed=6 * total, transcendentals=0),
    )(*[pltpu.with_memory_space_constraint(v, pltpu.HBM) for v in (texts, images)])


def call(body, outs, args, specs, limit, flops, scratch=()):
    size = sum(a.size * a.dtype.itemsize for a in args)
    size += sum(o.size * o.dtype.itemsize for o in outs)
    return pl.pallas_call(
        body,
        out_shape=outs,
        in_specs=specs,
        out_specs=[VMEM] * len(outs),
        scratch_shapes=scratch,
        compiler_params=pltpu.CompilerParams(vmem_limit_bytes=limit),
        cost_estimate=pl.CostEstimate(flops=flops, bytes_accessed=size, transcendentals=0),
    )(*args)


def struct(rows, cols, dtype):
    return jax.ShapeDtypeStruct((rows, cols), dtype)


def inverse_norm(values):
    return lax.rsqrt(jnp.sum(values * values, axis=1, keepdims=True) + EPSILON)


def backward_unit(values, upstream):
    inverse = inverse_norm(values)
    unit = values * inverse
    return inverse * (upstream - unit * jnp.sum(unit * upstream, axis=1, keepdims=True))


def unit_body(txt, img, txt_out, img_out, txt_held, img_held, sems):
    txt_copy = pltpu.make_async_copy(txt, txt_held, sems.at[0])
    img_copy = pltpu.make_async_copy(img, img_held, sems.at[1])
    txt_copy.start()
    img_copy.start()
    txt_copy.wait()
    values = txt_held[...]
    txt_out[...] = (values * inverse_norm(values)).astype(BF16)
    img_copy.wait()
    values = img_held[...]
    img_out[...] = (values * inverse_norm(values)).astype(BF16)


def weights_of(tile, scalars, factors, perm, img):
    rows = tile.shape[0] // scalars.shape[0]
    row = lax.broadcasted_iota(jnp.int32, (rows, 1), 0)
    ids = jnp.concatenate([row + scalars[k] for k in range(scalars.shape[0])], axis=0)
    products = lax.dot_general(tile, img, (((1,), (1,)), ((), ())), preferred_element_type=F32)
    positive = (ids == perm).astype(F32)
    return (jax.nn.sigmoid(factors[0] * products + factors[1]) - positive).astype(BF16)


def to_images(weights, tile):
    return lax.dot_general(weights, tile, (((0,), (0,)), ((), ())), preferred_element_type=F32)


def other_body(scalars, factors, perm, img, txt, kept, out):
    weights = weights_of(txt[...], scalars, factors, perm[...], img[...])
    kept[...] = weights
    out[...] = to_images(weights, txt[...]).astype(BF16)


def own_body(blocks, home, scalars, factors, perm, img_own, img_other, kept, txt, *refs):
    own_img, own_txt, *other_txt, held = refs
    rows = own_txt.shape[0]
    weights = weights_of(txt[...], scalars, factors, perm[...], img_own[...])
    own_img[...] = to_images(weights, txt[...])
    held[...] = jnp.dot(weights, img_own[...], preferred_element_type=F32) + jnp.dot(
        kept[...], img_other[...], preferred_element_type=F32
    )
    for k in range(blocks):
        start = pl.multiple_of(lax.rem(home[0] + k, blocks) * rows, rows)
        block = held[pl.ds(start, rows), :]
        if k == 0:
            own_txt[...] = block
        else:
            other_txt[k - 1][...] = block.astype(BF16)


def add_body(own, other, out):
    out[...] = (own[...] + other[...].astype(F32)).astype(BF16)


def total_of(parts, rows):
    total = parts[:rows, :].astype(F32)
    for k in range(1, parts.shape[0] // rows):
        total = total + parts[k * rows : (k + 1) * rows, :].astype(F32)
    return total


def finish_img(copies, position, factors, img_ref, parts, out):
    rows = parts.shape[0] // copies
    start = pl.multiple_of(position[0] * rows, rows)
    upstream = factors[0] * total_of(parts, rows)
    grad = backward_unit(img_ref[pl.ds(start, rows), :], upstream).astype(BF16)
    for k in range(copies):
        out[k * rows : (k + 1) * rows, :] = grad


def finish_body(factors, txt_ref, grads, own, *refs):
    *parts, img_out, txt_out = refs
    img_out[...] = grads[...].astype(F32)
    total = own[...]
    for part in parts:
        total = total + part[...].astype(F32)
    txt_out[...] = backward_unit(txt_ref[...], factors[0] * total)


def exchanged(value, axis, groups=None):
    return lax.all_to_all(value, axis, 0, 0, axis_index_groups=groups, tiled=True)


def shifted(value, axis, steps):
    count = lax.axis_size(axis)
    return lax.ppermute(value, axis, [(s, (s + steps) % count) for s in range(count)])


def swapped(value):
    count = lax.axis_size("txt")
    return lax.ppermute(value, "txt", [(s, s ^ 1) for s in range(count)])


def local(images, texts, perm, scale, shift):
    rows, width = images.shape
    txt_rows = texts.shape[0]
    line = lax.axis_size("txt")
    blocks = line // 2
    groups = [list(range(core, line, 2)) for core in range(2)]
    count = lax.axis_size("img")
    part = rows // count
    column = lax.axis_index("txt")
    place = lax.axis_index("img")
    position = place.reshape(1).astype(jnp.int32)
    factors = jnp.concatenate([scale, shift])
    perm_row = perm.reshape(1, rows)

    txt_bf, img_bf = unit_rows(texts, images)
    tiles = exchanged(jnp.concatenate([txt_bf] * blocks, axis=0), "txt", groups)
    perm_other = swapped(perm_row)
    img_other = swapped(img_bf)
    firsts = jnp.stack(
        [(place * line + column % 2 + 2 * k) * txt_rows for k in range(blocks)]
    ).astype(jnp.int32)
    pairs = 2 * rows * blocks * txt_rows * width
    kept, other_img = call(
        other_body,
        [struct(blocks * txt_rows, rows, BF16), struct(rows, width, BF16)],
        [firsts, factors, perm_other, img_other, tiles],
        [SMEM] * 2 + [VMEM] * 3,
        40 << 20,
        2 * pairs,
    )
    from_other = swapped(other_img)
    home = (column // 2).reshape(1).astype(jnp.int32)
    own_img, own_txt, *other_txt = call(
        functools.partial(own_body, blocks),
        [struct(rows, width, F32), struct(txt_rows, width, F32)]
        + [struct(txt_rows, width, BF16)] * (blocks - 1),
        [home, firsts, factors, perm_row, img_bf, img_other, kept, tiles],
        [SMEM] * 3 + [VMEM] * 5,
        40 << 20,
        4 * pairs,
        [pltpu.VMEM((blocks * txt_rows, width), F32)],
    )
    back = [shifted(other_txt[k - 1], "txt", 2 * k) for k in range(1, blocks)]
    (sums,) = call(
        add_body,
        [struct(rows, width, BF16)],
        [own_img, from_other],
        [VMEM] * 2,
        24 << 20,
        rows * width,
    )
    parts = exchanged(sums, "img")
    (grad_part,) = call(
        functools.partial(finish_img, count),
        [struct(rows, width, BF16)],
        [position, factors, images, parts],
        [SMEM] * 2 + [VMEM] * 2,
        24 << 20,
        10 * part * width,
    )
    grad_images, grad_texts = call(
        finish_body,
        [struct(rows, width, F32), struct(txt_rows, width, F32)],
        [factors, texts, exchanged(grad_part, "img"), own_txt, *back],
        [SMEM] + [VMEM] * (2 + blocks),
        24 << 20,
        10 * txt_rows * width,
    )
    return (grad_images, grad_texts)


def solution(mesh):
    placed = (P("txt", None), P(("img", "txt"), None), P("txt"), P(), P())
    return jax.shard_map(
        local,
        mesh=mesh,
        in_specs=placed,
        out_specs=(P("txt", None), P(("img", "txt"), None)),
        check_vma=False,
    )
```

```python
import functools

import jax
import jax.numpy as jnp
from jax import lax
from jax.experimental import pallas as pl
from jax.experimental.pallas import tpu as pltpu
from jax.sharding import PartitionSpec as P

EPSILON = 1e-06
F32 = jnp.float32
BF16 = jnp.bfloat16
VMEM = pl.BlockSpec(memory_space=pltpu.VMEM)
SMEM = pl.BlockSpec(memory_space=pltpu.SMEM)


def unit_rows(texts, images):
    sizes = [texts.shape, images.shape]
    total = texts.size + images.size
    return pl.pallas_call(
        unit_body,
        out_shape=[struct(*size, BF16) for size in sizes],
        in_specs=[pl.BlockSpec(memory_space=pltpu.HBM)] * 2,
        out_specs=[VMEM] * 2,
        scratch_shapes=[pltpu.VMEM(size, F32) for size in sizes] + [pltpu.SemaphoreType.DMA((2,))],
        compiler_params=pltpu.CompilerParams(vmem_limit_bytes=16 << 20),
        cost_estimate=pl.CostEstimate(flops=4 * total, bytes_accessed=6 * total, transcendentals=0),
    )(*[pltpu.with_memory_space_constraint(v, pltpu.HBM) for v in (texts, images)])


def call(body, outs, args, specs, limit, flops):
    size = sum(a.size * a.dtype.itemsize for a in args)
    size += sum(o.size * o.dtype.itemsize for o in outs)
    return pl.pallas_call(
        body,
        out_shape=outs,
        in_specs=specs,
        out_specs=[VMEM] * len(outs),
        compiler_params=pltpu.CompilerParams(vmem_limit_bytes=limit),
        cost_estimate=pl.CostEstimate(flops=flops, bytes_accessed=size, transcendentals=0),
    )(*args)


def struct(rows, cols, dtype):
    return jax.ShapeDtypeStruct((rows, cols), dtype)


def inverse_norm(values):
    return lax.rsqrt(jnp.sum(values * values, axis=1, keepdims=True) + EPSILON)


def backward_unit(values, upstream):
    inverse = inverse_norm(values)
    unit = values * inverse
    return inverse * (upstream - unit * jnp.sum(unit * upstream, axis=1, keepdims=True))


def unit_body(txt, img, txt_out, img_out, txt_held, img_held, sems):
    txt_copy = pltpu.make_async_copy(txt, txt_held, sems.at[0])
    img_copy = pltpu.make_async_copy(img, img_held, sems.at[1])
    txt_copy.start()
    img_copy.start()
    txt_copy.wait()
    values = txt_held[...]
    txt_out[...] = (values * inverse_norm(values)).astype(BF16)
    img_copy.wait()
    values = img_held[...]
    img_out[...] = (values * inverse_norm(values)).astype(BF16)


def weights_of(tile, scalars, factors, perm, img):
    rows = tile.shape[0] // scalars.shape[0]
    row = lax.broadcasted_iota(jnp.int32, (rows, 1), 0)
    ids = jnp.concatenate([row + scalars[k] for k in range(scalars.shape[0])], axis=0)
    products = lax.dot_general(tile, img, (((1,), (1,)), ((), ())), preferred_element_type=F32)
    positive = (ids == perm).astype(F32)
    return (jax.nn.sigmoid(factors[0] * products + factors[1]) - positive).astype(BF16)


def to_images(weights, tile):
    return lax.dot_general(weights, tile, (((0,), (0,)), ((), ())), preferred_element_type=F32)


def to_texts(weights, img):
    return jnp.dot(weights, img, preferred_element_type=F32)


def joined(tiles):
    return jnp.concatenate([t[...] for t in tiles], axis=0)


def early_body(blocks, scalars, factors, perm, perm_other, img, img_other, *refs):
    txt = refs[:blocks]
    own_sum, other_sum, own_txt, *other_txt = refs[blocks:]
    rows = own_txt.shape[0]
    tile = joined(txt)
    w_other = weights_of(tile, scalars, factors, perm_other[...], img_other[...])
    other_sum[...] = to_images(w_other, tile)
    w_own = weights_of(tile, scalars, factors, perm[...], img[...])
    own_sum[...] = to_images(w_own, tile)
    to_txt = to_texts(w_own, img[...]) + to_texts(w_other, img_other[...])
    own_txt[...] = to_txt[:rows]
    for k in range(1, blocks):
        other_txt[k - 1][...] = to_txt[k * rows : (k + 1) * rows].astype(BF16)


def other_body(blocks, scalars, factors, perm, img, before, *refs):
    *txt, kept, out = refs
    tile = joined(txt)
    weights = weights_of(tile, scalars, factors, perm[...], img[...])
    kept[...] = weights
    out[...] = (before[...] + to_images(weights, tile)).astype(BF16)


def own_body(blocks, scalars, factors, perm, img, img_other, kept, before, *refs):
    txt = refs[:blocks]
    own_sum, *out_txt = refs[blocks:]
    rows = out_txt[0].shape[0]
    tile = joined(txt)
    weights = weights_of(tile, scalars, factors, perm[...], img[...])
    own_sum[...] = before[...] + to_images(weights, tile)
    to_txt = to_texts(weights, img[...]) + to_texts(kept[...], img_other[...])
    for k in range(blocks):
        out_txt[k][...] = to_txt[k * rows : (k + 1) * rows].astype(BF16)


def split_body(count, position, own, other, keep, *send):
    rows = keep.shape[0]
    for k in range(count):
        start = pl.multiple_of((position[0] ^ k) * rows, rows)
        part = own[pl.ds(start, rows), :] + other[pl.ds(start, rows), :].astype(F32)
        if k == 0:
            keep[...] = part
        else:
            send[k - 1][...] = part.astype(BF16)


def total_of(own, parts):
    total = own[...]
    for part in parts:
        total = total + part[...].astype(F32)
    return total


def finish_img_body(position, factors, img_ref, own, *refs):
    *parts, out = refs
    rows = own.shape[0]
    start = pl.multiple_of(position[0] * rows, rows)
    upstream = factors[0] * total_of(own, parts)
    out[...] = backward_unit(img_ref[pl.ds(start, rows), :], upstream).astype(BF16)


def finish_txt_body(factors, txt_ref, own, *refs):
    *parts, out = refs
    out[...] = backward_unit(txt_ref[...], factors[0] * total_of(own, parts))


def join_body(count, position, *refs):
    *parts, out = refs
    rows = parts[0].shape[0]
    for k in range(count):
        start = pl.multiple_of((position[0] ^ k) * rows, rows)
        out[pl.ds(start, rows), :] = parts[k][...].astype(F32)


def swapped(value, axis, step):
    count = lax.axis_size(axis)
    return lax.ppermute(value, axis, [(s, s ^ step) for s in range(count)])


def local(images, texts, perm, scale, shift):
    rows, width = images.shape
    txt_rows = texts.shape[0]
    line = lax.axis_size("txt")
    blocks = line // 2
    early = 2
    count = lax.axis_size("img")
    part = rows // count
    column = lax.axis_index("txt")
    place = lax.axis_index("img")
    position = place.reshape(1).astype(jnp.int32)
    factors = jnp.concatenate([scale, shift])
    perm_row = perm.reshape(1, rows)

    txt_bf, img_bf = unit_rows(texts, images)
    far = [swapped(txt_bf, "txt", 2 * k) for k in range(blocks - 1, 1, -1)]
    tiles = [txt_bf, swapped(txt_bf, "txt", 2)] + far[::-1]
    perm_other = swapped(perm_row, "txt", 1)
    img_other = swapped(img_bf, "txt", 1)
    firsts = jnp.stack(
        [(place * line + (column ^ (2 * k))) * txt_rows for k in range(blocks)]
    ).astype(jnp.int32)
    pairs = 2 * rows * txt_rows * width
    tile_out = struct(txt_rows, width, BF16)
    own_sum, other_sum, own_txt, *other_txt = call(
        functools.partial(early_body, early),
        [struct(rows, width, F32)] * 2 + [struct(txt_rows, width, F32)] + [tile_out] * (early - 1),
        [firsts[:early], factors, perm_row, perm_other, img_bf, img_other, *tiles[:early]],
        [SMEM] * 2 + [VMEM] * (4 + early),
        40 << 20,
        6 * early * pairs,
    )
    back = [swapped(other_txt[k - 1], "txt", 2 * k) for k in range(1, early)]

    late = blocks - early
    kept, other_img = call(
        functools.partial(other_body, late),
        [struct(late * txt_rows, rows, BF16), struct(rows, width, BF16)],
        [firsts[early:], factors, perm_other, img_other, other_sum, *tiles[early:]],
        [SMEM] * 2 + [VMEM] * (3 + late),
        40 << 20,
        2 * late * pairs,
    )
    from_other = swapped(other_img, "txt", 1)
    own_img, *other_txt = call(
        functools.partial(own_body, late),
        [struct(rows, width, F32)] + [tile_out] * late,
        [firsts[early:], factors, perm_row, img_bf, img_other, kept, own_sum, *tiles[early:]],
        [SMEM] * 2 + [VMEM] * (5 + late),
        40 << 20,
        4 * late * pairs,
    )
    back += [swapped(other_txt[k], "txt", 2 * (early + k)) for k in range(late)]

    keep, *send = call(
        functools.partial(split_body, count),
        [struct(part, width, F32)] + [struct(part, width, BF16)] * (count - 1),
        [position, own_img, from_other],
        [SMEM, VMEM, VMEM],
        24 << 20,
        rows * width,
    )
    got = [swapped(send[k - 1], "img", k) for k in range(1, count)]
    (grad_part,) = call(
        finish_img_body,
        [struct(part, width, BF16)],
        [position, factors, images, keep, *got],
        [SMEM] * 2 + [VMEM] * (1 + count),
        24 << 20,
        10 * part * width,
    )
    grads = [grad_part] + [swapped(grad_part, "img", k) for k in range(1, count)]
    (grad_images,) = call(
        functools.partial(join_body, count),
        [struct(rows, width, F32)],
        [position, *grads],
        [SMEM] + [VMEM] * count,
        24 << 20,
        rows * width,
    )
    (grad_texts,) = call(
        finish_txt_body,
        [struct(txt_rows, width, F32)],
        [factors, texts, own_txt, *back],
        [SMEM] + [VMEM] * (1 + blocks),
        24 << 20,
        10 * txt_rows * width,
    )
    return (grad_images, grad_texts)


def solution(mesh):
    placed = (P("txt", None), P(("img", "txt"), None), P("txt"), P(), P())
    return jax.shard_map(
        local,
        mesh=mesh,
        in_specs=placed,
        out_specs=(P("txt", None), P(("img", "txt"), None)),
        check_vma=False,
    )
```

```python
import functools

import jax
import jax.numpy as jnp
from jax import lax
from jax.experimental import pallas as pl
from jax.experimental.pallas import tpu as pltpu
from jax.sharding import PartitionSpec as P

EPSILON = 1e-06
F32 = jnp.float32
BF16 = jnp.bfloat16
VMEM = pl.BlockSpec(memory_space=pltpu.VMEM)
SMEM = pl.BlockSpec(memory_space=pltpu.SMEM)


def unit_rows(place, texts, images, part):
    width = texts.shape[1]
    sizes = [texts.shape, images.shape]
    total = texts.size + images.size
    own = [texts.shape, (part, width)]
    return pl.pallas_call(
        unit_body,
        out_shape=[struct(*size, BF16) for size in sizes]
        + [struct(*size, F32) for size in own]
        + [struct(size[0], 128, F32) for size in own],
        in_specs=[SMEM] + [pl.BlockSpec(memory_space=pl.ANY)] * 2,
        out_specs=[VMEM] * 6,
        scratch_shapes=[pltpu.VMEM(size, F32) for size in sizes] + [pltpu.SemaphoreType.DMA((2,))],
        compiler_params=pltpu.CompilerParams(vmem_limit_bytes=16 << 20),
        cost_estimate=pl.CostEstimate(flops=4 * total, bytes_accessed=6 * total, transcendentals=0),
    )(place, *[pltpu.with_memory_space_constraint(v, pltpu.HBM) for v in (texts, images)])


def call(body, outs, args, specs, limit, flops):
    size = sum(a.size * a.dtype.itemsize for a in args)
    size += sum(o.size * o.dtype.itemsize for o in outs)
    return pl.pallas_call(
        body,
        out_shape=outs,
        in_specs=specs,
        out_specs=[VMEM] * len(outs),
        compiler_params=pltpu.CompilerParams(vmem_limit_bytes=limit),
        cost_estimate=pl.CostEstimate(flops=flops, bytes_accessed=size, transcendentals=0),
    )(*args)


def struct(rows, cols, dtype):
    return jax.ShapeDtypeStruct((rows, cols), dtype)


def inverse_norm(values):
    return lax.rsqrt(jnp.sum(values * values, axis=1, keepdims=True) + EPSILON)


def unit_body(
    place, txt, img, txt_bf, img_bf, txt_unit, img_unit, txt_inv, img_inv, txt_held, img_held, sems
):
    txt_copy = pltpu.make_async_copy(txt, txt_held, sems.at[0])
    img_copy = pltpu.make_async_copy(img, img_held, sems.at[1])
    txt_copy.start()
    img_copy.start()
    txt_copy.wait()
    values = txt_held[...]
    inverse = inverse_norm(values)
    unit = values * inverse
    txt_bf[...] = unit.astype(BF16)
    txt_unit[...] = unit
    txt_inv[...] = jnp.broadcast_to(inverse, txt_inv.shape)
    img_copy.wait()
    values = img_held[...]
    img_bf[...] = (values * inverse_norm(values)).astype(BF16)
    rows = img_unit.shape[0]
    values = img_held[pl.ds(pl.multiple_of(place[0] * rows, rows), rows), :]
    inverse = inverse_norm(values)
    img_unit[...] = values * inverse
    img_inv[...] = jnp.broadcast_to(inverse, img_inv.shape)


def weights_of(tile, order, line, place, column, scale, shift, perm, img):
    rows = tile.shape[0] // len(order)
    row = lax.broadcasted_iota(jnp.int32, (rows, 1), 0)
    ids = jnp.concatenate(
        [row + (place[0] * line + (column[0] ^ (2 * k))) * rows for k in order], axis=0
    )
    products = lax.dot_general(tile, img, (((1,), (1,)), ((), ())), preferred_element_type=F32)
    positive = (ids == perm).astype(F32)
    return (jax.nn.sigmoid(scale[0] * products + shift[0]) - positive).astype(BF16)


def to_images(weights, tile):
    return lax.dot_general(weights, tile, (((0,), (0,)), ((), ())), preferred_element_type=F32)


def to_texts(weights, img):
    return jnp.dot(weights, img, preferred_element_type=F32)


def joined(tiles):
    return jnp.concatenate([t[...] for t in tiles], axis=0)


def other_body(order, line, place, column, scale, shift, perm, img, *refs):
    *txt, kept, out = refs
    tile = joined(txt)
    weights = weights_of(tile, order, line, place, column, scale, shift, perm[...], img[...])
    kept[...] = weights
    out[...] = to_images(weights, tile).astype(BF16)


def own_body(order, line, place, column, scale, shift, perm, img, img_other, kept, *refs):
    *txt, own_sum, own_txt, even_txt, odd_txt = refs
    rows = own_txt.shape[0]
    tile = joined(txt)
    weights = weights_of(tile, order, line, place, column, scale, shift, perm[...], img[...])
    own_sum[...] = to_images(weights, tile)
    to_txt = to_texts(weights, img[...]) + to_texts(kept[...], img_other[...])
    half = odd_txt.shape[0]
    own_txt[...] = to_txt[:rows]
    even_txt[...] = to_txt[rows:half]
    odd_txt[...] = to_txt[half:].astype(BF16)


def add_body(even, got, *outs):
    rows = outs[0].shape[0]
    for k, out in enumerate(outs):
        mine = even[k * rows : (k + 1) * rows, :]
        out[...] = (mine + got[(k + 1) * rows : (k + 2) * rows, :].astype(F32)).astype(BF16)


def split_body(count, position, own, other, keep, *send):
    rows = keep.shape[0]
    for k in range(count):
        start = pl.multiple_of((position[0] ^ k) * rows, rows)
        part = own[pl.ds(start, rows), :] + other[pl.ds(start, rows), :].astype(F32)
        if k == 0:
            keep[...] = part
        else:
            send[k - 1][...] = part.astype(BF16)


def total_of(own, parts):
    total = own[...]
    for part in parts:
        total = total + part[...].astype(F32)
    return total


def backward_unit(unit, inverse, upstream):
    along = jnp.sum(unit * upstream, axis=1, keepdims=True)
    return inverse[:, :1] * (upstream - unit * along)


def finish_img_body(scale, unit, inverse, own, *refs):
    *parts, out = refs
    out[...] = backward_unit(
        unit[...], inverse[...], scale[0] * total_of(own, parts)
    ).astype(BF16)


def last_body(count, place, scale, unit, inverse, own, *refs):
    parts = refs[:count]
    *back, img_out, txt_out, img_held, txt_held, sems = refs[count:]
    rows = parts[0].shape[0]
    copies = []
    for k in range(count):
        img_held[k * rows : (k + 1) * rows, :] = parts[k][...].astype(F32)
        start = pl.multiple_of((place[0] ^ k) * rows, rows)
        copies.append(
            pltpu.make_async_copy(
                img_held.at[pl.ds(k * rows, rows), :],
                img_out.at[pl.ds(start, rows), :],
                sems.at[k],
            )
        )
        copies[-1].start()
    rows = unit.shape[0]
    total = total_of(own, back[1:]) + back[0][:rows, :].astype(F32)
    txt_held[...] = backward_unit(unit[...], inverse[...], scale[0] * total)
    copies.append(pltpu.make_async_copy(txt_held, txt_out, sems.at[count]))
    copies[-1].start()
    for copy in copies:
        copy.wait()


def swapped(value, axis, step):
    count = lax.axis_size(axis)
    return lax.ppermute(value, axis, [(s, s ^ step) for s in range(count)])


def local(images, texts, perm, scale, shift):
    rows, width = images.shape
    txt_rows = texts.shape[0]
    line = lax.axis_size("txt")
    blocks = line // 2
    count = lax.axis_size("img")
    part = rows // count
    column = lax.axis_index("txt").reshape(1).astype(jnp.int32)
    place = lax.axis_index("img").reshape(1).astype(jnp.int32)
    perm_row = perm.reshape(1, rows)

    txt_bf, img_bf, txt_unit, img_unit, txt_inv, img_inv = unit_rows(place, texts, images, part)
    half = blocks // 2
    order = list(range(0, blocks, 2)) + list(range(1, blocks, 2))
    tiles = [txt_bf] + [swapped(txt_bf, "txt", 2 * k) for k in order[1:]]
    perm_other = swapped(perm_row, "txt", 1)
    img_other = swapped(img_bf, "txt", 1)
    scalars = [place, column, scale, shift]
    pairs = 2 * rows * blocks * txt_rows * width
    kept, other_img = call(
        functools.partial(other_body, order, line),
        [struct(blocks * txt_rows, rows, BF16), struct(rows, width, BF16)],
        [*scalars, perm_other, img_other, *tiles],
        [SMEM] * 4 + [VMEM] * (2 + blocks),
        40 << 20,
        2 * pairs,
    )
    from_other = swapped(other_img, "txt", 1)
    own_img, own_txt, even_txt, odd_txt = call(
        functools.partial(own_body, order, line),
        [
            struct(rows, width, F32),
            struct(txt_rows, width, F32),
            struct((half - 1) * txt_rows, width, F32),
            struct(half * txt_rows, width, BF16),
        ],
        [*scalars, perm_row, img_bf, img_other, kept, *tiles],
        [SMEM] * 4 + [VMEM] * (4 + blocks),
        40 << 20,
        4 * pairs,
    )
    near = swapped(odd_txt, "txt", 2)
    sums = call(
        add_body,
        [struct(txt_rows, width, BF16)] * (half - 1),
        [even_txt, near],
        [VMEM] * 2,
        24 << 20,
        rows * width,
    )
    back = [near] + [swapped(sums[k - 1], "txt", 4 * k) for k in range(1, half)]

    keep, *send = call(
        functools.partial(split_body, count),
        [struct(part, width, F32)] + [struct(part, width, BF16)] * (count - 1),
        [place, own_img, from_other],
        [SMEM, VMEM, VMEM],
        24 << 20,
        rows * width,
    )
    got = [swapped(send[k - 1], "img", k) for k in range(1, count)]
    (grad_part,) = call(
        finish_img_body,
        [struct(part, width, BF16)],
        [scale, img_unit, img_inv, keep, *got],
        [SMEM] + [VMEM] * (2 + count),
        24 << 20,
        10 * part * width,
    )
    grads = [grad_part] + [swapped(grad_part, "img", k) for k in range(1, count)]
    anywhere = pl.BlockSpec(memory_space=pl.ANY)
    return pl.pallas_call(
        functools.partial(last_body, count),
        out_shape=[struct(rows, width, F32), struct(txt_rows, width, F32)],
        in_specs=[SMEM] * 2 + [VMEM] * (3 + count + half),
        out_specs=[anywhere] * 2,
        scratch_shapes=[
            pltpu.VMEM((rows, width), F32),
            pltpu.VMEM((txt_rows, width), F32),
            pltpu.SemaphoreType.DMA((count + 1,)),
        ],
        compiler_params=pltpu.CompilerParams(vmem_limit_bytes=24 << 20),
        cost_estimate=pl.CostEstimate(
            flops=10 * txt_rows * width, bytes_accessed=8 * rows * width, transcendentals=0
        ),
    )(place, scale, txt_unit, txt_inv, own_txt, *grads, *back)


def solution(mesh):
    placed = (P("txt", None), P(("img", "txt"), None), P("txt"), P(), P())
    return jax.shard_map(
        local,
        mesh=mesh,
        in_specs=placed,
        out_specs=(P("txt", None), P(("img", "txt"), None)),
        check_vma=False,
    )
```

```python
import functools

import jax
import jax.numpy as jnp
from jax import lax
from jax.experimental import pallas as pl
from jax.experimental.pallas import tpu as pltpu
from jax.sharding import PartitionSpec as P

EPSILON = 1e-06
F32 = jnp.float32
BF16 = jnp.bfloat16
VMEM = pl.BlockSpec(memory_space=pltpu.VMEM)
SMEM = pl.BlockSpec(memory_space=pltpu.SMEM)


def unit_rows(place, texts, images, part):
    width = texts.shape[1]
    sizes = [texts.shape, images.shape]
    total = texts.size + images.size
    own = [texts.shape, (part, width)]
    return pl.pallas_call(
        unit_body,
        out_shape=[struct(*size, BF16) for size in sizes]
        + [struct(*size, F32) for size in own]
        + [struct(size[0], 128, F32) for size in own],
        in_specs=[SMEM] + [pl.BlockSpec(memory_space=pl.ANY)] * 2,
        out_specs=[VMEM] * 6,
        scratch_shapes=[pltpu.VMEM(size, F32) for size in sizes] + [pltpu.SemaphoreType.DMA((2,))],
        compiler_params=pltpu.CompilerParams(vmem_limit_bytes=16 << 20),
        cost_estimate=pl.CostEstimate(flops=4 * total, bytes_accessed=6 * total, transcendentals=0),
    )(place, *[pltpu.with_memory_space_constraint(v, pltpu.HBM) for v in (texts, images)])


def call(body, outs, args, specs, limit, flops):
    size = sum(a.size * a.dtype.itemsize for a in args)
    size += sum(o.size * o.dtype.itemsize for o in outs)
    return pl.pallas_call(
        body,
        out_shape=outs,
        in_specs=specs,
        out_specs=[VMEM] * len(outs),
        compiler_params=pltpu.CompilerParams(vmem_limit_bytes=limit),
        cost_estimate=pl.CostEstimate(flops=flops, bytes_accessed=size, transcendentals=0),
    )(*args)


def struct(rows, cols, dtype):
    return jax.ShapeDtypeStruct((rows, cols), dtype)


def inverse_norm(values):
    return lax.rsqrt(jnp.sum(values * values, axis=1, keepdims=True) + EPSILON)


def unit_body(
    place, txt, img, txt_bf, img_bf, txt_unit, img_unit, txt_inv, img_inv, txt_held, img_held, sems
):
    txt_copy = pltpu.make_async_copy(txt, txt_held, sems.at[0])
    img_copy = pltpu.make_async_copy(img, img_held, sems.at[1])
    txt_copy.start()
    img_copy.start()
    txt_copy.wait()
    values = txt_held[...]
    inverse = inverse_norm(values)
    unit = values * inverse
    txt_bf[...] = unit.astype(BF16)
    txt_unit[...] = unit
    txt_inv[...] = jnp.broadcast_to(inverse, txt_inv.shape)
    img_copy.wait()
    values = img_held[...]
    img_bf[...] = (values * inverse_norm(values)).astype(BF16)
    rows = img_unit.shape[0]
    values = img_held[pl.ds(pl.multiple_of(place[0] * rows, rows), rows), :]
    inverse = inverse_norm(values)
    img_unit[...] = values * inverse
    img_inv[...] = jnp.broadcast_to(inverse, img_inv.shape)


def weights_of(tile, order, line, place, column, scale, shift, perm, img):
    rows = tile.shape[0] // len(order)
    row = lax.broadcasted_iota(jnp.int32, (rows, 1), 0)
    ids = jnp.concatenate(
        [row + (place[0] * line + (column[0] ^ (2 * k))) * rows for k in order], axis=0
    )
    products = lax.dot_general(tile, img, (((1,), (1,)), ((), ())), preferred_element_type=F32)
    positive = (ids == perm).astype(F32)
    return (jax.nn.sigmoid(scale[0] * products + shift[0]) - positive).astype(BF16)


def to_images(weights, tile):
    return lax.dot_general(weights, tile, (((0,), (0,)), ((), ())), preferred_element_type=F32)


def to_texts(weights, img):
    return jnp.dot(weights, img, preferred_element_type=F32)


def joined(tiles):
    return jnp.concatenate([t[...] for t in tiles], axis=0)


def other_body(order, line, place, column, scale, shift, perm, img, *refs):
    *txt, kept, out = refs
    tile = joined(txt)
    weights = weights_of(tile, order, line, place, column, scale, shift, perm[...], img[...])
    kept[...] = weights
    out[...] = to_images(weights, tile).astype(BF16)


def own_body(order, line, place, column, scale, shift, perm, img, img_other, kept, *refs):
    *txt, own_sum, own_txt, even_txt, near_txt, odd_txt = refs
    rows = own_txt.shape[0]
    tile = joined(txt)
    weights = weights_of(tile, order, line, place, column, scale, shift, perm[...], img[...])
    own_sum[...] = to_images(weights, tile)
    to_txt = to_texts(weights, img[...]) + to_texts(kept[...], img_other[...])
    half = rows + even_txt.shape[0]
    own_txt[...] = to_txt[:rows]
    even_txt[...] = to_txt[rows:half]
    near_txt[...] = to_txt[half : half + rows].astype(BF16)
    odd_txt[...] = to_txt[half + rows :].astype(BF16)


def add_body(even, got, *outs):
    rows = outs[0].shape[0]
    for k, out in enumerate(outs):
        mine = even[k * rows : (k + 1) * rows, :]
        out[...] = (mine + got[k * rows : (k + 1) * rows, :].astype(F32)).astype(BF16)


def split_body(count, position, own, other, keep, *send):
    rows = keep.shape[0]
    for k in range(count):
        start = pl.multiple_of((position[0] ^ k) * rows, rows)
        part = own[pl.ds(start, rows), :] + other[pl.ds(start, rows), :].astype(F32)
        if k == 0:
            keep[...] = part
        else:
            send[k - 1][...] = part.astype(BF16)


def total_of(own, parts):
    total = own[...]
    for part in parts:
        total = total + part[...].astype(F32)
    return total


def backward_unit(unit, inverse, upstream):
    along = jnp.sum(unit * upstream, axis=1, keepdims=True)
    return inverse[:, :1] * (upstream - unit * along)


def finish_img_body(scale, unit, inverse, own, *refs):
    *parts, out = refs
    out[...] = backward_unit(
        unit[...], inverse[...], scale[0] * total_of(own, parts)
    ).astype(BF16)


def last_body(count, place, scale, unit, inverse, own, *refs):
    parts = refs[:count]
    *back, img_out, txt_out, img_held, txt_held, sems = refs[count:]
    rows = parts[0].shape[0]
    copies = []
    for k in range(count):
        img_held[k * rows : (k + 1) * rows, :] = parts[k][...].astype(F32)
        start = pl.multiple_of((place[0] ^ k) * rows, rows)
        copies.append(
            pltpu.make_async_copy(
                img_held.at[pl.ds(k * rows, rows), :],
                img_out.at[pl.ds(start, rows), :],
                sems.at[k],
            )
        )
        copies[-1].start()
    txt_held[...] = backward_unit(unit[...], inverse[...], scale[0] * total_of(own, back))
    copies.append(pltpu.make_async_copy(txt_held, txt_out, sems.at[count]))
    copies[-1].start()
    for copy in copies:
        copy.wait()


def swapped(value, axis, step):
    count = lax.axis_size(axis)
    return lax.ppermute(value, axis, [(s, s ^ step) for s in range(count)])


def local(images, texts, perm, scale, shift):
    rows, width = images.shape
    txt_rows = texts.shape[0]
    line = lax.axis_size("txt")
    blocks = line // 2
    count = lax.axis_size("img")
    part = rows // count
    column = lax.axis_index("txt").reshape(1).astype(jnp.int32)
    place = lax.axis_index("img").reshape(1).astype(jnp.int32)
    perm_row = perm.reshape(1, rows)

    txt_bf, img_bf, txt_unit, img_unit, txt_inv, img_inv = unit_rows(place, texts, images, part)
    half = blocks // 2
    order = list(range(0, blocks, 2)) + list(range(1, blocks, 2))
    far = [swapped(txt_bf, "txt", 4 * k) for k in range(1, half)]
    near = [swapped(tile, "txt", 2) for tile in [txt_bf] + far]
    tiles = [txt_bf] + far + near
    perm_other = swapped(perm_row, "txt", 1)
    img_other = swapped(img_bf, "txt", 1)
    scalars = [place, column, scale, shift]
    pairs = 2 * rows * blocks * txt_rows * width
    kept, other_img = call(
        functools.partial(other_body, order, line),
        [struct(blocks * txt_rows, rows, BF16), struct(rows, width, BF16)],
        [*scalars, perm_other, img_other, *tiles],
        [SMEM] * 4 + [VMEM] * (2 + blocks),
        40 << 20,
        2 * pairs,
    )
    from_other = swapped(other_img, "txt", 1)
    own_img, own_txt, even_txt, near_txt, odd_txt = call(
        functools.partial(own_body, order, line),
        [
            struct(rows, width, F32),
            struct(txt_rows, width, F32),
            struct((half - 1) * txt_rows, width, F32),
            struct(txt_rows, width, BF16),
            struct((half - 1) * txt_rows, width, BF16),
        ],
        [*scalars, perm_row, img_bf, img_other, kept, *tiles],
        [SMEM] * 4 + [VMEM] * (4 + blocks),
        40 << 20,
        4 * pairs,
    )
    sums = call(
        add_body,
        [struct(txt_rows, width, BF16)] * (half - 1),
        [even_txt, swapped(odd_txt, "txt", 2)],
        [VMEM] * 2,
        24 << 20,
        rows * width,
    )
    back = [swapped(near_txt, "txt", 2)] + [swapped(sums[k - 1], "txt", 4 * k) for k in range(1, half)]

    keep, *send = call(
        functools.partial(split_body, count),
        [struct(part, width, F32)] + [struct(part, width, BF16)] * (count - 1),
        [place, own_img, from_other],
        [SMEM, VMEM, VMEM],
        24 << 20,
        rows * width,
    )
    got = [swapped(send[k - 1], "img", k) for k in range(1, count)]
    (grad_part,) = call(
        finish_img_body,
        [struct(part, width, BF16)],
        [scale, img_unit, img_inv, keep, *got],
        [SMEM] + [VMEM] * (2 + count),
        24 << 20,
        10 * part * width,
    )
    grads = [grad_part] + [swapped(grad_part, "img", k) for k in range(1, count)]
    anywhere = pl.BlockSpec(memory_space=pl.ANY)
    return pl.pallas_call(
        functools.partial(last_body, count),
        out_shape=[struct(rows, width, F32), struct(txt_rows, width, F32)],
        in_specs=[SMEM] * 2 + [VMEM] * (3 + count + half),
        out_specs=[anywhere] * 2,
        scratch_shapes=[
            pltpu.VMEM((rows, width), F32),
            pltpu.VMEM((txt_rows, width), F32),
            pltpu.SemaphoreType.DMA((count + 1,)),
        ],
        compiler_params=pltpu.CompilerParams(vmem_limit_bytes=24 << 20),
        cost_estimate=pl.CostEstimate(
            flops=10 * txt_rows * width, bytes_accessed=8 * rows * width, transcendentals=0
        ),
    )(place, scale, txt_unit, txt_inv, own_txt, *grads, *back)


def solution(mesh):
    placed = (P("txt", None), P(("img", "txt"), None), P("txt"), P(), P())
    return jax.shard_map(
        local,
        mesh=mesh,
        in_specs=placed,
        out_specs=(P("txt", None), P(("img", "txt"), None)),
        check_vma=False,
    )
```

```python
import functools

import jax
import jax.numpy as jnp
from jax import lax
from jax.experimental import pallas as pl
from jax.experimental.pallas import tpu as pltpu
from jax.sharding import PartitionSpec as P

EPSILON = 1e-06
F32 = jnp.float32
BF16 = jnp.bfloat16
VMEM = pl.BlockSpec(memory_space=pltpu.VMEM)
ANY = pl.BlockSpec(memory_space=pl.ANY)
SMEM = pl.BlockSpec(memory_space=pltpu.SMEM)


def in_hbm(value):
    return pltpu.with_memory_space_constraint(value, pltpu.HBM)


def call(body, outs, args, specs, limit, flops, scratch=()):
    size = sum(a.size * a.dtype.itemsize for a in args)
    size += sum(o.size * o.dtype.itemsize for o in outs)
    return pl.pallas_call(
        body,
        out_shape=outs,
        in_specs=specs,
        out_specs=[VMEM] * len(outs),
        scratch_shapes=scratch,
        compiler_params=pltpu.CompilerParams(vmem_limit_bytes=limit),
        cost_estimate=pl.CostEstimate(flops=flops, bytes_accessed=size, transcendentals=0),
    )(*args)


def struct(rows, cols, dtype):
    return jax.ShapeDtypeStruct((rows, cols), dtype)


def inverse_norm(values):
    return lax.rsqrt(jnp.sum(values * values, axis=1, keepdims=True) + EPSILON)


def unit_txt_body(source, bf, unit_out, inv, held, sem):
    copy = pltpu.make_async_copy(source, held, sem)
    copy.start()
    copy.wait()
    values = held[...]
    inverse = inverse_norm(values)
    unit = values * inverse
    bf[...] = unit.astype(BF16)
    unit_out[...] = unit
    inv[...] = jnp.broadcast_to(inverse, inv.shape)


def unit_img_body(place, other, source, bf, other_bf, unit_out, inv, held, sem):
    copy = pltpu.make_async_copy(source, held, sem)
    copy.start()
    values = other[...]
    other_bf[...] = (values * inverse_norm(values)).astype(BF16)
    copy.wait()
    values = held[...]
    bf[...] = (values * inverse_norm(values)).astype(BF16)
    rows = unit_out.shape[0]
    values = held[pl.ds(pl.multiple_of(place[0] * rows, rows), rows), :]
    inverse = inverse_norm(values)
    unit_out[...] = values * inverse
    inv[...] = jnp.broadcast_to(inverse, inv.shape)


def weights_of(tile, order, line, place, column, scale, shift, perm, img):
    rows = tile.shape[0] // len(order)
    row = lax.broadcasted_iota(jnp.int32, (rows, 1), 0)
    ids = jnp.concatenate(
        [row + (place[0] * line + (column[0] ^ (2 * k))) * rows for k in order], axis=0
    )
    products = lax.dot_general(tile, img, (((1,), (1,)), ((), ())), preferred_element_type=F32)
    positive = (ids == perm).astype(F32)
    return (jax.nn.sigmoid(scale[0] * products + shift[0]) - positive).astype(BF16)


def to_images(weights, tile):
    return lax.dot_general(weights, tile, (((0,), (0,)), ((), ())), preferred_element_type=F32)


def to_texts(weights, img):
    return jnp.dot(weights, img, preferred_element_type=F32)


def joined(tiles):
    return jnp.concatenate([t[...] for t in tiles], axis=0)


def other_body(order, line, place, column, scale, shift, perm, img, *refs):
    *txt, kept, out = refs
    tile = joined(txt)
    weights = weights_of(tile, order, line, place, column, scale, shift, perm[...], img[...])
    kept[...] = weights
    out[...] = to_images(weights, tile).astype(BF16)


def own_body(order, line, place, column, scale, shift, perm, img, img_other, kept, *refs):
    *txt, own_sum, own_txt, even_txt, near_txt, odd_txt = refs
    rows = own_txt.shape[0]
    tile = joined(txt)
    weights = weights_of(tile, order, line, place, column, scale, shift, perm[...], img[...])
    own_sum[...] = to_images(weights, tile)
    to_txt = to_texts(weights, img[...]) + to_texts(kept[...], img_other[...])
    half = rows + even_txt.shape[0]
    own_txt[...] = to_txt[:rows]
    even_txt[...] = to_txt[rows:half]
    near_txt[...] = to_txt[half : half + rows].astype(BF16)
    odd_txt[...] = to_txt[half + rows :].astype(BF16)


def add_body(even, got, *outs):
    rows = outs[0].shape[0]
    for k, out in enumerate(outs):
        mine = even[k * rows : (k + 1) * rows, :]
        out[...] = (mine + got[k * rows : (k + 1) * rows, :].astype(F32)).astype(BF16)


def split_body(count, position, own, other, keep, *send):
    rows = keep.shape[0]
    for k in range(count):
        start = pl.multiple_of((position[0] ^ k) * rows, rows)
        part = own[pl.ds(start, rows), :] + other[pl.ds(start, rows), :].astype(F32)
        if k == 0:
            keep[...] = part
        else:
            send[k - 1][...] = part.astype(BF16)


def total_of(own, parts):
    total = own[...]
    for part in parts:
        total = total + part[...].astype(F32)
    return total


def backward_unit(unit, inverse, upstream):
    along = jnp.sum(unit * upstream, axis=1, keepdims=True)
    return inverse[:, :1] * (upstream - unit * along)


def finish_img_body(scale, unit, inverse, own, *refs):
    *parts, out = refs
    out[...] = backward_unit(
        unit[...], inverse[...], scale[0] * total_of(own, parts)
    ).astype(BF16)


def last_body(count, place, scale, unit, inverse, own, *refs):
    parts = refs[:count]
    *back, img_out, txt_out, img_held, txt_held, sems = refs[count:]
    rows = parts[0].shape[0]
    copies = []
    for k in range(count):
        img_held[k * rows : (k + 1) * rows, :] = parts[k][...].astype(F32)
        start = pl.multiple_of((place[0] ^ k) * rows, rows)
        copies.append(
            pltpu.make_async_copy(
                img_held.at[pl.ds(k * rows, rows), :],
                img_out.at[pl.ds(start, rows), :],
                sems.at[k],
            )
        )
        copies[-1].start()
    txt_held[...] = backward_unit(unit[...], inverse[...], scale[0] * total_of(own, back))
    copies.append(pltpu.make_async_copy(txt_held, txt_out, sems.at[count]))
    copies[-1].start()
    for copy in copies:
        copy.wait()


def swapped(value, axis, step):
    count = lax.axis_size(axis)
    return lax.ppermute(value, axis, [(s, s ^ step) for s in range(count)])


def local(images, texts, perm, scale, shift):
    rows, width = images.shape
    txt_rows = texts.shape[0]
    line = lax.axis_size("txt")
    blocks = line // 2
    count = lax.axis_size("img")
    part = rows // count
    column = lax.axis_index("txt").reshape(1).astype(jnp.int32)
    place = lax.axis_index("img").reshape(1).astype(jnp.int32)
    perm_row = perm.reshape(1, rows)

    perm_other = swapped(perm_row, "txt", 1)
    raw_other = swapped(images, "txt", 1)
    txt_bf, txt_unit, txt_inv = call(
        unit_txt_body,
        [struct(txt_rows, width, BF16), struct(txt_rows, width, F32), struct(txt_rows, 128, F32)],
        [in_hbm(texts)],
        [ANY],
        16 << 20,
        4 * txt_rows * width,
        [pltpu.VMEM((txt_rows, width), F32), pltpu.SemaphoreType.DMA],
    )
    half = blocks // 2
    order = list(range(0, blocks, 2)) + list(range(1, blocks, 2))
    far = [swapped(txt_bf, "txt", 4 * k) for k in range(1, half)]
    near = [swapped(tile, "txt", 2) for tile in [txt_bf] + far]
    tiles = [txt_bf] + far + near
    img_bf, img_other, img_unit, img_inv = call(
        unit_img_body,
        [struct(rows, width, BF16)] * 2 + [struct(part, width, F32), struct(part, 128, F32)],
        [place, raw_other, in_hbm(images)],
        [SMEM, VMEM, ANY],
        24 << 20,
        8 * rows * width,
        [pltpu.VMEM((rows, width), F32), pltpu.SemaphoreType.DMA],
    )
    scalars = [place, column, scale, shift]
    pairs = 2 * rows * blocks * txt_rows * width
    kept, other_img = call(
        functools.partial(other_body, order, line),
        [struct(blocks * txt_rows, rows, BF16), struct(rows, width, BF16)],
        [*scalars, perm_other, img_other, *tiles],
        [SMEM] * 4 + [VMEM] * (2 + blocks),
        40 << 20,
        2 * pairs,
    )
    from_other = swapped(other_img, "txt", 1)
    own_img, own_txt, even_txt, near_txt, odd_txt = call(
        functools.partial(own_body, order, line),
        [
            struct(rows, width, F32),
            struct(txt_rows, width, F32),
            struct((half - 1) * txt_rows, width, F32),
            struct(txt_rows, width, BF16),
            struct((half - 1) * txt_rows, width, BF16),
        ],
        [*scalars, perm_row, img_bf, img_other, kept, *tiles],
        [SMEM] * 4 + [VMEM] * (4 + blocks),
        40 << 20,
        4 * pairs,
    )
    sums = call(
        add_body,
        [struct(txt_rows, width, BF16)] * (half - 1),
        [even_txt, swapped(odd_txt, "txt", 2)],
        [VMEM] * 2,
        24 << 20,
        rows * width,
    )
    back = [swapped(near_txt, "txt", 2)] + [swapped(sums[k - 1], "txt", 4 * k) for k in range(1, half)]

    keep, *send = call(
        functools.partial(split_body, count),
        [struct(part, width, F32)] + [struct(part, width, BF16)] * (count - 1),
        [place, own_img, from_other],
        [SMEM, VMEM, VMEM],
        24 << 20,
        rows * width,
    )
    got = [swapped(send[k - 1], "img", k) for k in range(1, count)]
    (grad_part,) = call(
        finish_img_body,
        [struct(part, width, BF16)],
        [scale, img_unit, img_inv, keep, *got],
        [SMEM] + [VMEM] * (2 + count),
        24 << 20,
        10 * part * width,
    )
    grads = [grad_part] + [swapped(grad_part, "img", k) for k in range(1, count)]
    return pl.pallas_call(
        functools.partial(last_body, count),
        out_shape=[struct(rows, width, F32), struct(txt_rows, width, F32)],
        in_specs=[SMEM] * 2 + [VMEM] * (3 + count + half),
        out_specs=[ANY] * 2,
        scratch_shapes=[
            pltpu.VMEM((rows, width), F32),
            pltpu.VMEM((txt_rows, width), F32),
            pltpu.SemaphoreType.DMA((count + 1,)),
        ],
        compiler_params=pltpu.CompilerParams(vmem_limit_bytes=24 << 20),
        cost_estimate=pl.CostEstimate(
            flops=10 * txt_rows * width, bytes_accessed=8 * rows * width, transcendentals=0
        ),
    )(place, scale, txt_unit, txt_inv, own_txt, *grads, *back)


def solution(mesh):
    placed = (P("txt", None), P(("img", "txt"), None), P("txt"), P(), P())
    return jax.shard_map(
        local,
        mesh=mesh,
        in_specs=placed,
        out_specs=(P("txt", None), P(("img", "txt"), None)),
        check_vma=False,
    )
```

```python
import functools

import jax
import jax.numpy as jnp
from jax import lax
from jax.experimental import pallas as pl
from jax.experimental.pallas import tpu as pltpu
from jax.sharding import PartitionSpec as P

EPSILON = 1e-06
F32 = jnp.float32
BF16 = jnp.bfloat16
VMEM = pl.BlockSpec(memory_space=pltpu.VMEM)
ANY = pl.BlockSpec(memory_space=pl.ANY)
SMEM = pl.BlockSpec(memory_space=pltpu.SMEM)


def in_hbm(value):
    return pltpu.with_memory_space_constraint(value, pltpu.HBM)


def call(body, outs, args, specs, limit, flops, scratch=()):
    size = sum(a.size * a.dtype.itemsize for a in args)
    size += sum(o.size * o.dtype.itemsize for o in outs)
    return pl.pallas_call(
        body,
        out_shape=outs,
        in_specs=specs,
        out_specs=[VMEM] * len(outs),
        scratch_shapes=scratch,
        compiler_params=pltpu.CompilerParams(vmem_limit_bytes=limit),
        cost_estimate=pl.CostEstimate(flops=flops, bytes_accessed=size, transcendentals=0),
    )(*args)


def struct(rows, cols, dtype):
    return jax.ShapeDtypeStruct((rows, cols), dtype)


def inverse_norm(values):
    return lax.rsqrt(jnp.sum(values * values, axis=1, keepdims=True) + EPSILON)


def unit_txt_body(source, bf, unit_out, inv, held, sem):
    copy = pltpu.make_async_copy(source, held, sem)
    copy.start()
    copy.wait()
    values = held[...]
    inverse = inverse_norm(values)
    unit = values * inverse
    bf[...] = unit.astype(BF16)
    unit_out[...] = unit
    inv[...] = jnp.broadcast_to(inverse, inv.shape)


def unit_img_body(place, other, source, bf, other_bf, unit_out, inv, held, sem):
    copy = pltpu.make_async_copy(source, held, sem)
    copy.start()
    values = other[...]
    other_bf[...] = (values * inverse_norm(values)).astype(BF16)
    copy.wait()
    values = held[...]
    bf[...] = (values * inverse_norm(values)).astype(BF16)
    rows = unit_out.shape[0]
    values = held[pl.ds(pl.multiple_of(place[0] * rows, rows), rows), :]
    inverse = inverse_norm(values)
    unit_out[...] = values * inverse
    inv[...] = jnp.broadcast_to(inverse, inv.shape)


def weights_of(tile, order, line, place, column, scale, shift, perm, img):
    rows = tile.shape[0] // len(order)
    row = lax.broadcasted_iota(jnp.int32, (rows, 1), 0)
    ids = jnp.concatenate(
        [row + (place[0] * line + (column[0] ^ (2 * k))) * rows for k in order], axis=0
    )
    products = lax.dot_general(tile, img, (((1,), (1,)), ((), ())), preferred_element_type=F32)
    positive = (ids == perm).astype(F32)
    return (jax.nn.sigmoid(scale[0] * products + shift[0]) - positive).astype(BF16)


def to_images(weights, tile):
    return lax.dot_general(weights, tile, (((0,), (0,)), ((), ())), preferred_element_type=F32)


def to_texts(weights, img):
    return jnp.dot(weights, img, preferred_element_type=F32)


def joined(tiles):
    return jnp.concatenate([t[...] for t in tiles], axis=0)


def other_body(order, line, place, column, scale, shift, perm, img, *refs):
    *txt, kept, out = refs
    tile = joined(txt)
    weights = weights_of(tile, order, line, place, column, scale, shift, perm[...], img[...])
    kept[...] = weights
    out[...] = to_images(weights, tile).astype(BF16)


def own_body(order, line, place, column, scale, shift, perm, img, img_other, kept, *refs):
    *txt, own_sum, own_txt, even_txt, near_txt, odd_txt = refs
    rows = own_txt.shape[0]
    tile = joined(txt)
    weights = weights_of(tile, order, line, place, column, scale, shift, perm[...], img[...])
    own_sum[...] = to_images(weights, tile)
    to_txt = to_texts(weights, img[...]) + to_texts(kept[...], img_other[...])
    half = rows + even_txt.shape[0]
    own_txt[...] = to_txt[:rows]
    even_txt[...] = to_txt[rows:half]
    near_txt[...] = to_txt[half : half + rows].astype(BF16)
    odd_txt[...] = to_txt[half + rows :].astype(BF16)


def add_body(even, got, *outs):
    rows = outs[0].shape[0]
    for k, out in enumerate(outs):
        mine = even[k * rows : (k + 1) * rows, :]
        out[...] = (mine + got[k * rows : (k + 1) * rows, :].astype(F32)).astype(BF16)


def split_body(count, position, own, other, keep, *send):
    rows = keep.shape[0]
    for k in range(count):
        start = pl.multiple_of((position[0] ^ k) * rows, rows)
        part = own[pl.ds(start, rows), :] + other[pl.ds(start, rows), :].astype(F32)
        if k == 0:
            keep[...] = part
        else:
            send[k - 1][...] = part.astype(BF16)


def total_of(own, parts):
    total = own[...]
    for part in parts:
        total = total + part[...].astype(F32)
    return total


def backward_unit(unit, inverse, upstream):
    along = jnp.sum(unit * upstream, axis=1, keepdims=True)
    return inverse[:, :1] * (upstream - unit * along)


def finish_img_body(scale, unit, inverse, own, *refs):
    *parts, out = refs
    out[...] = backward_unit(
        unit[...], inverse[...], scale[0] * total_of(own, parts)
    ).astype(BF16)


def last_body(count, place, scale, unit, inverse, own, *refs):
    parts = refs[:count]
    *back, img_out, txt_out, img_held, txt_held, sems = refs[count:]
    rows = parts[0].shape[0]
    copies = []
    for k in range(count):
        img_held[k * rows : (k + 1) * rows, :] = parts[k][...].astype(F32)
        start = pl.multiple_of((place[0] ^ k) * rows, rows)
        copies.append(
            pltpu.make_async_copy(
                img_held.at[pl.ds(k * rows, rows), :],
                img_out.at[pl.ds(start, rows), :],
                sems.at[k],
            )
        )
        copies[-1].start()
    txt_held[...] = backward_unit(unit[...], inverse[...], scale[0] * total_of(own, back))
    copies.append(pltpu.make_async_copy(txt_held, txt_out, sems.at[count]))
    copies[-1].start()
    for copy in copies:
        copy.wait()


def swapped(value, axis, step):
    count = lax.axis_size(axis)
    return lax.ppermute(value, axis, [(s, s ^ step) for s in range(count)])


def local(images, texts, perm, scale, shift):
    rows, width = images.shape
    txt_rows = texts.shape[0]
    line = lax.axis_size("txt")
    blocks = line // 2
    count = lax.axis_size("img")
    part = rows // count
    column = lax.axis_index("txt").reshape(1).astype(jnp.int32)
    place = lax.axis_index("img").reshape(1).astype(jnp.int32)
    perm_row = perm.reshape(1, rows)

    perm_other = swapped(perm_row, "txt", 1)
    raw_other = swapped(images, "txt", 1)
    txt_bf, txt_unit, txt_inv = call(
        unit_txt_body,
        [struct(txt_rows, width, BF16), struct(txt_rows, width, F32), struct(txt_rows, 128, F32)],
        [in_hbm(texts)],
        [ANY],
        16 << 20,
        4 * txt_rows * width,
        [pltpu.VMEM((txt_rows, width), F32), pltpu.SemaphoreType.DMA],
    )
    half = blocks // 2
    order = list(range(0, blocks, 2)) + list(range(1, blocks, 2))
    far = [swapped(txt_bf, "txt", 4 * k) for k in range(1, half)]
    near = [swapped(tile, "txt", 2) for tile in [txt_bf] + far]
    tiles = [txt_bf] + far + near
    img_bf, img_other, img_unit, img_inv = call(
        unit_img_body,
        [struct(rows, width, BF16)] * 2 + [struct(part, width, F32), struct(part, 128, F32)],
        [place, raw_other, in_hbm(images)],
        [SMEM, VMEM, ANY],
        24 << 20,
        8 * rows * width,
        [pltpu.VMEM((rows, width), F32), pltpu.SemaphoreType.DMA],
    )
    scalars = [place, column, scale, shift]
    pairs = 2 * rows * blocks * txt_rows * width
    kept, other_img = call(
        functools.partial(other_body, order, line),
        [struct(blocks * txt_rows, rows, BF16), struct(rows, width, BF16)],
        [*scalars, perm_other, img_other, *tiles],
        [SMEM] * 4 + [VMEM] * (2 + blocks),
        40 << 20,
        2 * pairs,
    )
    from_other = swapped(other_img, "txt", 1)
    own_img, own_txt, even_txt, near_txt, odd_txt = call(
        functools.partial(own_body, order, line),
        [
            struct(rows, width, F32),
            struct(txt_rows, width, F32),
            struct((half - 1) * txt_rows, width, F32),
            struct(txt_rows, width, BF16),
            struct((half - 1) * txt_rows, width, BF16),
        ],
        [*scalars, perm_row, img_bf, img_other, kept, *tiles],
        [SMEM] * 4 + [VMEM] * (4 + blocks),
        40 << 20,
        4 * pairs,
    )
    sums = call(
        add_body,
        [struct(txt_rows, width, BF16)] * (half - 1),
        [even_txt, swapped(odd_txt, "txt", 2)],
        [VMEM] * 2,
        24 << 20,
        rows * width,
    )
    back = [swapped(near_txt, "txt", 2)] + [swapped(sums[k - 1], "txt", 4 * k) for k in range(1, half)]

    keep, *send = call(
        functools.partial(split_body, count),
        [struct(part, width, F32)] + [struct(part, width, BF16)] * (count - 1),
        [place, own_img, from_other],
        [SMEM, VMEM, VMEM],
        24 << 20,
        rows * width,
    )
    got = [swapped(send[k - 1], "img", k) for k in range(count - 1, 0, -1)]
    (grad_part,) = call(
        finish_img_body,
        [struct(part, width, BF16)],
        [scale, img_unit, img_inv, keep, *got],
        [SMEM] + [VMEM] * (2 + count),
        24 << 20,
        10 * part * width,
    )
    grads = [grad_part] + [swapped(grad_part, "img", k) for k in range(1, count)]
    return pl.pallas_call(
        functools.partial(last_body, count),
        out_shape=[struct(rows, width, F32), struct(txt_rows, width, F32)],
        in_specs=[SMEM] * 2 + [VMEM] * (3 + count + half),
        out_specs=[ANY] * 2,
        scratch_shapes=[
            pltpu.VMEM((rows, width), F32),
            pltpu.VMEM((txt_rows, width), F32),
            pltpu.SemaphoreType.DMA((count + 1,)),
        ],
        compiler_params=pltpu.CompilerParams(vmem_limit_bytes=24 << 20),
        cost_estimate=pl.CostEstimate(
            flops=10 * txt_rows * width, bytes_accessed=8 * rows * width, transcendentals=0
        ),
    )(place, scale, txt_unit, txt_inv, own_txt, *grads, *back)


def solution(mesh):
    placed = (P("txt", None), P(("img", "txt"), None), P("txt"), P(), P())
    return jax.shard_map(
        local,
        mesh=mesh,
        in_specs=placed,
        out_specs=(P("txt", None), P(("img", "txt"), None)),
        check_vma=False,
    )
```

```python
import functools

import jax
import jax.numpy as jnp
from jax import lax
from jax.experimental import pallas as pl
from jax.experimental.pallas import tpu as pltpu
from jax.sharding import PartitionSpec as P

EPSILON = 1e-06
F32 = jnp.float32
BF16 = jnp.bfloat16
VMEM = pl.BlockSpec(memory_space=pltpu.VMEM)
ANY = pl.BlockSpec(memory_space=pl.ANY)
SMEM = pl.BlockSpec(memory_space=pltpu.SMEM)


def in_hbm(value):
    return pltpu.with_memory_space_constraint(value, pltpu.HBM)


def call(body, outs, args, specs, limit, flops, scratch=()):
    size = sum(a.size * a.dtype.itemsize for a in args)
    size += sum(o.size * o.dtype.itemsize for o in outs)
    return pl.pallas_call(
        body,
        out_shape=outs,
        in_specs=specs,
        out_specs=[VMEM] * len(outs),
        scratch_shapes=scratch,
        compiler_params=pltpu.CompilerParams(vmem_limit_bytes=limit),
        cost_estimate=pl.CostEstimate(flops=flops, bytes_accessed=size, transcendentals=0),
    )(*args)


def struct(rows, cols, dtype):
    return jax.ShapeDtypeStruct((rows, cols), dtype)


def inverse_norm(values):
    return lax.rsqrt(jnp.sum(values * values, axis=1, keepdims=True) + EPSILON)


def unit_txt_body(source, bf, head, tail, unit_out, inv, held, sem):
    copy = pltpu.make_async_copy(source, held, sem)
    copy.start()
    copy.wait()
    values = held[...]
    inverse = inverse_norm(values)
    unit = values * inverse
    rounded = unit.astype(BF16)
    bf[...] = rounded
    head[...] = rounded[: head.shape[0]]
    tail[...] = rounded[head.shape[0] :]
    unit_out[...] = unit
    inv[...] = jnp.broadcast_to(inverse, inv.shape)


def unit_img_body(place, other, source, bf, other_bf, unit_out, inv, held, sem):
    copy = pltpu.make_async_copy(source, held, sem)
    copy.start()
    values = other[...]
    other_bf[...] = (values * inverse_norm(values)).astype(BF16)
    copy.wait()
    values = held[...]
    bf[...] = (values * inverse_norm(values)).astype(BF16)
    rows = unit_out.shape[0]
    values = held[pl.ds(pl.multiple_of(place[0] * rows, rows), rows), :]
    inverse = inverse_norm(values)
    unit_out[...] = values * inverse
    inv[...] = jnp.broadcast_to(inverse, inv.shape)


def weights_of(tile, order, line, place, column, scale, shift, perm, img):
    rows = tile.shape[0] // len(order)
    row = lax.broadcasted_iota(jnp.int32, (rows, 1), 0)
    ids = jnp.concatenate(
        [row + (place[0] * line + (column[0] ^ (2 * k))) * rows for k in order], axis=0
    )
    products = lax.dot_general(tile, img, (((1,), (1,)), ((), ())), preferred_element_type=F32)
    positive = (ids == perm).astype(F32)
    return (jax.nn.sigmoid(scale[0] * products + shift[0]) - positive).astype(BF16)


def to_images(weights, tile):
    return lax.dot_general(weights, tile, (((0,), (0,)), ((), ())), preferred_element_type=F32)


def to_texts(weights, img):
    return jnp.dot(weights, img, preferred_element_type=F32)


def joined(tiles):
    return jnp.concatenate([t[...] for t in tiles], axis=0)


def other_body(order, line, place, column, scale, shift, perm, img, *refs):
    *txt, kept, out = refs
    tile = joined(txt)
    weights = weights_of(tile, order, line, place, column, scale, shift, perm[...], img[...])
    kept[...] = weights
    out[...] = to_images(weights, tile).astype(BF16)


def own_body(order, line, place, column, scale, shift, perm, img, img_other, kept, *refs):
    *txt, own_sum, own_txt, even_txt, near_txt, odd_txt = refs
    rows = own_txt.shape[0]
    tile = joined(txt)
    weights = weights_of(tile, order, line, place, column, scale, shift, perm[...], img[...])
    own_sum[...] = to_images(weights, tile)
    to_txt = to_texts(weights, img[...]) + to_texts(kept[...], img_other[...])
    half = rows + even_txt.shape[0]
    own_txt[...] = to_txt[:rows]
    even_txt[...] = to_txt[rows:half]
    near_txt[...] = to_txt[half : half + rows].astype(BF16)
    odd_txt[...] = to_txt[half + rows :].astype(BF16)


def add_body(even, got, *outs):
    rows = outs[0].shape[0]
    for k, out in enumerate(outs):
        mine = even[k * rows : (k + 1) * rows, :]
        out[...] = (mine + got[k * rows : (k + 1) * rows, :].astype(F32)).astype(BF16)


def split_body(count, position, own, other, keep, *send):
    rows = keep.shape[0]
    for k in range(count):
        start = pl.multiple_of((position[0] ^ k) * rows, rows)
        part = own[pl.ds(start, rows), :] + other[pl.ds(start, rows), :].astype(F32)
        if k == 0:
            keep[...] = part
        else:
            send[k - 1][...] = part.astype(BF16)


def total_of(own, parts):
    total = own[...]
    for part in parts:
        total = total + part[...].astype(F32)
    return total


def backward_unit(unit, inverse, upstream):
    along = jnp.sum(unit * upstream, axis=1, keepdims=True)
    return inverse[:, :1] * (upstream - unit * along)


def finish_img_body(scale, unit, inverse, own, *refs):
    *parts, out = refs
    out[...] = backward_unit(
        unit[...], inverse[...], scale[0] * total_of(own, parts)
    ).astype(BF16)


def last_body(count, place, scale, unit, inverse, own, *refs):
    parts = refs[:count]
    *back, img_out, txt_out, img_held, txt_held, sems = refs[count:]
    rows = parts[0].shape[0]
    copies = []
    for k in range(count):
        img_held[k * rows : (k + 1) * rows, :] = parts[k][...].astype(F32)
        start = pl.multiple_of((place[0] ^ k) * rows, rows)
        copies.append(
            pltpu.make_async_copy(
                img_held.at[pl.ds(k * rows, rows), :],
                img_out.at[pl.ds(start, rows), :],
                sems.at[k],
            )
        )
        copies[-1].start()
    txt_held[...] = backward_unit(unit[...], inverse[...], scale[0] * total_of(own, back))
    copies.append(pltpu.make_async_copy(txt_held, txt_out, sems.at[count]))
    copies[-1].start()
    for copy in copies:
        copy.wait()


def swapped(value, axis, step):
    count = lax.axis_size(axis)
    return lax.ppermute(value, axis, [(s, s ^ step) for s in range(count)])


def local(images, texts, perm, scale, shift):
    rows, width = images.shape
    txt_rows = texts.shape[0]
    line = lax.axis_size("txt")
    blocks = line // 2
    count = lax.axis_size("img")
    part = rows // count
    column = lax.axis_index("txt").reshape(1).astype(jnp.int32)
    place = lax.axis_index("img").reshape(1).astype(jnp.int32)
    perm_row = perm.reshape(1, rows)

    perm_other = swapped(perm_row, "txt", 1)
    raw_other = swapped(images, "txt", 1)
    first = txt_rows // 2
    txt_bf, head, tail, txt_unit, txt_inv = call(
        unit_txt_body,
        [struct(size, width, BF16) for size in (txt_rows, first, txt_rows - first)]
        + [struct(txt_rows, width, F32), struct(txt_rows, 128, F32)],
        [in_hbm(texts)],
        [ANY],
        16 << 20,
        4 * txt_rows * width,
        [pltpu.VMEM((txt_rows, width), F32), pltpu.SemaphoreType.DMA],
    )
    half = blocks // 2
    order = list(range(0, blocks, 2)) + list(range(1, blocks, 2))
    far = [swapped(piece, "txt", 4 * k) for k in range(1, half) for piece in (head, tail)]
    near = [swapped(tile, "txt", 2) for tile in [txt_bf] + far]
    tiles = [txt_bf] + far + near
    img_bf, img_other, img_unit, img_inv = call(
        unit_img_body,
        [struct(rows, width, BF16)] * 2 + [struct(part, width, F32), struct(part, 128, F32)],
        [place, raw_other, in_hbm(images)],
        [SMEM, VMEM, ANY],
        24 << 20,
        8 * rows * width,
        [pltpu.VMEM((rows, width), F32), pltpu.SemaphoreType.DMA],
    )
    scalars = [place, column, scale, shift]
    pairs = 2 * rows * blocks * txt_rows * width
    kept, other_img = call(
        functools.partial(other_body, order, line),
        [struct(blocks * txt_rows, rows, BF16), struct(rows, width, BF16)],
        [*scalars, perm_other, img_other, *tiles],
        [SMEM] * 4 + [VMEM] * (2 + len(tiles)),
        40 << 20,
        2 * pairs,
    )
    from_other = swapped(other_img, "txt", 1)
    own_img, own_txt, even_txt, near_txt, odd_txt = call(
        functools.partial(own_body, order, line),
        [
            struct(rows, width, F32),
            struct(txt_rows, width, F32),
            struct((half - 1) * txt_rows, width, F32),
            struct(txt_rows, width, BF16),
            struct((half - 1) * txt_rows, width, BF16),
        ],
        [*scalars, perm_row, img_bf, img_other, kept, *tiles],
        [SMEM] * 4 + [VMEM] * (4 + len(tiles)),
        40 << 20,
        4 * pairs,
    )
    sums = call(
        add_body,
        [struct(txt_rows, width, BF16)] * (half - 1),
        [even_txt, swapped(odd_txt, "txt", 2)],
        [VMEM] * 2,
        24 << 20,
        rows * width,
    )
    back = [swapped(near_txt, "txt", 2)] + [swapped(sums[k - 1], "txt", 4 * k) for k in range(1, half)]

    keep, *send = call(
        functools.partial(split_body, count),
        [struct(part, width, F32)] + [struct(part, width, BF16)] * (count - 1),
        [place, own_img, from_other],
        [SMEM, VMEM, VMEM],
        24 << 20,
        rows * width,
    )
    got = [swapped(send[k - 1], "img", k) for k in range(1, count)]
    (grad_part,) = call(
        finish_img_body,
        [struct(part, width, BF16)],
        [scale, img_unit, img_inv, keep, *got],
        [SMEM] + [VMEM] * (2 + count),
        24 << 20,
        10 * part * width,
    )
    grads = [grad_part] + [swapped(grad_part, "img", k) for k in range(1, count)]
    return pl.pallas_call(
        functools.partial(last_body, count),
        out_shape=[struct(rows, width, F32), struct(txt_rows, width, F32)],
        in_specs=[SMEM] * 2 + [VMEM] * (3 + count + half),
        out_specs=[ANY] * 2,
        scratch_shapes=[
            pltpu.VMEM((rows, width), F32),
            pltpu.VMEM((txt_rows, width), F32),
            pltpu.SemaphoreType.DMA((count + 1,)),
        ],
        compiler_params=pltpu.CompilerParams(vmem_limit_bytes=24 << 20),
        cost_estimate=pl.CostEstimate(
            flops=10 * txt_rows * width, bytes_accessed=8 * rows * width, transcendentals=0
        ),
    )(place, scale, txt_unit, txt_inv, own_txt, *grads, *back)


def solution(mesh):
    placed = (P("txt", None), P(("img", "txt"), None), P("txt"), P(), P())
    return jax.shard_map(
        local,
        mesh=mesh,
        in_specs=placed,
        out_specs=(P("txt", None), P(("img", "txt"), None)),
        check_vma=False,
    )
```

```python
import functools

import jax
import jax.numpy as jnp
from jax import lax
from jax.experimental import pallas as pl
from jax.experimental.pallas import tpu as pltpu
from jax.sharding import PartitionSpec as P

EPSILON = 1e-06
F32 = jnp.float32
BF16 = jnp.bfloat16
VMEM = pl.BlockSpec(memory_space=pltpu.VMEM)
ANY = pl.BlockSpec(memory_space=pl.ANY)
SMEM = pl.BlockSpec(memory_space=pltpu.SMEM)


def in_hbm(value):
    return pltpu.with_memory_space_constraint(value, pltpu.HBM)


def call(body, outs, args, specs, limit, flops, scratch=()):
    size = sum(a.size * a.dtype.itemsize for a in args)
    size += sum(o.size * o.dtype.itemsize for o in outs)
    return pl.pallas_call(
        body,
        out_shape=outs,
        in_specs=specs,
        out_specs=[VMEM] * len(outs),
        scratch_shapes=scratch,
        compiler_params=pltpu.CompilerParams(vmem_limit_bytes=limit),
        cost_estimate=pl.CostEstimate(flops=flops, bytes_accessed=size, transcendentals=0),
    )(*args)


def struct(rows, cols, dtype):
    return jax.ShapeDtypeStruct((rows, cols), dtype)


def inverse_norm(values):
    return lax.rsqrt(jnp.sum(values * values, axis=1, keepdims=True) + EPSILON)


def unit_txt_body(source, bf, head, tail, unit_out, inv, held, sem):
    copy = pltpu.make_async_copy(source, held, sem)
    copy.start()
    copy.wait()
    values = held[...]
    inverse = inverse_norm(values)
    unit = values * inverse
    rounded = unit.astype(BF16)
    bf[...] = rounded
    head[...] = rounded[: head.shape[0]]
    tail[...] = rounded[head.shape[0] :]
    unit_out[...] = unit
    inv[...] = jnp.broadcast_to(inverse, inv.shape)


def unit_img_body(place, other, source, bf, other_bf, unit_out, inv, held, sem):
    copy = pltpu.make_async_copy(source, held, sem)
    copy.start()
    values = other[...]
    other_bf[...] = (values * inverse_norm(values)).astype(BF16)
    copy.wait()
    values = held[...]
    bf[...] = (values * inverse_norm(values)).astype(BF16)
    rows = unit_out.shape[0]
    values = held[pl.ds(pl.multiple_of(place[0] * rows, rows), rows), :]
    inverse = inverse_norm(values)
    unit_out[...] = values * inverse
    inv[...] = jnp.broadcast_to(inverse, inv.shape)


def weights_of(tile, order, line, place, column, scale, shift, perm, img):
    rows = tile.shape[0] // len(order)
    row = lax.broadcasted_iota(jnp.int32, (rows, 1), 0)
    ids = jnp.concatenate(
        [row + (place[0] * line + (column[0] ^ (2 * k))) * rows for k in order], axis=0
    )
    products = lax.dot_general(tile, img, (((1,), (1,)), ((), ())), preferred_element_type=F32)
    positive = (ids == perm).astype(F32)
    return (jax.nn.sigmoid(scale[0] * products + shift[0]) - positive).astype(BF16)


def to_images(weights, tile):
    return lax.dot_general(weights, tile, (((0,), (0,)), ((), ())), preferred_element_type=F32)


def to_texts(weights, img):
    return jnp.dot(weights, img, preferred_element_type=F32)


def joined(tiles):
    return jnp.concatenate([t[...] for t in tiles], axis=0)


def other_body(order, line, place, column, scale, shift, perm, img, *refs):
    *txt, kept, out = refs
    tile = joined(txt)
    weights = weights_of(tile, order, line, place, column, scale, shift, perm[...], img[...])
    kept[...] = weights
    out[...] = to_images(weights, tile).astype(BF16)


def own_body(order, line, place, column, scale, shift, perm, img, img_other, kept, *refs):
    *txt, own_sum, own_txt, even_txt, near_txt, odd_txt = refs
    rows = own_txt.shape[0]
    tile = joined(txt)
    weights = weights_of(tile, order, line, place, column, scale, shift, perm[...], img[...])
    own_sum[...] = to_images(weights, tile)
    to_txt = to_texts(weights, img[...]) + to_texts(kept[...], img_other[...])
    half = rows + even_txt.shape[0]
    own_txt[...] = to_txt[:rows]
    even_txt[...] = to_txt[rows:half]
    near_txt[...] = to_txt[half : half + rows].astype(BF16)
    odd_txt[...] = to_txt[half + rows :].astype(BF16)


def add_body(even, got, *outs):
    rows = outs[0].shape[0]
    for k, out in enumerate(outs):
        mine = even[k * rows : (k + 1) * rows, :]
        out[...] = (mine + got[k * rows : (k + 1) * rows, :].astype(F32)).astype(BF16)


def split_body(partners, place, column, own, other, keep, *send):
    rows = keep.shape[0]
    core = column[0] & 1
    for out, (even, odd) in zip([keep, *send], [(0, 0), *partners]):
        block = place[0] ^ (even + core * (odd - even))
        start = pl.multiple_of(block * rows, rows)
        part = own[pl.ds(start, rows), :] + other[pl.ds(start, rows), :].astype(F32)
        out[...] = part.astype(out.dtype)


def total_of(own, parts):
    total = own[...]
    for part in parts:
        total = total + part[...].astype(F32)
    return total


def backward_unit(unit, inverse, upstream):
    along = jnp.sum(unit * upstream, axis=1, keepdims=True)
    return inverse[:, :1] * (upstream - unit * along)


def finish_img_body(scale, unit, inverse, own, *refs):
    *parts, out = refs
    out[...] = backward_unit(
        unit[...], inverse[...], scale[0] * total_of(own, parts)
    ).astype(BF16)


def last_body(count, place, scale, unit, inverse, own, *refs):
    parts = refs[:count]
    *back, img_out, txt_out, img_held, txt_held, sems = refs[count:]
    rows = parts[0].shape[0]
    copies = []
    for k in range(count):
        img_held[k * rows : (k + 1) * rows, :] = parts[k][...].astype(F32)
        start = pl.multiple_of((place[0] ^ k) * rows, rows)
        copies.append(
            pltpu.make_async_copy(
                img_held.at[pl.ds(k * rows, rows), :],
                img_out.at[pl.ds(start, rows), :],
                sems.at[k],
            )
        )
        copies[-1].start()
    txt_held[...] = backward_unit(unit[...], inverse[...], scale[0] * total_of(own, back))
    copies.append(pltpu.make_async_copy(txt_held, txt_out, sems.at[count]))
    copies[-1].start()
    for copy in copies:
        copy.wait()


def swapped(value, axis, step):
    count = lax.axis_size(axis)
    return lax.ppermute(value, axis, [(s, s ^ step) for s in range(count)])


def plane_swapped(value, even, odd):
    count, line = lax.axis_size("img"), lax.axis_size("txt")
    pairs = [
        (i * line + t, (i ^ (odd if t % 2 else even)) * line + t)
        for i in range(count)
        for t in range(line)
    ]
    return lax.ppermute(value, ("img", "txt"), pairs)


def local(images, texts, perm, scale, shift):
    rows, width = images.shape
    txt_rows = texts.shape[0]
    line = lax.axis_size("txt")
    blocks = line // 2
    count = lax.axis_size("img")
    part = rows // count
    column = lax.axis_index("txt").reshape(1).astype(jnp.int32)
    place = lax.axis_index("img").reshape(1).astype(jnp.int32)
    perm_row = perm.reshape(1, rows)

    perm_other = swapped(perm_row, "txt", 1)
    raw_other = swapped(images, "txt", 1)
    first = txt_rows // 2
    txt_bf, head, tail, txt_unit, txt_inv = call(
        unit_txt_body,
        [struct(size, width, BF16) for size in (txt_rows, first, txt_rows - first)]
        + [struct(txt_rows, width, F32), struct(txt_rows, 128, F32)],
        [in_hbm(texts)],
        [ANY],
        16 << 20,
        4 * txt_rows * width,
        [pltpu.VMEM((txt_rows, width), F32), pltpu.SemaphoreType.DMA],
    )
    half = blocks // 2
    order = list(range(0, blocks, 2)) + list(range(1, blocks, 2))
    far = [swapped(piece, "txt", 4 * k) for k in range(1, half) for piece in (head, tail)]
    near = [swapped(tile, "txt", 2) for tile in [txt_bf] + far]
    tiles = [txt_bf] + far + near
    img_bf, img_other, img_unit, img_inv = call(
        unit_img_body,
        [struct(rows, width, BF16)] * 2 + [struct(part, width, F32), struct(part, 128, F32)],
        [place, raw_other, in_hbm(images)],
        [SMEM, VMEM, ANY],
        24 << 20,
        8 * rows * width,
        [pltpu.VMEM((rows, width), F32), pltpu.SemaphoreType.DMA],
    )
    scalars = [place, column, scale, shift]
    pairs = 2 * rows * blocks * txt_rows * width
    kept, other_img = call(
        functools.partial(other_body, order, line),
        [struct(blocks * txt_rows, rows, BF16), struct(rows, width, BF16)],
        [*scalars, perm_other, img_other, *tiles],
        [SMEM] * 4 + [VMEM] * (2 + len(tiles)),
        40 << 20,
        2 * pairs,
    )
    from_other = swapped(other_img, "txt", 1)
    own_img, own_txt, even_txt, near_txt, odd_txt = call(
        functools.partial(own_body, order, line),
        [
            struct(rows, width, F32),
            struct(txt_rows, width, F32),
            struct((half - 1) * txt_rows, width, F32),
            struct(txt_rows, width, BF16),
            struct((half - 1) * txt_rows, width, BF16),
        ],
        [*scalars, perm_row, img_bf, img_other, kept, *tiles],
        [SMEM] * 4 + [VMEM] * (4 + len(tiles)),
        40 << 20,
        4 * pairs,
    )
    sums = call(
        add_body,
        [struct(txt_rows, width, BF16)] * (half - 1),
        [even_txt, swapped(odd_txt, "txt", 2)],
        [VMEM] * 2,
        24 << 20,
        rows * width,
    )
    back = [swapped(near_txt, "txt", 2)] + [swapped(sums[k - 1], "txt", 4 * k) for k in range(1, half)]

    partners = [(1, 2), (2, 1)] + [(k, k) for k in range(3, count)]
    keep, *send = call(
        functools.partial(split_body, partners),
        [struct(part, width, F32)] + [struct(part, width, BF16)] * (count - 1),
        [place, column, own_img, from_other],
        [SMEM] * 2 + [VMEM] * 2,
        24 << 20,
        rows * width,
    )
    got = [plane_swapped(block, *pair) for block, pair in zip(send, partners)]
    (grad_part,) = call(
        finish_img_body,
        [struct(part, width, BF16)],
        [scale, img_unit, img_inv, keep, *got],
        [SMEM] + [VMEM] * (2 + count),
        24 << 20,
        10 * part * width,
    )
    grads = [grad_part] + [swapped(grad_part, "img", k) for k in range(1, count)]
    return pl.pallas_call(
        functools.partial(last_body, count),
        out_shape=[struct(rows, width, F32), struct(txt_rows, width, F32)],
        in_specs=[SMEM] * 2 + [VMEM] * (3 + count + half),
        out_specs=[ANY] * 2,
        scratch_shapes=[
            pltpu.VMEM((rows, width), F32),
            pltpu.VMEM((txt_rows, width), F32),
            pltpu.SemaphoreType.DMA((count + 1,)),
        ],
        compiler_params=pltpu.CompilerParams(vmem_limit_bytes=24 << 20),
        cost_estimate=pl.CostEstimate(
            flops=10 * txt_rows * width, bytes_accessed=8 * rows * width, transcendentals=0
        ),
    )(place, scale, txt_unit, txt_inv, own_txt, *grads, *back)


def solution(mesh):
    placed = (P("txt", None), P(("img", "txt"), None), P("txt"), P(), P())
    return jax.shard_map(
        local,
        mesh=mesh,
        in_specs=placed,
        out_specs=(P("txt", None), P(("img", "txt"), None)),
        check_vma=False,
    )
```

```python
import functools

import jax
import jax.numpy as jnp
from jax import lax
from jax.experimental import pallas as pl
from jax.experimental.pallas import tpu as pltpu
from jax.sharding import PartitionSpec as P

EPSILON = 1e-06
F32 = jnp.float32
BF16 = jnp.bfloat16
VMEM = pl.BlockSpec(memory_space=pltpu.VMEM)
ANY = pl.BlockSpec(memory_space=pl.ANY)
SMEM = pl.BlockSpec(memory_space=pltpu.SMEM)


def in_hbm(value):
    return pltpu.with_memory_space_constraint(value, pltpu.HBM)


def call(body, outs, args, specs, limit, flops, scratch=()):
    size = sum(a.size * a.dtype.itemsize for a in args)
    size += sum(o.size * o.dtype.itemsize for o in outs)
    return pl.pallas_call(
        body,
        out_shape=outs,
        in_specs=specs,
        out_specs=[VMEM] * len(outs),
        scratch_shapes=scratch,
        compiler_params=pltpu.CompilerParams(vmem_limit_bytes=limit),
        cost_estimate=pl.CostEstimate(flops=flops, bytes_accessed=size, transcendentals=0),
    )(*args)


def struct(rows, cols, dtype):
    return jax.ShapeDtypeStruct((rows, cols), dtype)


def inverse_norm(values):
    return lax.rsqrt(jnp.sum(values * values, axis=1, keepdims=True) + EPSILON)


def unit_txt_body(source, bf, head, tail, unit_out, inv, held, sem):
    copy = pltpu.make_async_copy(source, held, sem)
    copy.start()
    copy.wait()
    values = held[...]
    inverse = inverse_norm(values)
    unit = values * inverse
    rounded = unit.astype(BF16)
    bf[...] = rounded
    head[...] = rounded[: head.shape[0]]
    tail[...] = rounded[head.shape[0] :]
    unit_out[...] = unit
    inv[...] = jnp.broadcast_to(inverse, inv.shape)


def unit_img_body(place, other, source, bf, other_bf, unit_out, inv, held, sem):
    copy = pltpu.make_async_copy(source, held, sem)
    copy.start()
    values = other[...]
    other_bf[...] = (values * inverse_norm(values)).astype(BF16)
    copy.wait()
    values = held[...]
    bf[...] = (values * inverse_norm(values)).astype(BF16)
    rows = unit_out.shape[0]
    values = held[pl.ds(pl.multiple_of(place[0] * rows, rows), rows), :]
    inverse = inverse_norm(values)
    unit_out[...] = values * inverse
    inv[...] = jnp.broadcast_to(inverse, inv.shape)


def weights_of(tile, order, line, place, column, scale, shift, perm, img):
    rows = tile.shape[0] // len(order)
    row = lax.broadcasted_iota(jnp.int32, (rows, 1), 0)
    ids = jnp.concatenate(
        [row + (place[0] * line + (column[0] ^ (2 * k))) * rows for k in order], axis=0
    )
    products = lax.dot_general(tile, img, (((1,), (1,)), ((), ())), preferred_element_type=F32)
    positive = (ids == perm).astype(F32)
    return (jax.nn.sigmoid(scale[0] * products + shift[0]) - positive).astype(BF16)


def to_images(weights, tile):
    return lax.dot_general(weights, tile, (((0,), (0,)), ((), ())), preferred_element_type=F32)


def to_texts(weights, img):
    return jnp.dot(weights, img, preferred_element_type=F32)


def joined(tiles):
    return jnp.concatenate([t[...] for t in tiles], axis=0)


def other_body(order, line, place, column, scale, shift, perm, img, *refs):
    *txt, kept, out = refs
    tile = joined(txt)
    weights = weights_of(tile, order, line, place, column, scale, shift, perm[...], img[...])
    kept[...] = weights
    out[...] = to_images(weights, tile).astype(BF16)


def own_body(order, line, place, column, scale, shift, perm, img, img_other, kept, *refs):
    *txt, own_sum, own_txt, even_txt, near_txt, odd_txt = refs
    rows = own_txt.shape[0]
    tile = joined(txt)
    weights = weights_of(tile, order, line, place, column, scale, shift, perm[...], img[...])
    own_sum[...] = to_images(weights, tile)
    to_txt = to_texts(weights, img[...]) + to_texts(kept[...], img_other[...])
    half = rows + even_txt.shape[0]
    own_txt[...] = to_txt[:rows]
    even_txt[...] = to_txt[rows:half]
    near_txt[...] = to_txt[half : half + rows].astype(BF16)
    odd_txt[...] = to_txt[half + rows :].astype(BF16)


def add_body(even, got, *outs):
    rows = outs[0].shape[0]
    for k, out in enumerate(outs):
        mine = even[k * rows : (k + 1) * rows, :]
        out[...] = (mine + got[k * rows : (k + 1) * rows, :].astype(F32)).astype(BF16)


def split_body(count, position, own, other, keep, *send):
    rows = keep.shape[0]
    for k in range(count):
        start = pl.multiple_of((position[0] ^ k) * rows, rows)
        part = own[pl.ds(start, rows), :] + other[pl.ds(start, rows), :].astype(F32)
        if k == 0:
            keep[...] = part
        else:
            send[k - 1][...] = part.astype(BF16)


def total_of(own, parts):
    total = own[...]
    for part in parts:
        total = total + part[...].astype(F32)
    return total


def backward_unit(unit, inverse, upstream):
    along = jnp.sum(unit * upstream, axis=1, keepdims=True)
    return inverse[:, :1] * (upstream - unit * along)


def finish_img_body(scale, unit, inverse, own, *refs):
    *parts, out = refs
    out[...] = backward_unit(
        unit[...], inverse[...], scale[0] * total_of(own, parts)
    ).astype(BF16)


def last_body(count, place, scale, unit, inverse, own, *refs):
    parts = refs[:count]
    *back, img_out, txt_out, img_held, txt_held, sems = refs[count:]
    rows = parts[0].shape[0]
    copies = []
    for k in range(count):
        img_held[k * rows : (k + 1) * rows, :] = parts[k][...].astype(F32)
        start = pl.multiple_of((place[0] ^ k) * rows, rows)
        copies.append(
            pltpu.make_async_copy(
                img_held.at[pl.ds(k * rows, rows), :],
                img_out.at[pl.ds(start, rows), :],
                sems.at[k],
            )
        )
        copies[-1].start()
    txt_held[...] = backward_unit(unit[...], inverse[...], scale[0] * total_of(own, back))
    copies.append(pltpu.make_async_copy(txt_held, txt_out, sems.at[count]))
    copies[-1].start()
    for copy in copies:
        copy.wait()


def swapped(value, axis, step):
    count = lax.axis_size(axis)
    return lax.ppermute(value, axis, [(s, s ^ step) for s in range(count)])


def local(images, texts, perm, scale, shift):
    rows, width = images.shape
    txt_rows = texts.shape[0]
    line = lax.axis_size("txt")
    blocks = line // 2
    count = lax.axis_size("img")
    part = rows // count
    column = lax.axis_index("txt").reshape(1).astype(jnp.int32)
    place = lax.axis_index("img").reshape(1).astype(jnp.int32)
    perm_row = perm.reshape(1, rows)

    perm_other = swapped(perm_row, "txt", 1)
    raw_other = swapped(images, "txt", 1)
    first = txt_rows // 2
    txt_bf, head, tail, txt_unit, txt_inv = call(
        unit_txt_body,
        [struct(size, width, BF16) for size in (txt_rows, first, txt_rows - first)]
        + [struct(txt_rows, width, F32), struct(txt_rows, 128, F32)],
        [in_hbm(texts)],
        [ANY],
        16 << 20,
        4 * txt_rows * width,
        [pltpu.VMEM((txt_rows, width), F32), pltpu.SemaphoreType.DMA],
    )
    half = blocks // 2
    order = list(range(0, blocks, 2)) + list(range(1, blocks, 2))
    far = [swapped(piece, "txt", 4 * k) for k in range(1, half) for piece in (head, tail)]
    near = [swapped(txt_bf, "txt", 2)]
    for k in range(1, half):
        near += [swapped(far[2 * k - 2], "txt", 2), swapped(tail, "txt", 4 * k + 2)]
    tiles = [txt_bf] + far + near
    img_bf, img_other, img_unit, img_inv = call(
        unit_img_body,
        [struct(rows, width, BF16)] * 2 + [struct(part, width, F32), struct(part, 128, F32)],
        [place, raw_other, in_hbm(images)],
        [SMEM, VMEM, ANY],
        24 << 20,
        8 * rows * width,
        [pltpu.VMEM((rows, width), F32), pltpu.SemaphoreType.DMA],
    )
    scalars = [place, column, scale, shift]
    pairs = 2 * rows * blocks * txt_rows * width
    kept, other_img = call(
        functools.partial(other_body, order, line),
        [struct(blocks * txt_rows, rows, BF16), struct(rows, width, BF16)],
        [*scalars, perm_other, img_other, *tiles],
        [SMEM] * 4 + [VMEM] * (2 + len(tiles)),
        40 << 20,
        2 * pairs,
    )
    from_other = swapped(other_img, "txt", 1)
    own_img, own_txt, even_txt, near_txt, odd_txt = call(
        functools.partial(own_body, order, line),
        [
            struct(rows, width, F32),
            struct(txt_rows, width, F32),
            struct((half - 1) * txt_rows, width, F32),
            struct(txt_rows, width, BF16),
            struct((half - 1) * txt_rows, width, BF16),
        ],
        [*scalars, perm_row, img_bf, img_other, kept, *tiles],
        [SMEM] * 4 + [VMEM] * (4 + len(tiles)),
        40 << 20,
        4 * pairs,
    )
    sums = call(
        add_body,
        [struct(txt_rows, width, BF16)] * (half - 1),
        [even_txt, swapped(odd_txt, "txt", 2)],
        [VMEM] * 2,
        24 << 20,
        rows * width,
    )
    back = [swapped(near_txt, "txt", 2)] + [swapped(sums[k - 1], "txt", 4 * k) for k in range(1, half)]

    keep, *send = call(
        functools.partial(split_body, count),
        [struct(part, width, F32)] + [struct(part, width, BF16)] * (count - 1),
        [place, own_img, from_other],
        [SMEM, VMEM, VMEM],
        24 << 20,
        rows * width,
    )
    got = [swapped(send[k - 1], "img", k) for k in range(1, count)]
    (grad_part,) = call(
        finish_img_body,
        [struct(part, width, BF16)],
        [scale, img_unit, img_inv, keep, *got],
        [SMEM] + [VMEM] * (2 + count),
        24 << 20,
        10 * part * width,
    )
    grads = [grad_part] + [swapped(grad_part, "img", k) for k in range(1, count)]
    return pl.pallas_call(
        functools.partial(last_body, count),
        out_shape=[struct(rows, width, F32), struct(txt_rows, width, F32)],
        in_specs=[SMEM] * 2 + [VMEM] * (3 + count + half),
        out_specs=[ANY] * 2,
        scratch_shapes=[
            pltpu.VMEM((rows, width), F32),
            pltpu.VMEM((txt_rows, width), F32),
            pltpu.SemaphoreType.DMA((count + 1,)),
        ],
        compiler_params=pltpu.CompilerParams(vmem_limit_bytes=24 << 20),
        cost_estimate=pl.CostEstimate(
            flops=10 * txt_rows * width, bytes_accessed=8 * rows * width, transcendentals=0
        ),
    )(place, scale, txt_unit, txt_inv, own_txt, *grads, *back)


def solution(mesh):
    placed = (P("txt", None), P(("img", "txt"), None), P("txt"), P(), P())
    return jax.shard_map(
        local,
        mesh=mesh,
        in_specs=placed,
        out_specs=(P("txt", None), P(("img", "txt"), None)),
        check_vma=False,
    )
```

```python
import functools

import jax
import jax.numpy as jnp
from jax import lax
from jax.experimental import pallas as pl
from jax.experimental.pallas import tpu as pltpu
from jax.sharding import PartitionSpec as P

EPSILON = 1e-06
F32 = jnp.float32
BF16 = jnp.bfloat16
VMEM = pl.BlockSpec(memory_space=pltpu.VMEM)
ANY = pl.BlockSpec(memory_space=pl.ANY)
SMEM = pl.BlockSpec(memory_space=pltpu.SMEM)


def in_hbm(value):
    return pltpu.with_memory_space_constraint(value, pltpu.HBM)


def call(body, outs, args, specs, limit, flops, scratch=()):
    size = sum(a.size * a.dtype.itemsize for a in args)
    size += sum(o.size * o.dtype.itemsize for o in outs)
    return pl.pallas_call(
        body,
        out_shape=outs,
        in_specs=specs,
        out_specs=[VMEM] * len(outs),
        scratch_shapes=scratch,
        compiler_params=pltpu.CompilerParams(vmem_limit_bytes=limit),
        cost_estimate=pl.CostEstimate(flops=flops, bytes_accessed=size, transcendentals=0),
    )(*args)


def struct(rows, cols, dtype):
    return jax.ShapeDtypeStruct((rows, cols), dtype)


def inverse_norm(values):
    return lax.rsqrt(jnp.sum(values * values, axis=1, keepdims=True) + EPSILON)


def unit_txt_body(source, bf, head, tail, unit_out, inv, held, sem):
    copy = pltpu.make_async_copy(source, held, sem)
    copy.start()
    copy.wait()
    values = held[...]
    inverse = inverse_norm(values)
    unit = values * inverse
    rounded = unit.astype(BF16)
    bf[...] = rounded
    head[...] = rounded[: head.shape[0]]
    tail[...] = rounded[head.shape[0] :]
    unit_out[...] = unit
    inv[...] = jnp.broadcast_to(inverse, inv.shape)


def unit_img_body(place, other, source, bf, other_bf, unit_out, inv, held, sem):
    copy = pltpu.make_async_copy(source, held, sem)
    copy.start()
    values = other[...]
    other_bf[...] = (values * inverse_norm(values)).astype(BF16)
    copy.wait()
    values = held[...]
    bf[...] = (values * inverse_norm(values)).astype(BF16)
    rows = unit_out.shape[0]
    values = held[pl.ds(pl.multiple_of(place[0] * rows, rows), rows), :]
    inverse = inverse_norm(values)
    unit_out[...] = values * inverse
    inv[...] = jnp.broadcast_to(inverse, inv.shape)


def weights_of(tile, order, line, place, column, scale, shift, perm, img):
    rows = tile.shape[0] // len(order)
    row = lax.broadcasted_iota(jnp.int32, (rows, 1), 0)
    ids = jnp.concatenate(
        [row + (place[0] * line + (column[0] ^ (2 * k))) * rows for k in order], axis=0
    )
    products = lax.dot_general(tile, img, (((1,), (1,)), ((), ())), preferred_element_type=F32)
    positive = (ids == perm).astype(F32)
    return (jax.nn.sigmoid(scale[0] * products + shift[0]) - positive).astype(BF16)


def to_images(weights, tile):
    return lax.dot_general(weights, tile, (((0,), (0,)), ((), ())), preferred_element_type=F32)


def to_texts(weights, img):
    return jnp.dot(weights, img, preferred_element_type=F32)


def joined(tiles):
    return jnp.concatenate([t[...] for t in tiles], axis=0)


def other_body(order, line, place, column, scale, shift, perm, img, *refs):
    *txt, kept, out = refs
    tile = joined(txt)
    weights = weights_of(tile, order, line, place, column, scale, shift, perm[...], img[...])
    kept[...] = weights
    out[...] = to_images(weights, tile).astype(BF16)


def own_body(order, line, place, column, scale, shift, perm, img, img_other, kept, *refs):
    *txt, own_sum, txt_sums = refs
    tile = joined(txt)
    weights = weights_of(tile, order, line, place, column, scale, shift, perm[...], img[...])
    own_sum[...] = to_images(weights, tile)
    txt_sums[...] = to_texts(weights, img[...]) + to_texts(kept[...], img_other[...])


def split_body(count, blocks, place, own, other, txt_sums, *refs):
    txt_out, (keep, *send) = refs[:blocks], refs[blocks:]
    rows = txt_out[0].shape[0]
    for k, out in enumerate(txt_out):
        out[...] = txt_sums[k * rows : (k + 1) * rows, :].astype(out.dtype)
    rows = keep.shape[0]
    for k in range(count):
        start = pl.multiple_of((place[0] ^ k) * rows, rows)
        part = own[pl.ds(start, rows), :] + other[pl.ds(start, rows), :].astype(F32)
        if k == 0:
            keep[...] = part
        else:
            send[k - 1][...] = part.astype(BF16)


def total_of(own, parts):
    total = own[...]
    for part in parts:
        total = total + part[...].astype(F32)
    return total


def backward_unit(unit, inverse, upstream):
    along = jnp.sum(unit * upstream, axis=1, keepdims=True)
    return inverse[:, :1] * (upstream - unit * along)


def finish_img_body(scale, unit, inverse, own, *refs):
    *parts, out = refs
    out[...] = backward_unit(
        unit[...], inverse[...], scale[0] * total_of(own, parts)
    ).astype(BF16)


def last_body(count, place, scale, unit, inverse, own, *refs):
    parts = refs[:count]
    *back, img_out, txt_out, img_held, txt_held, sems = refs[count:]
    rows = parts[0].shape[0]
    copies = []
    for k in range(count):
        img_held[k * rows : (k + 1) * rows, :] = parts[k][...].astype(F32)
        start = pl.multiple_of((place[0] ^ k) * rows, rows)
        copies.append(
            pltpu.make_async_copy(
                img_held.at[pl.ds(k * rows, rows), :],
                img_out.at[pl.ds(start, rows), :],
                sems.at[k],
            )
        )
        copies[-1].start()
    txt_held[...] = backward_unit(unit[...], inverse[...], scale[0] * total_of(own, back))
    copies.append(pltpu.make_async_copy(txt_held, txt_out, sems.at[count]))
    copies[-1].start()
    for copy in copies:
        copy.wait()


def swapped(value, axis, step):
    count = lax.axis_size(axis)
    return lax.ppermute(value, axis, [(s, s ^ step) for s in range(count)])


def local(images, texts, perm, scale, shift):
    rows, width = images.shape
    txt_rows = texts.shape[0]
    line = lax.axis_size("txt")
    blocks = line // 2
    count = lax.axis_size("img")
    part = rows // count
    column = lax.axis_index("txt").reshape(1).astype(jnp.int32)
    place = lax.axis_index("img").reshape(1).astype(jnp.int32)
    perm_row = perm.reshape(1, rows)

    perm_other = swapped(perm_row, "txt", 1)
    raw_other = swapped(images, "txt", 1)
    first = txt_rows // 2
    txt_bf, head, tail, txt_unit, txt_inv = call(
        unit_txt_body,
        [struct(size, width, BF16) for size in (txt_rows, first, txt_rows - first)]
        + [struct(txt_rows, width, F32), struct(txt_rows, 128, F32)],
        [in_hbm(texts)],
        [ANY],
        16 << 20,
        4 * txt_rows * width,
        [pltpu.VMEM((txt_rows, width), F32), pltpu.SemaphoreType.DMA],
    )
    half = blocks // 2
    order = list(range(0, blocks, 2)) + list(range(1, blocks, 2))
    far = [swapped(piece, "txt", 4 * k) for k in range(1, half) for piece in (head, tail)]
    near = [swapped(txt_bf, "txt", 2)]
    for k in range(1, half):
        near += [swapped(far[2 * k - 2], "txt", 2), swapped(tail, "txt", 4 * k + 2)]
    tiles = [txt_bf] + far + near
    img_bf, img_other, img_unit, img_inv = call(
        unit_img_body,
        [struct(rows, width, BF16)] * 2 + [struct(part, width, F32), struct(part, 128, F32)],
        [place, raw_other, in_hbm(images)],
        [SMEM, VMEM, ANY],
        24 << 20,
        8 * rows * width,
        [pltpu.VMEM((rows, width), F32), pltpu.SemaphoreType.DMA],
    )
    scalars = [place, column, scale, shift]
    pairs = 2 * rows * blocks * txt_rows * width
    kept, other_img = call(
        functools.partial(other_body, order, line),
        [struct(blocks * txt_rows, rows, BF16), struct(rows, width, BF16)],
        [*scalars, perm_other, img_other, *tiles],
        [SMEM] * 4 + [VMEM] * (2 + len(tiles)),
        40 << 20,
        2 * pairs,
    )
    from_other = swapped(other_img, "txt", 1)
    own_img, txt_sums = call(
        functools.partial(own_body, order, line),
        [struct(rows, width, F32), struct(blocks * txt_rows, width, F32)],
        [*scalars, perm_row, img_bf, img_other, kept, *tiles],
        [SMEM] * 4 + [VMEM] * (4 + len(tiles)),
        40 << 20,
        4 * pairs,
    )
    outs = call(
        functools.partial(split_body, count, blocks),
        [struct(txt_rows, width, F32)]
        + [struct(txt_rows, width, BF16)] * (blocks - 1)
        + [struct(part, width, F32)]
        + [struct(part, width, BF16)] * (count - 1),
        [place, own_img, from_other, txt_sums],
        [SMEM] + [VMEM] * 3,
        24 << 20,
        rows * width,
    )
    (own_txt, *send_txt), (keep, *send) = outs[:blocks], outs[blocks:]
    got = [swapped(send[k - 1], "img", k) for k in range(1, count)]
    homes = sorted(zip(order[1:], send_txt), key=lambda pair: pair[0])
    back = [swapped(block, "txt", 2 * k) for k, block in homes]
    (grad_part,) = call(
        finish_img_body,
        [struct(part, width, BF16)],
        [scale, img_unit, img_inv, keep, *got],
        [SMEM] + [VMEM] * (2 + count),
        24 << 20,
        10 * part * width,
    )
    grads = [grad_part] + [swapped(grad_part, "img", k) for k in range(1, count)]
    return pl.pallas_call(
        functools.partial(last_body, count),
        out_shape=[struct(rows, width, F32), struct(txt_rows, width, F32)],
        in_specs=[SMEM] * 2 + [VMEM] * (2 + count + blocks),
        out_specs=[ANY] * 2,
        scratch_shapes=[
            pltpu.VMEM((rows, width), F32),
            pltpu.VMEM((txt_rows, width), F32),
            pltpu.SemaphoreType.DMA((count + 1,)),
        ],
        compiler_params=pltpu.CompilerParams(vmem_limit_bytes=24 << 20),
        cost_estimate=pl.CostEstimate(
            flops=10 * txt_rows * width, bytes_accessed=8 * rows * width, transcendentals=0
        ),
    )(place, scale, txt_unit, txt_inv, own_txt, *grads, *back)


def solution(mesh):
    placed = (P("txt", None), P(("img", "txt"), None), P("txt"), P(), P())
    return jax.shard_map(
        local,
        mesh=mesh,
        in_specs=placed,
        out_specs=(P("txt", None), P(("img", "txt"), None)),
        check_vma=False,
    )
```

```python
import functools

import jax
import jax.numpy as jnp
from jax import lax
from jax.experimental import pallas as pl
from jax.experimental.pallas import tpu as pltpu
from jax.sharding import PartitionSpec as P

EPSILON = 1e-06
F32 = jnp.float32
BF16 = jnp.bfloat16
VMEM = pl.BlockSpec(memory_space=pltpu.VMEM)
ANY = pl.BlockSpec(memory_space=pl.ANY)
SMEM = pl.BlockSpec(memory_space=pltpu.SMEM)


def in_hbm(value):
    return pltpu.with_memory_space_constraint(value, pltpu.HBM)


def call(body, outs, args, specs, limit, flops, scratch=()):
    size = sum(a.size * a.dtype.itemsize for a in args)
    size += sum(o.size * o.dtype.itemsize for o in outs)
    return pl.pallas_call(
        body,
        out_shape=outs,
        in_specs=specs,
        out_specs=[VMEM] * len(outs),
        scratch_shapes=scratch,
        compiler_params=pltpu.CompilerParams(vmem_limit_bytes=limit),
        cost_estimate=pl.CostEstimate(flops=flops, bytes_accessed=size, transcendentals=0),
    )(*args)


def struct(rows, cols, dtype):
    return jax.ShapeDtypeStruct((rows, cols), dtype)


def inverse_norm(values):
    return lax.rsqrt(jnp.sum(values * values, axis=1, keepdims=True) + EPSILON)


def unit_txt_body(source, bf, head, tail, unit_out, inv, held, sem):
    copy = pltpu.make_async_copy(source, held, sem)
    copy.start()
    copy.wait()
    values = held[...]
    inverse = inverse_norm(values)
    unit = values * inverse
    rounded = unit.astype(BF16)
    bf[...] = rounded
    head[...] = rounded[: head.shape[0]]
    tail[...] = rounded[head.shape[0] :]
    unit_out[...] = unit
    inv[...] = jnp.broadcast_to(inverse, inv.shape)


def unit_img_body(place, other, source, bf, other_bf, unit_out, inv, held, sem):
    copy = pltpu.make_async_copy(source, held, sem)
    copy.start()
    values = other[...]
    other_bf[...] = (values * inverse_norm(values)).astype(BF16)
    copy.wait()
    values = held[...]
    bf[...] = (values * inverse_norm(values)).astype(BF16)
    rows = unit_out.shape[0]
    values = held[pl.ds(pl.multiple_of(place[0] * rows, rows), rows), :]
    inverse = inverse_norm(values)
    unit_out[...] = values * inverse
    inv[...] = jnp.broadcast_to(inverse, inv.shape)


def weights_of(tile, order, line, place, column, scale, shift, perm, img):
    rows = tile.shape[0] // len(order)
    row = lax.broadcasted_iota(jnp.int32, (rows, 1), 0)
    ids = jnp.concatenate(
        [row + (place[0] * line + (column[0] ^ (2 * k))) * rows for k in order], axis=0
    )
    products = lax.dot_general(tile, img, (((1,), (1,)), ((), ())), preferred_element_type=F32)
    positive = (ids == perm).astype(F32)
    return (jax.nn.sigmoid(scale[0] * products + shift[0]) - positive).astype(BF16)


def to_images(weights, tile):
    return lax.dot_general(weights, tile, (((0,), (0,)), ((), ())), preferred_element_type=F32)


def to_texts(weights, img):
    return jnp.dot(weights, img, preferred_element_type=F32)


def joined(tiles):
    return jnp.concatenate([t[...] for t in tiles], axis=0)


def other_body(order, line, place, column, scale, shift, perm, img, *refs):
    *txt, kept, out = refs
    tile = joined(txt)
    weights = weights_of(tile, order, line, place, column, scale, shift, perm[...], img[...])
    kept[...] = weights
    out[...] = to_images(weights, tile).astype(BF16)


def own_body(order, line, place, column, scale, shift, perm, img, img_other, kept, *refs):
    *txt, own_sum, txt_sums = refs
    tile = joined(txt)
    weights = weights_of(tile, order, line, place, column, scale, shift, perm[...], img[...])
    own_sum[...] = to_images(weights, tile)
    txt_sums[...] = to_texts(weights, img[...]) + to_texts(kept[...], img_other[...])


def split_body(count, blocks, place, own, other, txt_sums, *refs):
    txt_out, (keep, *send) = refs[:blocks], refs[blocks:]
    rows = txt_out[0].shape[0]
    for k, out in enumerate(txt_out):
        out[...] = txt_sums[k * rows : (k + 1) * rows, :].astype(out.dtype)
    rows = keep.shape[0]
    for k in range(count):
        start = pl.multiple_of((place[0] ^ k) * rows, rows)
        part = own[pl.ds(start, rows), :] + other[pl.ds(start, rows), :].astype(F32)
        if k == 0:
            keep[...] = part
        else:
            send[k - 1][...] = part.astype(BF16)


def total_of(own, parts):
    total = own[...]
    for part in parts:
        total = total + part[...].astype(F32)
    return total


def backward_unit(unit, inverse, upstream):
    along = jnp.sum(unit * upstream, axis=1, keepdims=True)
    return inverse[:, :1] * (upstream - unit * along)


def finish_img_body(scale, unit, inverse, own, *refs):
    *parts, out = refs
    out[...] = backward_unit(
        unit[...], inverse[...], scale[0] * total_of(own, parts)
    ).astype(BF16)


def last_body(partners, place, scale, unit, inverse, own, *refs):
    count = len(partners)
    parts = refs[:count]
    *back, img_out, txt_out, img_held, txt_held, sems = refs[count:]
    rows = parts[0].shape[0]
    copies = []
    for k, partner in enumerate(partners):
        img_held[k * rows : (k + 1) * rows, :] = parts[k][...].astype(F32)
        start = pl.multiple_of((place[0] ^ partner) * rows, rows)
        copies.append(
            pltpu.make_async_copy(
                img_held.at[pl.ds(k * rows, rows), :],
                img_out.at[pl.ds(start, rows), :],
                sems.at[k],
            )
        )
        copies[-1].start()
    txt_held[...] = backward_unit(unit[...], inverse[...], scale[0] * total_of(own, back))
    copies.append(pltpu.make_async_copy(txt_held, txt_out, sems.at[count]))
    copies[-1].start()
    for copy in copies:
        copy.wait()


def swapped(value, axis, step):
    count = lax.axis_size(axis)
    return lax.ppermute(value, axis, [(s, s ^ step) for s in range(count)])


def local(images, texts, perm, scale, shift):
    rows, width = images.shape
    txt_rows = texts.shape[0]
    line = lax.axis_size("txt")
    blocks = line // 2
    count = lax.axis_size("img")
    part = rows // count
    column = lax.axis_index("txt").reshape(1).astype(jnp.int32)
    place = lax.axis_index("img").reshape(1).astype(jnp.int32)
    perm_row = perm.reshape(1, rows)

    perm_other = swapped(perm_row, "txt", 1)
    raw_other = swapped(images, "txt", 1)
    first = txt_rows // 2
    txt_bf, head, tail, txt_unit, txt_inv = call(
        unit_txt_body,
        [struct(size, width, BF16) for size in (txt_rows, first, txt_rows - first)]
        + [struct(txt_rows, width, F32), struct(txt_rows, 128, F32)],
        [in_hbm(texts)],
        [ANY],
        16 << 20,
        4 * txt_rows * width,
        [pltpu.VMEM((txt_rows, width), F32), pltpu.SemaphoreType.DMA],
    )
    half = blocks // 2
    order = list(range(0, blocks, 2)) + list(range(1, blocks, 2))
    far = [swapped(piece, "txt", 4 * k) for k in range(1, half) for piece in (head, tail)]
    near = [swapped(txt_bf, "txt", 2)]
    for k in range(1, half):
        near += [swapped(far[2 * k - 2], "txt", 2), swapped(tail, "txt", 4 * k + 2)]
    tiles = [txt_bf] + far + near
    img_bf, img_other, img_unit, img_inv = call(
        unit_img_body,
        [struct(rows, width, BF16)] * 2 + [struct(part, width, F32), struct(part, 128, F32)],
        [place, raw_other, in_hbm(images)],
        [SMEM, VMEM, ANY],
        24 << 20,
        8 * rows * width,
        [pltpu.VMEM((rows, width), F32), pltpu.SemaphoreType.DMA],
    )
    scalars = [place, column, scale, shift]
    pairs = 2 * rows * blocks * txt_rows * width
    kept, other_img = call(
        functools.partial(other_body, order, line),
        [struct(blocks * txt_rows, rows, BF16), struct(rows, width, BF16)],
        [*scalars, perm_other, img_other, *tiles],
        [SMEM] * 4 + [VMEM] * (2 + len(tiles)),
        40 << 20,
        2 * pairs,
    )
    from_other = swapped(other_img, "txt", 1)
    own_img, txt_sums = call(
        functools.partial(own_body, order, line),
        [struct(rows, width, F32), struct(blocks * txt_rows, width, F32)],
        [*scalars, perm_row, img_bf, img_other, kept, *tiles],
        [SMEM] * 4 + [VMEM] * (4 + len(tiles)),
        40 << 20,
        4 * pairs,
    )
    outs = call(
        functools.partial(split_body, count, blocks),
        [struct(txt_rows, width, F32)]
        + [struct(txt_rows, width, BF16)] * (blocks - 1)
        + [struct(part, width, F32)]
        + [struct(part, width, BF16)] * (count - 1),
        [place, own_img, from_other, txt_sums],
        [SMEM] + [VMEM] * 3,
        24 << 20,
        rows * width,
    )
    (own_txt, *send_txt), (keep, *send) = outs[:blocks], outs[blocks:]
    got = [swapped(send[k - 1], "img", k) for k in range(1, count)]
    homes = sorted(zip(order[1:], send_txt), key=lambda pair: pair[0])
    back = [swapped(block, "txt", 2 * k) for k, block in homes]
    (grad_part,) = call(
        finish_img_body,
        [struct(part, width, BF16)],
        [scale, img_unit, img_inv, keep, *got],
        [SMEM] + [VMEM] * (2 + count),
        24 << 20,
        10 * part * width,
    )
    partners = list(range(count - 1, 0, -1))
    grads = [grad_part] + [swapped(grad_part, "img", k) for k in partners]
    return pl.pallas_call(
        functools.partial(last_body, [0, *partners]),
        out_shape=[struct(rows, width, F32), struct(txt_rows, width, F32)],
        in_specs=[SMEM] * 2 + [VMEM] * (2 + count + blocks),
        out_specs=[ANY] * 2,
        scratch_shapes=[
            pltpu.VMEM((rows, width), F32),
            pltpu.VMEM((txt_rows, width), F32),
            pltpu.SemaphoreType.DMA((count + 1,)),
        ],
        compiler_params=pltpu.CompilerParams(vmem_limit_bytes=24 << 20),
        cost_estimate=pl.CostEstimate(
            flops=10 * txt_rows * width, bytes_accessed=8 * rows * width, transcendentals=0
        ),
    )(place, scale, txt_unit, txt_inv, own_txt, *grads, *back)


def solution(mesh):
    placed = (P("txt", None), P(("img", "txt"), None), P("txt"), P(), P())
    return jax.shard_map(
        local,
        mesh=mesh,
        in_specs=placed,
        out_specs=(P("txt", None), P(("img", "txt"), None)),
        check_vma=False,
    )
```

```python
import functools

import jax
import jax.numpy as jnp
from jax import lax
from jax.experimental import pallas as pl
from jax.experimental.pallas import tpu as pltpu
from jax.sharding import PartitionSpec as P

EPSILON = 1e-06
F32 = jnp.float32
BF16 = jnp.bfloat16
VMEM = pl.BlockSpec(memory_space=pltpu.VMEM)
ANY = pl.BlockSpec(memory_space=pl.ANY)
SMEM = pl.BlockSpec(memory_space=pltpu.SMEM)


def in_hbm(value):
    return pltpu.with_memory_space_constraint(value, pltpu.HBM)


def call(body, outs, args, specs, limit, flops, scratch=()):
    size = sum(a.size * a.dtype.itemsize for a in args)
    size += sum(o.size * o.dtype.itemsize for o in outs)
    return pl.pallas_call(
        body,
        out_shape=outs,
        in_specs=specs,
        out_specs=[VMEM] * len(outs),
        scratch_shapes=scratch,
        compiler_params=pltpu.CompilerParams(vmem_limit_bytes=limit),
        cost_estimate=pl.CostEstimate(flops=flops, bytes_accessed=size, transcendentals=0),
    )(*args)


def struct(rows, cols, dtype):
    return jax.ShapeDtypeStruct((rows, cols), dtype)


def inverse_norm(values):
    return lax.rsqrt(jnp.sum(values * values, axis=1, keepdims=True) + EPSILON)


def unit_txt_body(source, bf, head, tail, unit_out, inv, held, sem):
    copy = pltpu.make_async_copy(source, held, sem)
    copy.start()
    copy.wait()
    values = held[...]
    inverse = inverse_norm(values)
    unit = values * inverse
    rounded = unit.astype(BF16)
    bf[...] = rounded
    head[...] = rounded[: head.shape[0]]
    tail[...] = rounded[head.shape[0] :]
    unit_out[...] = unit
    inv[...] = jnp.broadcast_to(inverse, inv.shape)


def unit_img_body(place, other, source, bf, other_bf, other_turned, unit_out, inv, held, sem):
    copy = pltpu.make_async_copy(source, held, sem)
    copy.start()
    values = other[...]
    rounded = (values * inverse_norm(values)).astype(BF16)
    other_bf[...] = rounded
    other_turned[...] = rounded.T
    copy.wait()
    values = held[...]
    bf[...] = (values * inverse_norm(values)).astype(BF16)
    rows = unit_out.shape[0]
    values = held[pl.ds(pl.multiple_of(place[0] * rows, rows), rows), :]
    inverse = inverse_norm(values)
    unit_out[...] = values * inverse
    inv[...] = jnp.broadcast_to(inverse, inv.shape)


def weights_of(tile, order, line, place, column, scale, shift, perm, img, img_dim=1):
    rows = tile.shape[0] // len(order)
    row = lax.broadcasted_iota(jnp.int32, (rows, 1), 0)
    ids = jnp.concatenate(
        [row + (place[0] * line + (column[0] ^ (2 * k))) * rows for k in order], axis=0
    )
    products = lax.dot_general(
        tile, img, (((1,), (img_dim,)), ((), ())), preferred_element_type=F32
    )
    positive = (ids == perm).astype(F32)
    return (jax.nn.sigmoid(scale[0] * products + shift[0]) - positive).astype(BF16)


def to_images(weights, tile):
    return lax.dot_general(weights, tile, (((0,), (0,)), ((), ())), preferred_element_type=F32)


def to_texts(weights, img):
    return jnp.dot(weights, img, preferred_element_type=F32)


def joined(tiles):
    return jnp.concatenate([t[...] for t in tiles], axis=0)


def other_body(order, line, place, column, scale, shift, perm, turned, *refs):
    *txt, kept, out = refs
    tile = joined(txt)
    weights = weights_of(tile, order, line, place, column, scale, shift, perm[...], turned[...], 0)
    kept[...] = weights
    out[...] = to_images(weights, tile).astype(BF16)


def own_body(order, line, place, column, scale, shift, perm, img, img_other, kept, *refs):
    *txt, own_sum, txt_sums = refs
    tile = joined(txt)
    weights = weights_of(tile, order, line, place, column, scale, shift, perm[...], img[...])
    own_sum[...] = to_images(weights, tile)
    txt_sums[...] = to_texts(weights, img[...]) + to_texts(kept[...], img_other[...])


def split_body(count, blocks, place, own, other, txt_sums, *refs):
    txt_out, (keep, *send) = refs[:blocks], refs[blocks:]
    rows = txt_out[0].shape[0]
    for k, out in enumerate(txt_out):
        out[...] = txt_sums[k * rows : (k + 1) * rows, :].astype(out.dtype)
    rows = keep.shape[0]
    for k in range(count):
        start = pl.multiple_of((place[0] ^ k) * rows, rows)
        part = own[pl.ds(start, rows), :] + other[pl.ds(start, rows), :].astype(F32)
        if k == 0:
            keep[...] = part
        else:
            send[k - 1][...] = part.astype(BF16)


def total_of(own, parts):
    total = own[...]
    for part in parts:
        total = total + part[...].astype(F32)
    return total


def backward_unit(unit, inverse, upstream):
    along = jnp.sum(unit * upstream, axis=1, keepdims=True)
    return inverse[:, :1] * (upstream - unit * along)


def finish_img_body(scale, unit, inverse, own, *refs):
    *parts, out = refs
    out[...] = backward_unit(
        unit[...], inverse[...], scale[0] * total_of(own, parts)
    ).astype(BF16)


def quarter_copies(partners, place, parts, img_out, img_held, sems):
    rows = parts[0].shape[0]
    copies = []
    for k, (partner, part) in enumerate(zip(partners, parts)):
        img_held[k * rows : (k + 1) * rows, :] = part[...].astype(F32)
        start = pl.multiple_of((place[0] ^ partner) * rows, rows)
        copies.append(
            pltpu.make_async_copy(
                img_held.at[pl.ds(k * rows, rows), :],
                img_out.at[pl.ds(start, rows), :],
                sems.at[k],
            )
        )
        copies[-1].start()
    return copies


def first_body(partners, place, scale, unit, inverse, own, *refs):
    count = len(partners)
    parts = refs[:count]
    *back, img_out, txt_out, img_held, txt_held, sems = refs[count:]
    copies = quarter_copies(partners, place, parts, img_out, img_held, sems)
    txt_held[...] = backward_unit(unit[...], inverse[...], scale[0] * total_of(own, back))
    copies.append(pltpu.make_async_copy(txt_held, txt_out, sems.at[count]))
    copies[-1].start()
    for copy in copies:
        copy.wait()


def last_body(partners, place, begun, *refs):
    del begun
    *parts, img_out, img_held, sems = refs
    for copy in quarter_copies(partners, place, parts, img_out, img_held, sems):
        copy.wait()


def swapped(value, axis, step):
    count = lax.axis_size(axis)
    return lax.ppermute(value, axis, [(s, s ^ step) for s in range(count)])


def local(images, texts, perm, scale, shift):
    rows, width = images.shape
    txt_rows = texts.shape[0]
    line = lax.axis_size("txt")
    blocks = line // 2
    count = lax.axis_size("img")
    part = rows // count
    column = lax.axis_index("txt").reshape(1).astype(jnp.int32)
    place = lax.axis_index("img").reshape(1).astype(jnp.int32)
    perm_row = perm.reshape(1, rows)

    perm_other = swapped(perm_row, "txt", 1)
    raw_other = swapped(images, "txt", 1)
    first = txt_rows // 2
    txt_bf, head, tail, txt_unit, txt_inv = call(
        unit_txt_body,
        [struct(size, width, BF16) for size in (txt_rows, first, txt_rows - first)]
        + [struct(txt_rows, width, F32), struct(txt_rows, 128, F32)],
        [in_hbm(texts)],
        [ANY],
        16 << 20,
        4 * txt_rows * width,
        [pltpu.VMEM((txt_rows, width), F32), pltpu.SemaphoreType.DMA],
    )
    half = blocks // 2
    order = list(range(0, blocks, 2)) + list(range(1, blocks, 2))
    far = [swapped(piece, "txt", 4 * k) for k in range(1, half) for piece in (head, tail)]
    near = [swapped(txt_bf, "txt", 2)]
    for k in range(1, half):
        near += [swapped(far[2 * k - 2], "txt", 2), swapped(tail, "txt", 4 * k + 2)]
    tiles = [txt_bf] + far + near
    img_bf, img_other, turned_other, img_unit, img_inv = call(
        unit_img_body,
        [struct(rows, width, BF16)] * 2
        + [struct(width, rows, BF16), struct(part, width, F32), struct(part, 128, F32)],
        [place, raw_other, in_hbm(images)],
        [SMEM, VMEM, ANY],
        24 << 20,
        8 * rows * width,
        [pltpu.VMEM((rows, width), F32), pltpu.SemaphoreType.DMA],
    )
    scalars = [place, column, scale, shift]
    pairs = 2 * rows * blocks * txt_rows * width
    kept, other_img = call(
        functools.partial(other_body, order, line),
        [struct(blocks * txt_rows, rows, BF16), struct(rows, width, BF16)],
        [*scalars, perm_other, turned_other, *tiles],
        [SMEM] * 4 + [VMEM] * (2 + len(tiles)),
        40 << 20,
        2 * pairs,
    )
    from_other = swapped(other_img, "txt", 1)
    own_img, txt_sums = call(
        functools.partial(own_body, order, line),
        [struct(rows, width, F32), struct(blocks * txt_rows, width, F32)],
        [*scalars, perm_row, img_bf, img_other, kept, *tiles],
        [SMEM] * 4 + [VMEM] * (4 + len(tiles)),
        40 << 20,
        4 * pairs,
    )
    outs = call(
        functools.partial(split_body, count, blocks),
        [struct(txt_rows, width, F32)]
        + [struct(txt_rows, width, BF16)] * (blocks - 1)
        + [struct(part, width, F32)]
        + [struct(part, width, BF16)] * (count - 1),
        [place, own_img, from_other, txt_sums],
        [SMEM] + [VMEM] * 3,
        24 << 20,
        rows * width,
    )
    (own_txt, *send_txt), (keep, *send) = outs[:blocks], outs[blocks:]
    got = [swapped(send[k - 1], "img", k) for k in range(1, count)]
    homes = sorted(zip(order[1:], send_txt), key=lambda pair: pair[0])
    back = [swapped(block, "txt", 2 * k) for k, block in homes]
    (grad_part,) = call(
        finish_img_body,
        [struct(part, width, BF16)],
        [scale, img_unit, img_inv, keep, *got],
        [SMEM] + [VMEM] * (2 + count),
        24 << 20,
        10 * part * width,
    )
    partners = [1, *range(count - 1, 1, -1)]
    grads = [grad_part] + [swapped(grad_part, "img", k) for k in partners]
    partners = [0, *partners]
    early = 2
    begun, grad_texts = pl.pallas_call(
        functools.partial(first_body, partners[:early]),
        out_shape=[struct(rows, width, F32), struct(txt_rows, width, F32)],
        in_specs=[SMEM] * 2 + [VMEM] * (2 + early + blocks),
        out_specs=[ANY] * 2,
        scratch_shapes=[
            pltpu.VMEM((early * part, width), F32),
            pltpu.VMEM((txt_rows, width), F32),
            pltpu.SemaphoreType.DMA((early + 1,)),
        ],
        compiler_params=pltpu.CompilerParams(vmem_limit_bytes=24 << 20),
        cost_estimate=pl.CostEstimate(
            flops=10 * txt_rows * width, bytes_accessed=8 * rows * width, transcendentals=0
        ),
    )(place, scale, txt_unit, txt_inv, own_txt, *grads[:early], *back)
    grad_images = pl.pallas_call(
        functools.partial(last_body, partners[early:]),
        out_shape=struct(rows, width, F32),
        in_specs=[SMEM, ANY] + [VMEM] * (count - early),
        out_specs=ANY,
        scratch_shapes=[
            pltpu.VMEM(((count - early) * part, width), F32),
            pltpu.SemaphoreType.DMA((count - early,)),
        ],
        input_output_aliases={1: 0},
        compiler_params=pltpu.CompilerParams(vmem_limit_bytes=24 << 20),
        cost_estimate=pl.CostEstimate(
            flops=rows * width, bytes_accessed=8 * rows * width, transcendentals=0
        ),
    )(place, begun, *grads[early:])
    return (grad_images, grad_texts)


def solution(mesh):
    placed = (P("txt", None), P(("img", "txt"), None), P("txt"), P(), P())
    return jax.shard_map(
        local,
        mesh=mesh,
        in_specs=placed,
        out_specs=(P("txt", None), P(("img", "txt"), None)),
        check_vma=False,
    )
```

```python
import functools

import jax
import jax.numpy as jnp
from jax import lax
from jax.experimental import pallas as pl
from jax.experimental.pallas import tpu as pltpu
from jax.sharding import PartitionSpec as P

EPSILON = 1e-06
F32 = jnp.float32
BF16 = jnp.bfloat16
VMEM = pl.BlockSpec(memory_space=pltpu.VMEM)
ANY = pl.BlockSpec(memory_space=pl.ANY)
SMEM = pl.BlockSpec(memory_space=pltpu.SMEM)


def in_hbm(value):
    return pltpu.with_memory_space_constraint(value, pltpu.HBM)


def call(body, outs, args, specs, limit, flops, scratch=()):
    size = sum(a.size * a.dtype.itemsize for a in args)
    size += sum(o.size * o.dtype.itemsize for o in outs)
    return pl.pallas_call(
        body,
        out_shape=outs,
        in_specs=specs,
        out_specs=[VMEM] * len(outs),
        scratch_shapes=scratch,
        compiler_params=pltpu.CompilerParams(vmem_limit_bytes=limit),
        cost_estimate=pl.CostEstimate(flops=flops, bytes_accessed=size, transcendentals=0),
    )(*args)


def struct(rows, cols, dtype):
    return jax.ShapeDtypeStruct((rows, cols), dtype)


def inverse_norm(values):
    return lax.rsqrt(jnp.sum(values * values, axis=1, keepdims=True) + EPSILON)


def unit_txt_body(source, bf, head, tail, unit_out, inv, held, sem):
    copy = pltpu.make_async_copy(source, held, sem)
    copy.start()
    copy.wait()
    values = held[...]
    inverse = inverse_norm(values)
    unit = values * inverse
    rounded = unit.astype(BF16)
    bf[...] = rounded
    head[...] = rounded[: head.shape[0]]
    tail[...] = rounded[head.shape[0] :]
    unit_out[...] = unit
    inv[...] = jnp.broadcast_to(inverse, inv.shape)


def unit_img_body(place, other, source, bf, other_bf, other_turned, unit_out, inv, held, sem):
    copy = pltpu.make_async_copy(source, held, sem)
    copy.start()
    values = other[...]
    rounded = (values * inverse_norm(values)).astype(BF16)
    other_bf[...] = rounded
    other_turned[...] = rounded.T
    copy.wait()
    values = held[...]
    bf[...] = (values * inverse_norm(values)).astype(BF16)
    rows = unit_out.shape[0]
    values = held[pl.ds(pl.multiple_of(place[0] * rows, rows), rows), :]
    inverse = inverse_norm(values)
    unit_out[...] = values * inverse
    inv[...] = jnp.broadcast_to(inverse, inv.shape)


def weights_of(tile, order, line, place, column, scale, shift, perm, img, img_dim=1):
    rows = tile.shape[0] // len(order)
    row = lax.broadcasted_iota(jnp.int32, (rows, 1), 0)
    ids = jnp.concatenate(
        [row + (place[0] * line + (column[0] ^ (2 * k))) * rows for k in order], axis=0
    )
    products = lax.dot_general(
        tile, img, (((1,), (img_dim,)), ((), ())), preferred_element_type=F32
    )
    positive = (ids == perm).astype(F32)
    return (jax.nn.sigmoid(scale[0] * products + shift[0]) - positive).astype(BF16)


def to_images(weights, tile):
    return lax.dot_general(weights, tile, (((0,), (0,)), ((), ())), preferred_element_type=F32)


def to_texts(weights, img):
    return jnp.dot(weights, img, preferred_element_type=F32)


def joined(tiles):
    return jnp.concatenate([t[...] for t in tiles], axis=0)


def other_body(slots, order, line, place, column, scale, shift, perm, turned, *refs):
    *txt, kept, out = refs
    tile = joined([txt[k] for k in slots])
    weights = weights_of(tile, order, line, place, column, scale, shift, perm[...], turned[...], 0)
    kept[...] = weights
    out[...] = to_images(weights, tile).astype(BF16)


def own_body(slots, order, line, place, column, scale, shift, perm, img, img_other, kept, *refs):
    *txt, own_sum, txt_sums = refs
    tile = joined([txt[k] for k in slots])
    weights = weights_of(tile, order, line, place, column, scale, shift, perm[...], img[...])
    own_sum[...] = to_images(weights, tile)
    txt_sums[...] = to_texts(weights, img[...]) + to_texts(kept[...], img_other[...])


def split_body(count, blocks, place, own, other, txt_sums, *refs):
    txt_out, (keep, *send) = refs[:blocks], refs[blocks:]
    rows = txt_out[0].shape[0]
    for k, out in enumerate(txt_out):
        out[...] = txt_sums[k * rows : (k + 1) * rows, :].astype(out.dtype)
    rows = keep.shape[0]
    for k in range(count):
        start = pl.multiple_of((place[0] ^ k) * rows, rows)
        part = own[pl.ds(start, rows), :] + other[pl.ds(start, rows), :].astype(F32)
        if k == 0:
            keep[...] = part
        else:
            send[k - 1][...] = part.astype(BF16)


def total_of(own, parts):
    total = own[...]
    for part in parts:
        total = total + part[...].astype(F32)
    return total


def backward_unit(unit, inverse, upstream):
    along = jnp.sum(unit * upstream, axis=1, keepdims=True)
    return inverse[:, :1] * (upstream - unit * along)


def finish_img_body(scale, unit, inverse, own, *refs):
    *parts, out = refs
    out[...] = backward_unit(
        unit[...], inverse[...], scale[0] * total_of(own, parts)
    ).astype(BF16)


def quarter_copies(partners, place, parts, img_out, img_held, sems):
    rows = parts[0].shape[0]
    copies = []
    for k, (partner, part) in enumerate(zip(partners, parts)):
        img_held[k * rows : (k + 1) * rows, :] = part[...].astype(F32)
        start = pl.multiple_of((place[0] ^ partner) * rows, rows)
        copies.append(
            pltpu.make_async_copy(
                img_held.at[pl.ds(k * rows, rows), :],
                img_out.at[pl.ds(start, rows), :],
                sems.at[k],
            )
        )
        copies[-1].start()
    return copies


def first_body(partners, place, scale, unit, inverse, own, *refs):
    count = len(partners)
    parts = refs[:count]
    *back, img_out, txt_out, img_held, txt_held, sems = refs[count:]
    copies = quarter_copies(partners, place, parts, img_out, img_held, sems)
    txt_held[...] = backward_unit(unit[...], inverse[...], scale[0] * total_of(own, back))
    copies.append(pltpu.make_async_copy(txt_held, txt_out, sems.at[count]))
    copies[-1].start()
    for copy in copies:
        copy.wait()


def last_body(partners, place, begun, *refs):
    del begun
    *parts, img_out, img_held, sems = refs
    for copy in quarter_copies(partners, place, parts, img_out, img_held, sems):
        copy.wait()


def swapped(value, axis, step):
    count = lax.axis_size(axis)
    return lax.ppermute(value, axis, [(s, s ^ step) for s in range(count)])


def local(images, texts, perm, scale, shift):
    rows, width = images.shape
    txt_rows = texts.shape[0]
    line = lax.axis_size("txt")
    blocks = line // 2
    count = lax.axis_size("img")
    part = rows // count
    column = lax.axis_index("txt").reshape(1).astype(jnp.int32)
    place = lax.axis_index("img").reshape(1).astype(jnp.int32)
    perm_row = perm.reshape(1, rows)

    perm_other = swapped(perm_row, "txt", 1)
    raw_other = swapped(images, "txt", 1)
    first = txt_rows // 2
    txt_bf, head, tail, txt_unit, txt_inv = call(
        unit_txt_body,
        [struct(size, width, BF16) for size in (txt_rows, first, txt_rows - first)]
        + [struct(txt_rows, width, F32), struct(txt_rows, 128, F32)],
        [in_hbm(texts)],
        [ANY],
        16 << 20,
        4 * txt_rows * width,
        [pltpu.VMEM((txt_rows, width), F32), pltpu.SemaphoreType.DMA],
    )
    half = blocks // 2
    order = list(range(0, blocks, 2)) + list(range(1, blocks, 2))
    far = [swapped(piece, "txt", 4 * k) for k in range(1, half) for piece in (head, tail)]
    near = [swapped(txt_bf, "txt", 2)]
    for k in range(1, half):
        near += [swapped(far[2 * k - 2], "txt", 2), swapped(tail, "txt", 4 * k + 2)]
    ranks = [0, *(1, 5) * (half - 1), 2, *(3, 4) * (half - 1)]
    stand = sorted(range(len(ranks)), key=lambda k: ranks[k])
    tiles = [([txt_bf] + far + near)[k] for k in stand]
    slots = [stand.index(k) for k in range(len(stand))]
    img_bf, img_other, turned_other, img_unit, img_inv = call(
        unit_img_body,
        [struct(rows, width, BF16)] * 2
        + [struct(width, rows, BF16), struct(part, width, F32), struct(part, 128, F32)],
        [place, raw_other, in_hbm(images)],
        [SMEM, VMEM, ANY],
        24 << 20,
        8 * rows * width,
        [pltpu.VMEM((rows, width), F32), pltpu.SemaphoreType.DMA],
    )
    scalars = [place, column, scale, shift]
    pairs = 2 * rows * blocks * txt_rows * width
    kept, other_img = call(
        functools.partial(other_body, slots, order, line),
        [struct(blocks * txt_rows, rows, BF16), struct(rows, width, BF16)],
        [*scalars, perm_other, turned_other, *tiles],
        [SMEM] * 4 + [VMEM] * (2 + len(tiles)),
        40 << 20,
        2 * pairs,
    )
    from_other = swapped(other_img, "txt", 1)
    own_img, txt_sums = call(
        functools.partial(own_body, slots, order, line),
        [struct(rows, width, F32), struct(blocks * txt_rows, width, F32)],
        [*scalars, perm_row, img_bf, img_other, kept, *tiles],
        [SMEM] * 4 + [VMEM] * (4 + len(tiles)),
        40 << 20,
        4 * pairs,
    )
    outs = call(
        functools.partial(split_body, count, blocks),
        [struct(txt_rows, width, F32)]
        + [struct(txt_rows, width, BF16)] * (blocks - 1)
        + [struct(part, width, F32)]
        + [struct(part, width, BF16)] * (count - 1),
        [place, own_img, from_other, txt_sums],
        [SMEM] + [VMEM] * 3,
        24 << 20,
        rows * width,
    )
    (own_txt, *send_txt), (keep, *send) = outs[:blocks], outs[blocks:]
    got = [swapped(send[k - 1], "img", k) for k in range(1, count)]
    homes = sorted(zip(order[1:], send_txt), key=lambda pair: pair[0])
    back = [swapped(block, "txt", 2 * k) for k, block in homes]
    (grad_part,) = call(
        finish_img_body,
        [struct(part, width, BF16)],
        [scale, img_unit, img_inv, keep, *got],
        [SMEM] + [VMEM] * (2 + count),
        24 << 20,
        10 * part * width,
    )
    partners = [1, *range(count - 1, 1, -1)]
    grads = [grad_part] + [swapped(grad_part, "img", k) for k in partners]
    partners = [0, *partners]
    early = 2
    begun, grad_texts = pl.pallas_call(
        functools.partial(first_body, partners[:early]),
        out_shape=[struct(rows, width, F32), struct(txt_rows, width, F32)],
        in_specs=[SMEM] * 2 + [VMEM] * (2 + early + blocks),
        out_specs=[ANY] * 2,
        scratch_shapes=[
            pltpu.VMEM((early * part, width), F32),
            pltpu.VMEM((txt_rows, width), F32),
            pltpu.SemaphoreType.DMA((early + 1,)),
        ],
        compiler_params=pltpu.CompilerParams(vmem_limit_bytes=24 << 20),
        cost_estimate=pl.CostEstimate(
            flops=10 * txt_rows * width, bytes_accessed=8 * rows * width, transcendentals=0
        ),
    )(place, scale, txt_unit, txt_inv, own_txt, *grads[:early], *back)
    grad_images = pl.pallas_call(
        functools.partial(last_body, partners[early:]),
        out_shape=struct(rows, width, F32),
        in_specs=[SMEM, ANY] + [VMEM] * (count - early),
        out_specs=ANY,
        scratch_shapes=[
            pltpu.VMEM(((count - early) * part, width), F32),
            pltpu.SemaphoreType.DMA((count - early,)),
        ],
        input_output_aliases={1: 0},
        compiler_params=pltpu.CompilerParams(vmem_limit_bytes=24 << 20),
        cost_estimate=pl.CostEstimate(
            flops=rows * width, bytes_accessed=8 * rows * width, transcendentals=0
        ),
    )(place, begun, *grads[early:])
    return (grad_images, grad_texts)


def solution(mesh):
    placed = (P("txt", None), P(("img", "txt"), None), P("txt"), P(), P())
    return jax.shard_map(
        local,
        mesh=mesh,
        in_specs=placed,
        out_specs=(P("txt", None), P(("img", "txt"), None)),
        check_vma=False,
    )
```

```python
import functools

import jax
import jax.numpy as jnp
from jax import lax
from jax.experimental import pallas as pl
from jax.experimental.pallas import tpu as pltpu
from jax.sharding import PartitionSpec as P

EPSILON = 1e-06
F32 = jnp.float32
BF16 = jnp.bfloat16
VMEM = pl.BlockSpec(memory_space=pltpu.VMEM)
ANY = pl.BlockSpec(memory_space=pl.ANY)
SMEM = pl.BlockSpec(memory_space=pltpu.SMEM)


def in_hbm(value):
    return pltpu.with_memory_space_constraint(value, pltpu.HBM)


def call(body, outs, args, specs, limit, flops, scratch=()):
    size = sum(a.size * a.dtype.itemsize for a in args)
    size += sum(o.size * o.dtype.itemsize for o in outs)
    return pl.pallas_call(
        body,
        out_shape=outs,
        in_specs=specs,
        out_specs=[VMEM] * len(outs),
        scratch_shapes=scratch,
        compiler_params=pltpu.CompilerParams(vmem_limit_bytes=limit),
        cost_estimate=pl.CostEstimate(flops=flops, bytes_accessed=size, transcendentals=0),
    )(*args)


def struct(rows, cols, dtype):
    return jax.ShapeDtypeStruct((rows, cols), dtype)


def inverse_norm(values):
    return lax.rsqrt(jnp.sum(values * values, axis=1, keepdims=True) + EPSILON)


def unit_txt_body(source, bf, head, tail, unit_out, inv, held, sem):
    copy = pltpu.make_async_copy(source, held, sem)
    copy.start()
    copy.wait()
    values = held[...]
    inverse = inverse_norm(values)
    unit = values * inverse
    rounded = unit.astype(BF16)
    bf[...] = rounded
    head[...] = rounded[: head.shape[0]]
    tail[...] = rounded[head.shape[0] :]
    unit_out[...] = unit
    inv[...] = jnp.broadcast_to(inverse, inv.shape)


def unit_img_body(place, other, source, bf, other_bf, other_turned, unit_out, inv, held, sem):
    copy = pltpu.make_async_copy(source, held, sem)
    copy.start()
    values = other[...]
    rounded = (values * inverse_norm(values)).astype(BF16)
    other_bf[...] = rounded
    other_turned[...] = rounded.T
    copy.wait()
    values = held[...]
    bf[...] = (values * inverse_norm(values)).astype(BF16)
    rows = unit_out.shape[0]
    values = held[pl.ds(pl.multiple_of(place[0] * rows, rows), rows), :]
    inverse = inverse_norm(values)
    unit_out[...] = values * inverse
    inv[...] = jnp.broadcast_to(inverse, inv.shape)


def weights_of(tile, order, line, place, column, scale, shift, perm, img, img_dim=1):
    rows = tile.shape[0] // len(order)
    row = lax.broadcasted_iota(jnp.int32, (rows, 1), 0)
    ids = jnp.concatenate(
        [row + (place[0] * line + (column[0] ^ (2 * k))) * rows for k in order], axis=0
    )
    products = lax.dot_general(
        tile, img, (((1,), (img_dim,)), ((), ())), preferred_element_type=F32
    )
    positive = (ids == perm).astype(F32)
    return (jax.nn.sigmoid(scale[0] * products + shift[0]) - positive).astype(BF16)


def to_images(weights, tile):
    return lax.dot_general(weights, tile, (((0,), (0,)), ((), ())), preferred_element_type=F32)


def to_texts(weights, img):
    return jnp.dot(weights, img, preferred_element_type=F32)


def joined(tiles):
    return jnp.concatenate([t[...] for t in tiles], axis=0)


def other_body(slots, order, line, place, column, scale, shift, perm, turned, *refs):
    *txt, kept, out = refs
    tile = joined([txt[k] for k in slots])
    weights = weights_of(tile, order, line, place, column, scale, shift, perm[...], turned[...], 0)
    kept[...] = weights
    out[...] = to_images(weights, tile).astype(BF16)


def own_body(slots, order, line, place, column, scale, shift, perm, img, img_other, kept, *refs):
    *txt, own_sum, txt_sums = refs
    tile = joined([txt[k] for k in slots])
    weights = weights_of(tile, order, line, place, column, scale, shift, perm[...], img[...])
    own_sum[...] = to_images(weights, tile)
    txt_sums[...] = to_texts(weights, img[...]) + to_texts(kept[...], img_other[...])


def split_body(count, blocks, place, own, other, txt_sums, *refs):
    txt_out, (keep, *send) = refs[:blocks], refs[blocks:]
    rows = txt_out[0].shape[0]
    for k, out in enumerate(txt_out):
        out[...] = txt_sums[k * rows : (k + 1) * rows, :].astype(out.dtype)
    rows = keep.shape[0]
    for k in range(count):
        start = pl.multiple_of((place[0] ^ k) * rows, rows)
        part = own[pl.ds(start, rows), :] + other[pl.ds(start, rows), :].astype(F32)
        if k == 0:
            keep[...] = part
        else:
            send[k - 1][...] = part.astype(BF16)


def total_of(own, parts):
    total = own[...]
    for part in parts:
        total = total + part[...].astype(F32)
    return total


def backward_unit(unit, inverse, upstream):
    along = jnp.sum(unit * upstream, axis=1, keepdims=True)
    return inverse[:, :1] * (upstream - unit * along)


def finish_img_body(scale, unit, inverse, own, *refs):
    *parts, out = refs
    out[...] = backward_unit(
        unit[...], inverse[...], scale[0] * total_of(own, parts)
    ).astype(BF16)


def quarter_copies(partners, place, parts, img_out, img_held, sems):
    rows = parts[0].shape[0]
    copies = []
    for k, (partner, part) in enumerate(zip(partners, parts)):
        img_held[k * rows : (k + 1) * rows, :] = part[...].astype(F32)
        start = pl.multiple_of((place[0] ^ partner) * rows, rows)
        copies.append(
            pltpu.make_async_copy(
                img_held.at[pl.ds(k * rows, rows), :],
                img_out.at[pl.ds(start, rows), :],
                sems.at[k],
            )
        )
        copies[-1].start()
    return copies


def first_body(partners, place, scale, unit, inverse, own, *refs):
    count = len(partners)
    parts = refs[:count]
    *back, img_out, txt_out, img_held, txt_held, sems = refs[count:]
    copies = quarter_copies(partners, place, parts, img_out, img_held, sems)
    txt_held[...] = backward_unit(unit[...], inverse[...], scale[0] * total_of(own, back))
    copies.append(pltpu.make_async_copy(txt_held, txt_out, sems.at[count]))
    copies[-1].start()
    for copy in copies:
        copy.wait()


def last_body(partners, place, begun, *refs):
    del begun
    *parts, img_out, img_held, sems = refs
    for copy in quarter_copies(partners, place, parts, img_out, img_held, sems):
        copy.wait()


def swapped(value, axis, step):
    count = lax.axis_size(axis)
    return lax.ppermute(value, axis, [(s, s ^ step) for s in range(count)])


def local(images, texts, perm, scale, shift):
    rows, width = images.shape
    txt_rows = texts.shape[0]
    line = lax.axis_size("txt")
    blocks = line // 2
    count = lax.axis_size("img")
    part = rows // count
    column = lax.axis_index("txt").reshape(1).astype(jnp.int32)
    place = lax.axis_index("img").reshape(1).astype(jnp.int32)
    perm_row = perm.reshape(1, rows)

    perm_other = swapped(perm_row, "txt", 1)
    raw_other = swapped(images, "txt", 1)
    first = txt_rows // 2
    txt_bf, head, tail, txt_unit, txt_inv = call(
        unit_txt_body,
        [struct(size, width, BF16) for size in (txt_rows, first, txt_rows - first)]
        + [struct(txt_rows, width, F32), struct(txt_rows, 128, F32)],
        [in_hbm(texts)],
        [ANY],
        16 << 20,
        4 * txt_rows * width,
        [pltpu.VMEM((txt_rows, width), F32), pltpu.SemaphoreType.DMA],
    )
    half = blocks // 2
    order = list(range(0, blocks, 2)) + list(range(1, blocks, 2))
    far = [swapped(piece, "txt", 4 * k) for k in range(1, half) for piece in (head, tail)]
    near = [swapped(txt_bf, "txt", 2)]
    for k in range(1, half):
        near += [swapped(far[2 * k - 2], "txt", 2), swapped(tail, "txt", 4 * k + 2)]
    ranks = [0, *(1, 5) * (half - 1), 2, *(3, 4) * (half - 1)]
    stand = sorted(range(len(ranks)), key=lambda k: ranks[k])
    tiles = [([txt_bf] + far + near)[k] for k in stand]
    slots = [stand.index(k) for k in range(len(stand))]
    img_bf, img_other, turned_other, img_unit, img_inv = call(
        unit_img_body,
        [struct(rows, width, BF16)] * 2
        + [struct(width, rows, BF16), struct(part, width, F32), struct(part, 128, F32)],
        [place, raw_other, in_hbm(images)],
        [SMEM, VMEM, ANY],
        24 << 20,
        8 * rows * width,
        [pltpu.VMEM((rows, width), F32), pltpu.SemaphoreType.DMA],
    )
    scalars = [place, column, scale, shift]
    pairs = 2 * rows * blocks * txt_rows * width
    kept, other_img = call(
        functools.partial(other_body, slots, order, line),
        [struct(blocks * txt_rows, rows, BF16), struct(rows, width, BF16)],
        [*scalars, perm_other, turned_other, *tiles],
        [SMEM] * 4 + [VMEM] * (2 + len(tiles)),
        40 << 20,
        2 * pairs,
    )
    from_other = swapped(other_img, "txt", 1)
    own_img, txt_sums = call(
        functools.partial(own_body, slots, order, line),
        [struct(rows, width, F32), struct(blocks * txt_rows, width, F32)],
        [*scalars, perm_row, img_bf, img_other, kept, *tiles],
        [SMEM] * 4 + [VMEM] * (4 + len(tiles)),
        40 << 20,
        4 * pairs,
    )
    outs = call(
        functools.partial(split_body, count, blocks),
        [struct(txt_rows, width, F32)]
        + [struct(txt_rows, width, BF16)] * (blocks - 1)
        + [struct(part, width, F32)]
        + [struct(part, width, BF16)] * (count - 1),
        [place, own_img, from_other, txt_sums],
        [SMEM] + [VMEM] * 3,
        24 << 20,
        rows * width,
    )
    (own_txt, *send_txt), (keep, *send) = outs[:blocks], outs[blocks:]
    got = [swapped(send[k - 1], "img", k) for k in (2, 1, *range(3, count))]
    homes = sorted(zip(order[1:], send_txt), key=lambda pair: pair[0])
    back = [swapped(block, "txt", 2 * k) for k, block in homes]
    (grad_part,) = call(
        finish_img_body,
        [struct(part, width, BF16)],
        [scale, img_unit, img_inv, keep, *got],
        [SMEM] + [VMEM] * (2 + count),
        24 << 20,
        10 * part * width,
    )
    partners = [1, *range(count - 1, 1, -1)]
    grads = [grad_part] + [swapped(grad_part, "img", k) for k in partners]
    partners = [0, *partners]
    early = 2
    begun, grad_texts = pl.pallas_call(
        functools.partial(first_body, partners[:early]),
        out_shape=[struct(rows, width, F32), struct(txt_rows, width, F32)],
        in_specs=[SMEM] * 2 + [VMEM] * (2 + early + blocks),
        out_specs=[ANY] * 2,
        scratch_shapes=[
            pltpu.VMEM((early * part, width), F32),
            pltpu.VMEM((txt_rows, width), F32),
            pltpu.SemaphoreType.DMA((early + 1,)),
        ],
        compiler_params=pltpu.CompilerParams(vmem_limit_bytes=24 << 20),
        cost_estimate=pl.CostEstimate(
            flops=10 * txt_rows * width, bytes_accessed=8 * rows * width, transcendentals=0
        ),
    )(place, scale, txt_unit, txt_inv, own_txt, *grads[:early], *back)
    grad_images = pl.pallas_call(
        functools.partial(last_body, partners[early:]),
        out_shape=struct(rows, width, F32),
        in_specs=[SMEM, ANY] + [VMEM] * (count - early),
        out_specs=ANY,
        scratch_shapes=[
            pltpu.VMEM(((count - early) * part, width), F32),
            pltpu.SemaphoreType.DMA((count - early,)),
        ],
        input_output_aliases={1: 0},
        compiler_params=pltpu.CompilerParams(vmem_limit_bytes=24 << 20),
        cost_estimate=pl.CostEstimate(
            flops=rows * width, bytes_accessed=8 * rows * width, transcendentals=0
        ),
    )(place, begun, *grads[early:])
    return (grad_images, grad_texts)


def solution(mesh):
    placed = (P("txt", None), P(("img", "txt"), None), P("txt"), P(), P())
    return jax.shard_map(
        local,
        mesh=mesh,
        in_specs=placed,
        out_specs=(P("txt", None), P(("img", "txt"), None)),
        check_vma=False,
    )
```

```python
import functools

import jax
import jax.numpy as jnp
from jax import lax
from jax.experimental import pallas as pl
from jax.experimental.pallas import tpu as pltpu
from jax.sharding import PartitionSpec as P

EPSILON = 1e-06
F32 = jnp.float32
BF16 = jnp.bfloat16
VMEM = pl.BlockSpec(memory_space=pltpu.VMEM)
ANY = pl.BlockSpec(memory_space=pl.ANY)
SMEM = pl.BlockSpec(memory_space=pltpu.SMEM)


def in_hbm(value):
    return pltpu.with_memory_space_constraint(value, pltpu.HBM)


def call(body, outs, args, specs, limit, flops, scratch=()):
    size = sum(a.size * a.dtype.itemsize for a in args)
    size += sum(o.size * o.dtype.itemsize for o in outs)
    return pl.pallas_call(
        body,
        out_shape=outs,
        in_specs=specs,
        out_specs=[VMEM] * len(outs),
        scratch_shapes=scratch,
        compiler_params=pltpu.CompilerParams(vmem_limit_bytes=limit),
        cost_estimate=pl.CostEstimate(flops=flops, bytes_accessed=size, transcendentals=0),
    )(*args)


def struct(rows, cols, dtype):
    return jax.ShapeDtypeStruct((rows, cols), dtype)


def inverse_norm(values):
    return lax.rsqrt(jnp.sum(values * values, axis=1, keepdims=True) + EPSILON)


def unit_txt_body(source, bf, head, tail, unit_out, inv, held, sem):
    copy = pltpu.make_async_copy(source, held, sem)
    copy.start()
    copy.wait()
    values = held[...]
    inverse = inverse_norm(values)
    unit = values * inverse
    rounded = unit.astype(BF16)
    bf[...] = rounded
    head[...] = rounded[: head.shape[0]]
    tail[...] = rounded[head.shape[0] :]
    unit_out[...] = unit
    inv[...] = jnp.broadcast_to(inverse, inv.shape)


def unit_img_body(place, other, source, bf, other_bf, other_turned, unit_out, inv, held, sem):
    copy = pltpu.make_async_copy(source, held, sem)
    copy.start()
    values = other[...]
    rounded = (values * inverse_norm(values)).astype(BF16)
    other_bf[...] = rounded
    other_turned[...] = rounded.T
    copy.wait()
    values = held[...]
    bf[...] = (values * inverse_norm(values)).astype(BF16)
    rows = unit_out.shape[0]
    values = held[pl.ds(pl.multiple_of(place[0] * rows, rows), rows), :]
    inverse = inverse_norm(values)
    unit_out[...] = values * inverse
    inv[...] = jnp.broadcast_to(inverse, inv.shape)


def weights_of(tile, order, line, place, column, scale, shift, perm, img, img_dim=1):
    rows = tile.shape[0] // len(order)
    row = lax.broadcasted_iota(jnp.int32, (rows, 1), 0)
    ids = jnp.concatenate(
        [row + (place[0] * line + (column[0] ^ (2 * k))) * rows for k in order], axis=0
    )
    products = lax.dot_general(
        tile, img, (((1,), (img_dim,)), ((), ())), preferred_element_type=F32
    )
    positive = (ids == perm).astype(F32)
    return (jax.nn.sigmoid(scale[0] * products + shift[0]) - positive).astype(BF16)


def to_images(weights, tile):
    return lax.dot_general(weights, tile, (((0,), (0,)), ((), ())), preferred_element_type=F32)


def to_texts(weights, img):
    return jnp.dot(weights, img, preferred_element_type=F32)


def joined(tiles):
    return jnp.concatenate([t[...] for t in tiles], axis=0)


def other_body(slots, order, line, place, column, scale, shift, perm, turned, *refs):
    *txt, kept, out = refs
    tile = joined([txt[k] for k in slots])
    weights = weights_of(tile, order, line, place, column, scale, shift, perm[...], turned[...], 0)
    kept[...] = weights
    out[...] = to_images(weights, tile).astype(BF16)


def own_body(slots, order, line, place, column, scale, shift, perm, img, img_other, kept, *refs):
    *txt, own_sum, txt_sums = refs
    tile = joined([txt[k] for k in slots])
    weights = weights_of(tile, order, line, place, column, scale, shift, perm[...], img[...])
    own_sum[...] = to_images(weights, tile)
    txt_sums[...] = to_texts(weights, img[...]) + to_texts(kept[...], img_other[...])


def split_body(partners, blocks, place, column, own, other, txt_sums, *refs):
    txt_out, (keep, *send) = refs[:blocks], refs[blocks:]
    rows = txt_out[0].shape[0]
    for k, out in enumerate(txt_out):
        out[...] = txt_sums[k * rows : (k + 1) * rows, :].astype(out.dtype)
    rows = keep.shape[0]
    core = column[0] & 1
    for out, (even, odd) in zip([keep, *send], [(0, 0), *partners]):
        start = pl.multiple_of((place[0] ^ (even + core * (odd - even))) * rows, rows)
        part = own[pl.ds(start, rows), :] + other[pl.ds(start, rows), :].astype(F32)
        out[...] = part.astype(out.dtype)


def total_of(own, parts):
    total = own[...]
    for part in parts:
        total = total + part[...].astype(F32)
    return total


def backward_unit(unit, inverse, upstream):
    along = jnp.sum(unit * upstream, axis=1, keepdims=True)
    return inverse[:, :1] * (upstream - unit * along)


def finish_img_body(scale, unit, inverse, own, *refs):
    *parts, out = refs
    out[...] = backward_unit(
        unit[...], inverse[...], scale[0] * total_of(own, parts)
    ).astype(BF16)


def quarter_copies(partners, place, parts, img_out, img_held, sems):
    rows = parts[0].shape[0]
    copies = []
    for k, (partner, part) in enumerate(zip(partners, parts)):
        img_held[k * rows : (k + 1) * rows, :] = part[...].astype(F32)
        start = pl.multiple_of((place[0] ^ partner) * rows, rows)
        copies.append(
            pltpu.make_async_copy(
                img_held.at[pl.ds(k * rows, rows), :],
                img_out.at[pl.ds(start, rows), :],
                sems.at[k],
            )
        )
        copies[-1].start()
    return copies


def first_body(partners, place, scale, unit, inverse, own, *refs):
    count = len(partners)
    parts = refs[:count]
    *back, img_out, txt_out, img_held, txt_held, sems = refs[count:]
    copies = quarter_copies(partners, place, parts, img_out, img_held, sems)
    txt_held[...] = backward_unit(unit[...], inverse[...], scale[0] * total_of(own, back))
    copies.append(pltpu.make_async_copy(txt_held, txt_out, sems.at[count]))
    copies[-1].start()
    for copy in copies:
        copy.wait()


def last_body(partners, place, begun, *refs):
    del begun
    *parts, img_out, img_held, sems = refs
    for copy in quarter_copies(partners, place, parts, img_out, img_held, sems):
        copy.wait()


def swapped(value, axis, step):
    count = lax.axis_size(axis)
    return lax.ppermute(value, axis, [(s, s ^ step) for s in range(count)])


def plane_swapped(value, even, odd):
    count, line = lax.axis_size("img"), lax.axis_size("txt")
    pairs = [
        (i * line + t, (i ^ (odd if t % 2 else even)) * line + t)
        for i in range(count)
        for t in range(line)
    ]
    return lax.ppermute(value, ("img", "txt"), pairs)


def local(images, texts, perm, scale, shift):
    rows, width = images.shape
    txt_rows = texts.shape[0]
    line = lax.axis_size("txt")
    blocks = line // 2
    count = lax.axis_size("img")
    part = rows // count
    column = lax.axis_index("txt").reshape(1).astype(jnp.int32)
    place = lax.axis_index("img").reshape(1).astype(jnp.int32)
    perm_row = perm.reshape(1, rows)

    perm_other = swapped(perm_row, "txt", 1)
    raw_other = swapped(images, "txt", 1)
    first = txt_rows // 2
    txt_bf, head, tail, txt_unit, txt_inv = call(
        unit_txt_body,
        [struct(size, width, BF16) for size in (txt_rows, first, txt_rows - first)]
        + [struct(txt_rows, width, F32), struct(txt_rows, 128, F32)],
        [in_hbm(texts)],
        [ANY],
        16 << 20,
        4 * txt_rows * width,
        [pltpu.VMEM((txt_rows, width), F32), pltpu.SemaphoreType.DMA],
    )
    half = blocks // 2
    order = list(range(0, blocks, 2)) + list(range(1, blocks, 2))
    far = [swapped(piece, "txt", 4 * k) for k in range(1, half) for piece in (head, tail)]
    near = [swapped(txt_bf, "txt", 2)]
    for k in range(1, half):
        near += [swapped(far[2 * k - 2], "txt", 2), swapped(tail, "txt", 4 * k + 2)]
    ranks = [0, *(1, 5) * (half - 1), 2, *(3, 4) * (half - 1)]
    stand = sorted(range(len(ranks)), key=lambda k: ranks[k])
    tiles = [([txt_bf] + far + near)[k] for k in stand]
    slots = [stand.index(k) for k in range(len(stand))]
    img_bf, img_other, turned_other, img_unit, img_inv = call(
        unit_img_body,
        [struct(rows, width, BF16)] * 2
        + [struct(width, rows, BF16), struct(part, width, F32), struct(part, 128, F32)],
        [place, raw_other, in_hbm(images)],
        [SMEM, VMEM, ANY],
        24 << 20,
        8 * rows * width,
        [pltpu.VMEM((rows, width), F32), pltpu.SemaphoreType.DMA],
    )
    scalars = [place, column, scale, shift]
    pairs = 2 * rows * blocks * txt_rows * width
    kept, other_img = call(
        functools.partial(other_body, slots, order, line),
        [struct(blocks * txt_rows, rows, BF16), struct(rows, width, BF16)],
        [*scalars, perm_other, turned_other, *tiles],
        [SMEM] * 4 + [VMEM] * (2 + len(tiles)),
        40 << 20,
        2 * pairs,
    )
    from_other = swapped(other_img, "txt", 1)
    own_img, txt_sums = call(
        functools.partial(own_body, slots, order, line),
        [struct(rows, width, F32), struct(blocks * txt_rows, width, F32)],
        [*scalars, perm_row, img_bf, img_other, kept, *tiles],
        [SMEM] * 4 + [VMEM] * (4 + len(tiles)),
        40 << 20,
        4 * pairs,
    )
    turns = [(1, 3), (2, 1), (3, 2)] + [(k, k) for k in range(4, count)]
    outs = call(
        functools.partial(split_body, turns, blocks),
        [struct(txt_rows, width, F32)]
        + [struct(txt_rows, width, BF16)] * (blocks - 1)
        + [struct(part, width, F32)]
        + [struct(part, width, BF16)] * (count - 1),
        [place, column, own_img, from_other, txt_sums],
        [SMEM] * 2 + [VMEM] * 3,
        24 << 20,
        rows * width,
    )
    (own_txt, *send_txt), (keep, *send) = outs[:blocks], outs[blocks:]
    got = [plane_swapped(block, *turn) for block, turn in zip(send, turns)]
    homes = sorted(zip(order[1:], send_txt), key=lambda pair: pair[0])
    back = [swapped(block, "txt", 2 * k) for k, block in homes]
    (grad_part,) = call(
        finish_img_body,
        [struct(part, width, BF16)],
        [scale, img_unit, img_inv, keep, *got],
        [SMEM] + [VMEM] * (2 + count),
        24 << 20,
        10 * part * width,
    )
    partners = [1, *range(count - 1, 1, -1)]
    grads = [grad_part] + [swapped(grad_part, "img", k) for k in partners]
    partners = [0, *partners]
    early = 2
    begun, grad_texts = pl.pallas_call(
        functools.partial(first_body, partners[:early]),
        out_shape=[struct(rows, width, F32), struct(txt_rows, width, F32)],
        in_specs=[SMEM] * 2 + [VMEM] * (2 + early + blocks),
        out_specs=[ANY] * 2,
        scratch_shapes=[
            pltpu.VMEM((early * part, width), F32),
            pltpu.VMEM((txt_rows, width), F32),
            pltpu.SemaphoreType.DMA((early + 1,)),
        ],
        compiler_params=pltpu.CompilerParams(vmem_limit_bytes=24 << 20),
        cost_estimate=pl.CostEstimate(
            flops=10 * txt_rows * width, bytes_accessed=8 * rows * width, transcendentals=0
        ),
    )(place, scale, txt_unit, txt_inv, own_txt, *grads[:early], *back)
    grad_images = pl.pallas_call(
        functools.partial(last_body, partners[early:]),
        out_shape=struct(rows, width, F32),
        in_specs=[SMEM, ANY] + [VMEM] * (count - early),
        out_specs=ANY,
        scratch_shapes=[
            pltpu.VMEM(((count - early) * part, width), F32),
            pltpu.SemaphoreType.DMA((count - early,)),
        ],
        input_output_aliases={1: 0},
        compiler_params=pltpu.CompilerParams(vmem_limit_bytes=24 << 20),
        cost_estimate=pl.CostEstimate(
            flops=rows * width, bytes_accessed=8 * rows * width, transcendentals=0
        ),
    )(place, begun, *grads[early:])
    return (grad_images, grad_texts)


def solution(mesh):
    placed = (P("txt", None), P(("img", "txt"), None), P("txt"), P(), P())
    return jax.shard_map(
        local,
        mesh=mesh,
        in_specs=placed,
        out_specs=(P("txt", None), P(("img", "txt"), None)),
        check_vma=False,
    )
```

```python
import functools

import jax
import jax.numpy as jnp
from jax import lax
from jax.experimental import pallas as pl
from jax.experimental.pallas import tpu as pltpu
from jax.sharding import PartitionSpec as P

EPSILON = 1e-06
F32 = jnp.float32
BF16 = jnp.bfloat16
VMEM = pl.BlockSpec(memory_space=pltpu.VMEM)
ANY = pl.BlockSpec(memory_space=pl.ANY)
SMEM = pl.BlockSpec(memory_space=pltpu.SMEM)


def in_hbm(value):
    return pltpu.with_memory_space_constraint(value, pltpu.HBM)


def call(body, outs, args, specs, limit, flops, scratch=()):
    size = sum(a.size * a.dtype.itemsize for a in args)
    size += sum(o.size * o.dtype.itemsize for o in outs)
    return pl.pallas_call(
        body,
        out_shape=outs,
        in_specs=specs,
        out_specs=[VMEM] * len(outs),
        scratch_shapes=scratch,
        compiler_params=pltpu.CompilerParams(vmem_limit_bytes=limit),
        cost_estimate=pl.CostEstimate(flops=flops, bytes_accessed=size, transcendentals=0),
    )(*args)


def struct(rows, cols, dtype):
    return jax.ShapeDtypeStruct((rows, cols), dtype)


def inverse_norm(values):
    return lax.rsqrt(jnp.sum(values * values, axis=1, keepdims=True) + EPSILON)


def unit_txt_body(source, bf, head, tail, unit_out, inv, held, sem):
    copy = pltpu.make_async_copy(source, held, sem)
    copy.start()
    copy.wait()
    values = held[...]
    inverse = inverse_norm(values)
    unit = values * inverse
    rounded = unit.astype(BF16)
    bf[...] = rounded
    head[...] = rounded[: head.shape[0]]
    tail[...] = rounded[head.shape[0] :]
    unit_out[...] = unit
    inv[...] = jnp.broadcast_to(inverse, inv.shape)


def unit_img_body(place, other, source, bf, other_bf, other_turned, unit_out, inv, held, sem):
    copy = pltpu.make_async_copy(source, held, sem)
    copy.start()
    values = other[...]
    rounded = (values * inverse_norm(values)).astype(BF16)
    other_bf[...] = rounded
    other_turned[...] = rounded.T
    copy.wait()
    values = held[...]
    bf[...] = (values * inverse_norm(values)).astype(BF16)
    rows = unit_out.shape[0]
    values = held[pl.ds(pl.multiple_of(place[0] * rows, rows), rows), :]
    inverse = inverse_norm(values)
    unit_out[...] = values * inverse
    inv[...] = jnp.broadcast_to(inverse, inv.shape)


def weights_of(tile, order, line, place, column, scale, shift, perm, img, img_dim=1):
    rows = tile.shape[0] // len(order)
    row = lax.broadcasted_iota(jnp.int32, (rows, 1), 0)
    ids = jnp.concatenate(
        [row + (place[0] * line + (column[0] ^ (2 * k))) * rows for k in order], axis=0
    )
    products = lax.dot_general(
        tile, img, (((1,), (img_dim,)), ((), ())), preferred_element_type=F32
    )
    positive = (ids == perm).astype(F32)
    return (jax.nn.sigmoid(scale[0] * products + shift[0]) - positive).astype(BF16)


def to_images(weights, tile):
    return lax.dot_general(weights, tile, (((0,), (0,)), ((), ())), preferred_element_type=F32)


def to_texts(weights, img):
    return jnp.dot(weights, img, preferred_element_type=F32)


def joined(tiles):
    return jnp.concatenate([t[...] for t in tiles], axis=0)


def other_body(slots, order, line, place, column, scale, shift, perm, turned, *refs):
    *txt, kept, out = refs
    tile = joined([txt[k] for k in slots])
    weights = weights_of(tile, order, line, place, column, scale, shift, perm[...], turned[...], 0)
    kept[...] = weights
    out[...] = to_images(weights, tile).astype(BF16)


def own_body(slots, order, line, place, column, scale, shift, perm, img, img_other, kept, *refs):
    *txt, own_sum, txt_sums = refs
    tile = joined([txt[k] for k in slots])
    weights = weights_of(tile, order, line, place, column, scale, shift, perm[...], img[...])
    own_sum[...] = to_images(weights, tile)
    txt_sums[...] = to_texts(weights, img[...]) + to_texts(kept[...], img_other[...])


def split_body(count, blocks, place, own, other, txt_sums, *refs):
    txt_out, (keep, *send) = refs[:blocks], refs[blocks:]
    rows = txt_out[0].shape[0]
    for k, out in enumerate(txt_out):
        out[...] = txt_sums[k * rows : (k + 1) * rows, :].astype(out.dtype)
    rows = keep.shape[0]
    for k in range(count):
        start = pl.multiple_of((place[0] ^ k) * rows, rows)
        part = own[pl.ds(start, rows), :] + other[pl.ds(start, rows), :].astype(F32)
        if k == 0:
            keep[...] = part
        else:
            send[k - 1][...] = part.astype(BF16)


def total_of(own, parts):
    total = own[...]
    for part in parts:
        total = total + part[...].astype(F32)
    return total


def backward_unit(unit, inverse, upstream):
    along = jnp.sum(unit * upstream, axis=1, keepdims=True)
    return inverse[:, :1] * (upstream - unit * along)


def finish_img_body(scale, unit, inverse, own, *refs):
    *parts, out = refs
    out[...] = backward_unit(
        unit[...], inverse[...], scale[0] * total_of(own, parts)
    ).astype(BF16)


def quarter_copies(partners, place, parts, img_out, img_held, sems):
    rows = parts[0].shape[0]
    copies = []
    for k, (partner, part) in enumerate(zip(partners, parts)):
        img_held[k * rows : (k + 1) * rows, :] = part[...].astype(F32)
        start = pl.multiple_of((place[0] ^ partner) * rows, rows)
        copies.append(
            pltpu.make_async_copy(
                img_held.at[pl.ds(k * rows, rows), :],
                img_out.at[pl.ds(start, rows), :],
                sems.at[k],
            )
        )
        copies[-1].start()
    return copies


def first_body(partners, place, scale, unit, inverse, own, *refs):
    count = len(partners)
    parts = refs[:count]
    *back, img_out, txt_out, img_held, txt_held, sems = refs[count:]
    copies = quarter_copies(partners, place, parts, img_out, img_held, sems)
    txt_held[...] = backward_unit(unit[...], inverse[...], scale[0] * total_of(own, back))
    copies.append(pltpu.make_async_copy(txt_held, txt_out, sems.at[count]))
    copies[-1].start()
    for copy in copies:
        copy.wait()


def last_body(partners, place, begun, *refs):
    del begun
    *parts, img_out, img_held, sems = refs
    for copy in quarter_copies(partners, place, parts, img_out, img_held, sems):
        copy.wait()


def swapped(value, axis, step):
    count = lax.axis_size(axis)
    return lax.ppermute(value, axis, [(s, s ^ step) for s in range(count)])


def local(images, texts, perm, scale, shift):
    rows, width = images.shape
    txt_rows = texts.shape[0]
    line = lax.axis_size("txt")
    blocks = line // 2
    count = lax.axis_size("img")
    part = rows // count
    column = lax.axis_index("txt").reshape(1).astype(jnp.int32)
    place = lax.axis_index("img").reshape(1).astype(jnp.int32)
    perm_row = perm.reshape(1, rows)

    perm_other = swapped(perm_row, "txt", 1)
    raw_other = swapped(images, "txt", 1)
    first = txt_rows // 2
    txt_bf, head, tail, txt_unit, txt_inv = call(
        unit_txt_body,
        [struct(size, width, BF16) for size in (txt_rows, first, txt_rows - first)]
        + [struct(txt_rows, width, F32), struct(txt_rows, 128, F32)],
        [in_hbm(texts)],
        [ANY],
        16 << 20,
        4 * txt_rows * width,
        [pltpu.VMEM((txt_rows, width), F32), pltpu.SemaphoreType.DMA],
    )
    half = blocks // 2
    order = list(range(0, blocks, 2)) + list(range(1, blocks, 2))
    far = [swapped(piece, "txt", 4 * k) for k in range(1, half) for piece in (head, tail)]
    near = [swapped(txt_bf, "txt", 2)]
    for k in range(1, half):
        near += [swapped(far[2 * k - 2], "txt", 2), swapped(tail, "txt", 4 * k + 2)]
    ranks = [0, *(1, 5) * (half - 1), 2, *(3, 4) * (half - 1)]
    stand = sorted(range(len(ranks)), key=lambda k: ranks[k])
    tiles = [([txt_bf] + far + near)[k] for k in stand]
    slots = [stand.index(k) for k in range(len(stand))]
    img_bf, img_other, turned_other, img_unit, img_inv = call(
        unit_img_body,
        [struct(rows, width, BF16)] * 2
        + [struct(width, rows, BF16), struct(part, width, F32), struct(part, 128, F32)],
        [place, raw_other, in_hbm(images)],
        [SMEM, VMEM, ANY],
        24 << 20,
        8 * rows * width,
        [pltpu.VMEM((rows, width), F32), pltpu.SemaphoreType.DMA],
    )
    scalars = [place, column, scale, shift]
    pairs = 2 * rows * blocks * txt_rows * width
    kept, other_img = call(
        functools.partial(other_body, slots, order, line),
        [struct(blocks * txt_rows, rows, BF16), struct(rows, width, BF16)],
        [*scalars, perm_other, turned_other, *tiles],
        [SMEM] * 4 + [VMEM] * (2 + len(tiles)),
        40 << 20,
        2 * pairs,
    )
    from_other = swapped(other_img, "txt", 1)
    own_img, txt_sums = call(
        functools.partial(own_body, slots, order, line),
        [struct(rows, width, F32), struct(blocks * txt_rows, width, F32)],
        [*scalars, perm_row, img_bf, img_other, kept, *tiles],
        [SMEM] * 4 + [VMEM] * (4 + len(tiles)),
        40 << 20,
        4 * pairs,
    )
    outs = call(
        functools.partial(split_body, count, blocks),
        [struct(txt_rows, width, F32)]
        + [struct(txt_rows, width, BF16)] * (blocks - 1)
        + [struct(part, width, F32)]
        + [struct(part, width, BF16)] * (count - 1),
        [place, own_img, from_other, txt_sums],
        [SMEM] + [VMEM] * 3,
        24 << 20,
        rows * width,
    )
    (own_txt, *send_txt), (keep, *send) = outs[:blocks], outs[blocks:]
    got = [swapped(send[k - 1], "img", k) for k in range(1, count)]
    homes = sorted(zip(order[1:], send_txt), key=lambda pair: (pair[0] % 2, pair[0]))
    back = [swapped(block, "txt", 2 * k) for k, block in homes]
    (grad_part,) = call(
        finish_img_body,
        [struct(part, width, BF16)],
        [scale, img_unit, img_inv, keep, *got],
        [SMEM] + [VMEM] * (2 + count),
        24 << 20,
        10 * part * width,
    )
    partners = [1, *range(count - 1, 1, -1)]
    grads = [grad_part] + [swapped(grad_part, "img", k) for k in partners]
    partners = [0, *partners]
    early = 2
    begun, grad_texts = pl.pallas_call(
        functools.partial(first_body, partners[:early]),
        out_shape=[struct(rows, width, F32), struct(txt_rows, width, F32)],
        in_specs=[SMEM] * 2 + [VMEM] * (2 + early + blocks),
        out_specs=[ANY] * 2,
        scratch_shapes=[
            pltpu.VMEM((early * part, width), F32),
            pltpu.VMEM((txt_rows, width), F32),
            pltpu.SemaphoreType.DMA((early + 1,)),
        ],
        compiler_params=pltpu.CompilerParams(vmem_limit_bytes=24 << 20),
        cost_estimate=pl.CostEstimate(
            flops=10 * txt_rows * width, bytes_accessed=8 * rows * width, transcendentals=0
        ),
    )(place, scale, txt_unit, txt_inv, own_txt, *grads[:early], *back)
    grad_images = pl.pallas_call(
        functools.partial(last_body, partners[early:]),
        out_shape=struct(rows, width, F32),
        in_specs=[SMEM, ANY] + [VMEM] * (count - early),
        out_specs=ANY,
        scratch_shapes=[
            pltpu.VMEM(((count - early) * part, width), F32),
            pltpu.SemaphoreType.DMA((count - early,)),
        ],
        input_output_aliases={1: 0},
        compiler_params=pltpu.CompilerParams(vmem_limit_bytes=24 << 20),
        cost_estimate=pl.CostEstimate(
            flops=rows * width, bytes_accessed=8 * rows * width, transcendentals=0
        ),
    )(place, begun, *grads[early:])
    return (grad_images, grad_texts)


def solution(mesh):
    placed = (P("txt", None), P(("img", "txt"), None), P("txt"), P(), P())
    return jax.shard_map(
        local,
        mesh=mesh,
        in_specs=placed,
        out_specs=(P("txt", None), P(("img", "txt"), None)),
        check_vma=False,
    )
```

```python
import functools

import jax
import jax.numpy as jnp
from jax import lax
from jax.experimental import pallas as pl
from jax.experimental.pallas import tpu as pltpu
from jax.sharding import PartitionSpec as P

EPSILON = 1e-06
F32 = jnp.float32
BF16 = jnp.bfloat16
VMEM = pl.BlockSpec(memory_space=pltpu.VMEM)
ANY = pl.BlockSpec(memory_space=pl.ANY)
SMEM = pl.BlockSpec(memory_space=pltpu.SMEM)


def in_hbm(value):
    return pltpu.with_memory_space_constraint(value, pltpu.HBM)


def call(body, outs, args, specs, limit, flops, scratch=()):
    size = sum(a.size * a.dtype.itemsize for a in args)
    size += sum(o.size * o.dtype.itemsize for o in outs)
    return pl.pallas_call(
        body,
        out_shape=outs,
        in_specs=specs,
        out_specs=[VMEM] * len(outs),
        scratch_shapes=scratch,
        compiler_params=pltpu.CompilerParams(vmem_limit_bytes=limit),
        cost_estimate=pl.CostEstimate(flops=flops, bytes_accessed=size, transcendentals=0),
    )(*args)


def struct(rows, cols, dtype):
    return jax.ShapeDtypeStruct((rows, cols), dtype)


def inverse_norm(values):
    return lax.rsqrt(jnp.sum(values * values, axis=1, keepdims=True) + EPSILON)


def unit_txt_body(source, bf, head, tail, unit_out, inv, held, sem):
    copy = pltpu.make_async_copy(source, held, sem)
    copy.start()
    copy.wait()
    values = held[...]
    inverse = inverse_norm(values)
    unit = values * inverse
    rounded = unit.astype(BF16)
    bf[...] = rounded
    head[...] = rounded[: head.shape[0]]
    tail[...] = rounded[head.shape[0] :]
    unit_out[...] = unit
    inv[...] = jnp.broadcast_to(inverse, inv.shape)


def unit_img_body(place, other, source, bf, other_bf, other_turned, unit_out, inv, held, sem):
    copy = pltpu.make_async_copy(source, held, sem)
    copy.start()
    values = other[...]
    rounded = (values * inverse_norm(values)).astype(BF16)
    other_bf[...] = rounded
    other_turned[...] = rounded.T
    copy.wait()
    values = held[...]
    bf[...] = (values * inverse_norm(values)).astype(BF16)
    rows = unit_out.shape[0]
    values = held[pl.ds(pl.multiple_of(place[0] * rows, rows), rows), :]
    inverse = inverse_norm(values)
    unit_out[...] = values * inverse
    inv[...] = jnp.broadcast_to(inverse, inv.shape)


def weights_of(tile, order, line, place, column, scale, shift, perm, img, img_dim=1):
    rows = tile.shape[0] // len(order)
    row = lax.broadcasted_iota(jnp.int32, (rows, 1), 0)
    ids = jnp.concatenate(
        [row + (place[0] * line + (column[0] ^ (2 * k))) * rows for k in order], axis=0
    )
    products = lax.dot_general(
        tile, img, (((1,), (img_dim,)), ((), ())), preferred_element_type=F32
    )
    positive = (ids == perm).astype(F32)
    return (jax.nn.sigmoid(scale[0] * products + shift[0]) - positive).astype(BF16)


def to_images(weights, tile):
    return lax.dot_general(weights, tile, (((0,), (0,)), ((), ())), preferred_element_type=F32)


def to_texts(weights, img):
    return jnp.dot(weights, img, preferred_element_type=F32)


def batch_body(*refs):
    *pieces, out = refs
    out[...] = joined(pieces)


def half_body(source, out):
    out[...] = source[out.shape[0] :, :]


def joined(tiles):
    return jnp.concatenate([t[...] for t in tiles], axis=0)


def other_body(slots, order, line, place, column, scale, shift, perm, turned, *refs):
    *txt, kept, out = refs
    tile = joined([txt[k] for k in slots])
    weights = weights_of(tile, order, line, place, column, scale, shift, perm[...], turned[...], 0)
    kept[...] = weights
    out[...] = to_images(weights, tile).astype(BF16)


def own_body(slots, order, line, place, column, scale, shift, perm, img, img_other, kept, *refs):
    *txt, own_sum, txt_sums, near_txt = refs
    tile = joined([txt[k] for k in slots])
    weights = weights_of(tile, order, line, place, column, scale, shift, perm[...], img[...])
    own_sum[...] = to_images(weights, tile)
    sums = to_texts(weights, img[...]) + to_texts(kept[...], img_other[...])
    txt_sums[...] = sums
    near = order.index(1) * near_txt.shape[0]
    near_txt[...] = sums[near : near + near_txt.shape[0]].astype(BF16)


def split_body(count, blocks, place, own, other, txt_sums, *refs):
    txt_out, (keep, *send) = refs[:blocks], refs[blocks:]
    rows = txt_out[0].shape[0]
    for k, out in enumerate(txt_out):
        out[...] = txt_sums[k * rows : (k + 1) * rows, :].astype(out.dtype)
    rows = keep.shape[0]
    for k in range(count):
        start = pl.multiple_of((place[0] ^ k) * rows, rows)
        part = own[pl.ds(start, rows), :] + other[pl.ds(start, rows), :].astype(F32)
        if k == 0:
            keep[...] = part
        else:
            send[k - 1][...] = part.astype(BF16)


def total_of(own, parts):
    total = own[...]
    for part in parts:
        total = total + part[...].astype(F32)
    return total


def backward_unit(unit, inverse, upstream):
    along = jnp.sum(unit * upstream, axis=1, keepdims=True)
    return inverse[:, :1] * (upstream - unit * along)


def finish_img_body(scale, unit, inverse, own, *refs):
    *parts, out = refs
    out[...] = backward_unit(
        unit[...], inverse[...], scale[0] * total_of(own, parts)
    ).astype(BF16)


def quarter_copies(partners, place, parts, img_out, img_held, sems):
    rows = parts[0].shape[0]
    copies = []
    for k, (partner, part) in enumerate(zip(partners, parts)):
        img_held[k * rows : (k + 1) * rows, :] = part[...].astype(F32)
        start = pl.multiple_of((place[0] ^ partner) * rows, rows)
        copies.append(
            pltpu.make_async_copy(
                img_held.at[pl.ds(k * rows, rows), :],
                img_out.at[pl.ds(start, rows), :],
                sems.at[k],
            )
        )
        copies[-1].start()
    return copies


def first_body(partners, place, scale, unit, inverse, own, *refs):
    count = len(partners)
    parts = refs[:count]
    *back, img_out, txt_out, img_held, txt_held, sems = refs[count:]
    copies = quarter_copies(partners, place, parts, img_out, img_held, sems)
    total = total_of(own, back[1:]) + back[0][: own.shape[0], :].astype(F32)
    txt_held[...] = backward_unit(unit[...], inverse[...], scale[0] * total)
    copies.append(pltpu.make_async_copy(txt_held, txt_out, sems.at[count]))
    copies[-1].start()
    for copy in copies:
        copy.wait()


def last_body(partners, place, begun, *refs):
    del begun
    *parts, img_out, img_held, sems = refs
    for copy in quarter_copies(partners, place, parts, img_out, img_held, sems):
        copy.wait()


def swapped(value, axis, step):
    count = lax.axis_size(axis)
    return lax.ppermute(value, axis, [(s, s ^ step) for s in range(count)])


def sent(value, step, core):
    line = lax.axis_size("txt")
    return lax.ppermute(value, "txt", [(t, t ^ step) for t in range(core, line, 2)])


def local(images, texts, perm, scale, shift):
    rows, width = images.shape
    txt_rows = texts.shape[0]
    line = lax.axis_size("txt")
    blocks = line // 2
    count = lax.axis_size("img")
    part = rows // count
    column = lax.axis_index("txt").reshape(1).astype(jnp.int32)
    place = lax.axis_index("img").reshape(1).astype(jnp.int32)
    perm_row = perm.reshape(1, rows)

    perm_other = swapped(perm_row, "txt", 1)
    raw_other = swapped(images, "txt", 1)
    first = txt_rows // 2
    txt_bf, head, tail, txt_unit, txt_inv = call(
        unit_txt_body,
        [struct(size, width, BF16) for size in (txt_rows, first, txt_rows - first)]
        + [struct(txt_rows, width, F32), struct(txt_rows, 128, F32)],
        [in_hbm(texts)],
        [ANY],
        16 << 20,
        4 * txt_rows * width,
        [pltpu.VMEM((txt_rows, width), F32), pltpu.SemaphoreType.DMA],
    )
    half = blocks // 2
    order = list(range(0, blocks, 2)) + list(range(1, blocks, 2))
    far = [swapped(piece, "txt", 4 * k) for k in range(1, half) for piece in (head, tail)]
    near = [swapped(txt_bf, "txt", 2)]
    for k in range(1, half):
        near += [swapped(far[2 * k - 2], "txt", 2), swapped(tail, "txt", 4 * k + 2)]
    ranks = [0, *(1, 5) * (half - 1), 2, *(3, 4) * (half - 1)]
    stand = sorted(range(len(ranks)), key=lambda k: ranks[k])
    tiles = [([txt_bf] + far + near)[k] for k in stand]
    slots = [stand.index(k) for k in range(len(stand))]
    img_bf, img_other, turned_other, img_unit, img_inv = call(
        unit_img_body,
        [struct(rows, width, BF16)] * 2
        + [struct(width, rows, BF16), struct(part, width, F32), struct(part, 128, F32)],
        [place, raw_other, in_hbm(images)],
        [SMEM, VMEM, ANY],
        24 << 20,
        8 * rows * width,
        [pltpu.VMEM((rows, width), F32), pltpu.SemaphoreType.DMA],
    )
    scalars = [place, column, scale, shift]
    pairs = 2 * rows * blocks * txt_rows * width
    kept, other_img = call(
        functools.partial(other_body, slots, order, line),
        [struct(blocks * txt_rows, rows, BF16), struct(rows, width, BF16)],
        [*scalars, perm_other, turned_other, *tiles],
        [SMEM] * 4 + [VMEM] * (2 + len(tiles)),
        40 << 20,
        2 * pairs,
    )
    from_other = swapped(other_img, "txt", 1)
    own_img, txt_sums, near_txt = call(
        functools.partial(own_body, slots, order, line),
        [struct(rows, width, F32), struct(blocks * txt_rows, width, F32)]
        + [struct(txt_rows, width, BF16)],
        [*scalars, perm_row, img_bf, img_other, kept, *tiles],
        [SMEM] * 4 + [VMEM] * (4 + len(tiles)),
        40 << 20,
        4 * pairs,
    )
    outs = call(
        functools.partial(split_body, count, blocks),
        [struct(txt_rows, width, F32)]
        + [struct(txt_rows, width, BF16)] * (blocks - 1)
        + [struct(part, width, F32)]
        + [struct(part, width, BF16)] * (count - 1),
        [place, own_img, from_other, txt_sums],
        [SMEM] + [VMEM] * 3,
        24 << 20,
        rows * width,
    )
    (own_txt, *send_txt), (keep, *send) = outs[:blocks], outs[blocks:]
    got = [swapped(send[k - 1], "img", k) for k in range(1, count)]
    homes = sorted(zip(order[1:], send_txt), key=lambda pair: pair[0])
    (both,) = call(
        batch_body,
        [struct(2 * txt_rows, width, BF16)],
        [near_txt, sent(near_txt, 1, 0)],
        [VMEM] * 2,
        16 << 20,
        txt_rows * width,
    )
    both = sent(both, 2, 1)
    (other_half,) = call(
        half_body, [struct(txt_rows, width, BF16)], [both], [VMEM], 16 << 20, txt_rows * width
    )
    back = [both, sent(other_half, 1, 1)]
    back += [swapped(block, "txt", 2 * k) for k, block in homes[1:]]
    (grad_part,) = call(
        finish_img_body,
        [struct(part, width, BF16)],
        [scale, img_unit, img_inv, keep, *got],
        [SMEM] + [VMEM] * (2 + count),
        24 << 20,
        10 * part * width,
    )
    partners = [1, *range(count - 1, 1, -1)]
    grads = [grad_part] + [swapped(grad_part, "img", k) for k in partners]
    partners = [0, *partners]
    early = 2
    begun, grad_texts = pl.pallas_call(
        functools.partial(first_body, partners[:early]),
        out_shape=[struct(rows, width, F32), struct(txt_rows, width, F32)],
        in_specs=[SMEM] * 2 + [VMEM] * (3 + early + blocks),
        out_specs=[ANY] * 2,
        scratch_shapes=[
            pltpu.VMEM((early * part, width), F32),
            pltpu.VMEM((txt_rows, width), F32),
            pltpu.SemaphoreType.DMA((early + 1,)),
        ],
        compiler_params=pltpu.CompilerParams(vmem_limit_bytes=24 << 20),
        cost_estimate=pl.CostEstimate(
            flops=10 * txt_rows * width, bytes_accessed=8 * rows * width, transcendentals=0
        ),
    )(place, scale, txt_unit, txt_inv, own_txt, *grads[:early], *back)
    grad_images = pl.pallas_call(
        functools.partial(last_body, partners[early:]),
        out_shape=struct(rows, width, F32),
        in_specs=[SMEM, ANY] + [VMEM] * (count - early),
        out_specs=ANY,
        scratch_shapes=[
            pltpu.VMEM(((count - early) * part, width), F32),
            pltpu.SemaphoreType.DMA((count - early,)),
        ],
        input_output_aliases={1: 0},
        compiler_params=pltpu.CompilerParams(vmem_limit_bytes=24 << 20),
        cost_estimate=pl.CostEstimate(
            flops=rows * width, bytes_accessed=8 * rows * width, transcendentals=0
        ),
    )(place, begun, *grads[early:])
    return (grad_images, grad_texts)


def solution(mesh):
    placed = (P("txt", None), P(("img", "txt"), None), P("txt"), P(), P())
    return jax.shard_map(
        local,
        mesh=mesh,
        in_specs=placed,
        out_specs=(P("txt", None), P(("img", "txt"), None)),
        check_vma=False,
    )
```

```python
import functools

import jax
import jax.numpy as jnp
from jax import lax
from jax.experimental import pallas as pl
from jax.experimental.pallas import tpu as pltpu
from jax.sharding import PartitionSpec as P

EPSILON = 1e-06
F32 = jnp.float32
BF16 = jnp.bfloat16
VMEM = pl.BlockSpec(memory_space=pltpu.VMEM)
ANY = pl.BlockSpec(memory_space=pl.ANY)
SMEM = pl.BlockSpec(memory_space=pltpu.SMEM)


def in_hbm(value):
    return pltpu.with_memory_space_constraint(value, pltpu.HBM)


def call(body, outs, args, specs, limit, flops, scratch=()):
    size = sum(a.size * a.dtype.itemsize for a in args)
    size += sum(o.size * o.dtype.itemsize for o in outs)
    return pl.pallas_call(
        body,
        out_shape=outs,
        in_specs=specs,
        out_specs=[VMEM] * len(outs),
        scratch_shapes=scratch,
        compiler_params=pltpu.CompilerParams(vmem_limit_bytes=limit),
        cost_estimate=pl.CostEstimate(flops=flops, bytes_accessed=size, transcendentals=0),
    )(*args)


def struct(rows, cols, dtype):
    return jax.ShapeDtypeStruct((rows, cols), dtype)


def inverse_norm(values):
    return lax.rsqrt(jnp.sum(values * values, axis=1, keepdims=True) + EPSILON)


def unit_txt_body(source, bf, head, tail, unit_out, inv, held, sem):
    copy = pltpu.make_async_copy(source, held, sem)
    copy.start()
    copy.wait()
    values = held[...]
    inverse = inverse_norm(values)
    unit = values * inverse
    rounded = unit.astype(BF16)
    bf[...] = rounded
    head[...] = rounded[: head.shape[0]]
    tail[...] = rounded[head.shape[0] :]
    unit_out[...] = unit
    inv[...] = jnp.broadcast_to(inverse, inv.shape)


def unit_img_body(place, other, source, bf, other_bf, unit_out, inv, held, sem):
    copy = pltpu.make_async_copy(source, held, sem)
    copy.start()
    values = other[...]
    other_bf[...] = (values * inverse_norm(values)).astype(BF16)
    copy.wait()
    values = held[...]
    bf[...] = (values * inverse_norm(values)).astype(BF16)
    rows = unit_out.shape[0]
    values = held[pl.ds(pl.multiple_of(place[0] * rows, rows), rows), :]
    inverse = inverse_norm(values)
    unit_out[...] = values * inverse
    inv[...] = jnp.broadcast_to(inverse, inv.shape)


def weights_of(tile, order, line, place, column, scale, shift, perm, img):
    rows = tile.shape[0] // len(order)
    row = lax.broadcasted_iota(jnp.int32, (rows, 1), 0)
    ids = jnp.concatenate(
        [row + (place[0] * line + (column[0] ^ (2 * k))) * rows for k in order], axis=0
    )
    products = lax.dot_general(tile, img, (((1,), (1,)), ((), ())), preferred_element_type=F32)
    positive = (ids == perm).astype(F32)
    return (jax.nn.sigmoid(scale[0] * products + shift[0]) - positive).astype(BF16)


def to_images(weights, tile):
    return lax.dot_general(weights, tile, (((0,), (0,)), ((), ())), preferred_element_type=F32)


def to_texts(weights, img):
    return jnp.dot(weights, img, preferred_element_type=F32)


def joined(tiles):
    return jnp.concatenate([t[...] for t in tiles], axis=0)


def other_body(slots, order, line, place, column, scale, shift, perm, img, *refs):
    *txt, kept, out = refs
    tile = joined([txt[k] for k in slots])
    texts, images = tile.shape[0], img.shape[0]
    rows = texts // len(order)
    lane = lax.broadcasted_iota(jnp.int32, (1, texts), 1)
    ids = lane
    for j, k in enumerate(order):
        shift_by = (place[0] * line + (column[0] ^ (2 * k))) * rows - j * rows
        ids = jnp.where(lane // rows == j, lane + shift_by, ids)
    paired = jnp.broadcast_to(perm[...], (128, images)).T[:, :1]
    products = lax.dot_general(
        img[...], tile, (((1,), (1,)), ((), ())), preferred_element_type=F32
    )
    positive = (paired == ids).astype(F32)
    weights = (jax.nn.sigmoid(scale[0] * products + shift[0]) - positive).astype(BF16)
    kept[...] = weights
    out[...] = jnp.dot(weights, tile, preferred_element_type=F32).astype(BF16)


def own_body(slots, order, line, place, column, scale, shift, perm, img, img_other, kept, *refs):
    *txt, own_sum, own_txt, txt_sums = refs
    tile = joined([txt[k] for k in slots])
    weights = weights_of(tile, order, line, place, column, scale, shift, perm[...], img[...])
    own_sum[...] = to_images(weights, tile)
    sums = to_texts(weights, img[...]) + to_images(kept[...], img_other[...])
    rows = own_txt.shape[0]
    own_txt[...] = sums[:rows]
    txt_sums[...] = sums[rows:].astype(BF16)


def split_body(count, blocks, place, own, other, txt_sums, *refs):
    txt_out, (keep, *send) = refs[:blocks], refs[blocks:]
    rows = txt_out[0].shape[0]
    for k, out in enumerate(txt_out):
        out[...] = txt_sums[k * rows : (k + 1) * rows, :]
    rows = keep.shape[0]
    for k in range(count):
        start = pl.multiple_of((place[0] ^ k) * rows, rows)
        part = own[pl.ds(start, rows), :] + other[pl.ds(start, rows), :].astype(F32)
        if k == 0:
            keep[...] = part
        else:
            send[k - 1][...] = part.astype(BF16)


def total_of(own, parts):
    total = own[...]
    for part in parts:
        total = total + part[...].astype(F32)
    return total


def backward_unit(unit, inverse, upstream):
    along = jnp.sum(unit * upstream, axis=1, keepdims=True)
    return inverse[:, :1] * (upstream - unit * along)


def finish_img_body(scale, unit, inverse, own, *refs):
    *parts, out = refs
    out[...] = backward_unit(
        unit[...], inverse[...], scale[0] * total_of(own, parts)
    ).astype(BF16)


def quarter_copies(partners, place, parts, img_out, img_held, sems):
    rows = parts[0].shape[0]
    copies = []
    for k, (partner, part) in enumerate(zip(partners, parts)):
        img_held[k * rows : (k + 1) * rows, :] = part[...].astype(F32)
        start = pl.multiple_of((place[0] ^ partner) * rows, rows)
        copies.append(
            pltpu.make_async_copy(
                img_held.at[pl.ds(k * rows, rows), :],
                img_out.at[pl.ds(start, rows), :],
                sems.at[k],
            )
        )
        copies[-1].start()
    return copies


def first_body(partners, place, scale, unit, inverse, own, *refs):
    count = len(partners)
    parts = refs[:count]
    *back, img_out, txt_out, img_held, txt_held, sems = refs[count:]
    copies = quarter_copies(partners, place, parts, img_out, img_held, sems)
    txt_held[...] = backward_unit(unit[...], inverse[...], scale[0] * total_of(own, back))
    copies.append(pltpu.make_async_copy(txt_held, txt_out, sems.at[count]))
    copies[-1].start()
    for copy in copies:
        copy.wait()


def last_body(partners, place, begun, *refs):
    del begun
    *parts, img_out, img_held, sems = refs
    for copy in quarter_copies(partners, place, parts, img_out, img_held, sems):
        copy.wait()


def swapped(value, axis, step):
    count = lax.axis_size(axis)
    return lax.ppermute(value, axis, [(s, s ^ step) for s in range(count)])


def local(images, texts, perm, scale, shift):
    rows, width = images.shape
    txt_rows = texts.shape[0]
    line = lax.axis_size("txt")
    blocks = line // 2
    count = lax.axis_size("img")
    part = rows // count
    column = lax.axis_index("txt").reshape(1).astype(jnp.int32)
    place = lax.axis_index("img").reshape(1).astype(jnp.int32)
    perm_row = perm.reshape(1, rows)

    perm_other = swapped(perm_row, "txt", 1)
    raw_other = swapped(images, "txt", 1)
    first = txt_rows // 2
    txt_bf, head, tail, txt_unit, txt_inv = call(
        unit_txt_body,
        [struct(size, width, BF16) for size in (txt_rows, first, txt_rows - first)]
        + [struct(txt_rows, width, F32), struct(txt_rows, 128, F32)],
        [in_hbm(texts)],
        [ANY],
        16 << 20,
        4 * txt_rows * width,
        [pltpu.VMEM((txt_rows, width), F32), pltpu.SemaphoreType.DMA],
    )
    half = blocks // 2
    order = list(range(0, blocks, 2)) + list(range(1, blocks, 2))
    far = [swapped(piece, "txt", 4 * k) for k in range(1, half) for piece in (head, tail)]
    near = [swapped(txt_bf, "txt", 2)]
    for k in range(1, half):
        near += [swapped(far[2 * k - 2], "txt", 2), swapped(tail, "txt", 4 * k + 2)]
    ranks = [0, *(1, 5) * (half - 1), 2, *(3, 4) * (half - 1)]
    stand = sorted(range(len(ranks)), key=lambda k: ranks[k])
    tiles = [([txt_bf] + far + near)[k] for k in stand]
    slots = [stand.index(k) for k in range(len(stand))]
    img_bf, img_other, img_unit, img_inv = call(
        unit_img_body,
        [struct(rows, width, BF16)] * 2 + [struct(part, width, F32), struct(part, 128, F32)],
        [place, raw_other, in_hbm(images)],
        [SMEM, VMEM, ANY],
        24 << 20,
        8 * rows * width,
        [pltpu.VMEM((rows, width), F32), pltpu.SemaphoreType.DMA],
    )
    scalars = [place, column, scale, shift]
    pairs = 2 * rows * blocks * txt_rows * width
    kept, other_img = call(
        functools.partial(other_body, slots, order, line),
        [struct(rows, blocks * txt_rows, BF16), struct(rows, width, BF16)],
        [*scalars, perm_other, img_other, *tiles],
        [SMEM] * 4 + [VMEM] * (2 + len(tiles)),
        40 << 20,
        2 * pairs,
    )
    from_other = swapped(other_img, "txt", 1)
    own_img, own_txt, txt_sums = call(
        functools.partial(own_body, slots, order, line),
        [
            struct(rows, width, F32),
            struct(txt_rows, width, F32),
            struct((blocks - 1) * txt_rows, width, BF16),
        ],
        [*scalars, perm_row, img_bf, img_other, kept, *tiles],
        [SMEM] * 4 + [VMEM] * (4 + len(tiles)),
        40 << 20,
        4 * pairs,
    )
    outs = call(
        functools.partial(split_body, count, blocks - 1),
        [struct(txt_rows, width, BF16)] * (blocks - 1)
        + [struct(part, width, F32)]
        + [struct(part, width, BF16)] * (count - 1),
        [place, own_img, from_other, txt_sums],
        [SMEM] + [VMEM] * 3,
        24 << 20,
        rows * width,
    )
    send_txt, (keep, *send) = outs[: blocks - 1], outs[blocks - 1 :]
    got = [swapped(send[k - 1], "img", k) for k in range(1, count)]
    homes = sorted(zip(order[1:], send_txt), key=lambda pair: pair[0])
    back = [swapped(block, "txt", 2 * k) for k, block in homes]
    (grad_part,) = call(
        finish_img_body,
        [struct(part, width, BF16)],
        [scale, img_unit, img_inv, keep, *got],
        [SMEM] + [VMEM] * (2 + count),
        24 << 20,
        10 * part * width,
    )
    partners = [1, *range(count - 1, 1, -1)]
    grads = [grad_part] + [swapped(grad_part, "img", k) for k in partners]
    partners = [0, *partners]
    early = 2
    begun, grad_texts = pl.pallas_call(
        functools.partial(first_body, partners[:early]),
        out_shape=[struct(rows, width, F32), struct(txt_rows, width, F32)],
        in_specs=[SMEM] * 2 + [VMEM] * (2 + early + blocks),
        out_specs=[ANY] * 2,
        scratch_shapes=[
            pltpu.VMEM((early * part, width), F32),
            pltpu.VMEM((txt_rows, width), F32),
            pltpu.SemaphoreType.DMA((early + 1,)),
        ],
        compiler_params=pltpu.CompilerParams(vmem_limit_bytes=24 << 20),
        cost_estimate=pl.CostEstimate(
            flops=10 * txt_rows * width, bytes_accessed=8 * rows * width, transcendentals=0
        ),
    )(place, scale, txt_unit, txt_inv, own_txt, *grads[:early], *back)
    grad_images = pl.pallas_call(
        functools.partial(last_body, partners[early:]),
        out_shape=struct(rows, width, F32),
        in_specs=[SMEM, ANY] + [VMEM] * (count - early),
        out_specs=ANY,
        scratch_shapes=[
            pltpu.VMEM(((count - early) * part, width), F32),
            pltpu.SemaphoreType.DMA((count - early,)),
        ],
        input_output_aliases={1: 0},
        compiler_params=pltpu.CompilerParams(vmem_limit_bytes=24 << 20),
        cost_estimate=pl.CostEstimate(
            flops=rows * width, bytes_accessed=8 * rows * width, transcendentals=0
        ),
    )(place, begun, *grads[early:])
    return (grad_images, grad_texts)


def solution(mesh):
    placed = (P("txt", None), P(("img", "txt"), None), P("txt"), P(), P())
    return jax.shard_map(
        local,
        mesh=mesh,
        in_specs=placed,
        out_specs=(P("txt", None), P(("img", "txt"), None)),
        check_vma=False,
    )
```

```python
import functools

import jax
import jax.numpy as jnp
from jax import lax
from jax.experimental import pallas as pl
from jax.experimental.pallas import tpu as pltpu
from jax.sharding import PartitionSpec as P

EPSILON = 1e-06
F32 = jnp.float32
BF16 = jnp.bfloat16
VMEM = pl.BlockSpec(memory_space=pltpu.VMEM)
ANY = pl.BlockSpec(memory_space=pl.ANY)
SMEM = pl.BlockSpec(memory_space=pltpu.SMEM)


def in_hbm(value):
    return pltpu.with_memory_space_constraint(value, pltpu.HBM)


def call(body, outs, args, specs, limit, flops, scratch=()):
    size = sum(a.size * a.dtype.itemsize for a in args)
    size += sum(o.size * o.dtype.itemsize for o in outs)
    return pl.pallas_call(
        body,
        out_shape=outs,
        in_specs=specs,
        out_specs=[VMEM] * len(outs),
        scratch_shapes=scratch,
        compiler_params=pltpu.CompilerParams(vmem_limit_bytes=limit),
        cost_estimate=pl.CostEstimate(flops=flops, bytes_accessed=size, transcendentals=0),
    )(*args)


def struct(rows, cols, dtype):
    return jax.ShapeDtypeStruct((rows, cols), dtype)


def inverse_norm(values):
    return lax.rsqrt(jnp.sum(values * values, axis=1, keepdims=True) + EPSILON)


def unit_txt_body(source, bf, head, tail, unit_out, inv, held, sem):
    copy = pltpu.make_async_copy(source, held, sem)
    copy.start()
    copy.wait()
    values = held[...]
    inverse = inverse_norm(values)
    unit = values * inverse
    rounded = unit.astype(BF16)
    bf[...] = rounded
    head[...] = rounded[: head.shape[0]]
    tail[...] = rounded[head.shape[0] :]
    unit_out[...] = unit
    inv[...] = jnp.broadcast_to(inverse, inv.shape)


def unit_img_body(place, other, source, bf, other_bf, unit_out, inv, held, sem):
    copy = pltpu.make_async_copy(source, held, sem)
    copy.start()
    values = other[...]
    other_bf[...] = (values * inverse_norm(values)).astype(BF16)
    copy.wait()
    values = held[...]
    bf[...] = (values * inverse_norm(values)).astype(BF16)
    rows = unit_out.shape[0]
    values = held[pl.ds(pl.multiple_of(place[0] * rows, rows), rows), :]
    inverse = inverse_norm(values)
    unit_out[...] = values * inverse
    inv[...] = jnp.broadcast_to(inverse, inv.shape)


def weights_of(tile, order, line, place, column, scale, shift, perm, img):
    rows = tile.shape[0] // len(order)
    row = lax.broadcasted_iota(jnp.int32, (rows, 1), 0)
    ids = jnp.concatenate(
        [row + (place[0] * line + (column[0] ^ (2 * k))) * rows for k in order], axis=0
    )
    products = lax.dot_general(tile, img, (((1,), (1,)), ((), ())), preferred_element_type=F32)
    positive = (ids == perm).astype(F32)
    return (jax.nn.sigmoid(scale[0] * products + shift[0]) - positive).astype(BF16)


def to_images(weights, tile):
    return lax.dot_general(weights, tile, (((0,), (0,)), ((), ())), preferred_element_type=F32)


def to_texts(weights, img):
    return jnp.dot(weights, img, preferred_element_type=F32)


def joined(tiles):
    return jnp.concatenate([t[...] for t in tiles], axis=0)


def other_body(slots, order, line, place, column, scale, shift, perm, img, *refs):
    *txt, kept, out = refs
    tile = joined([txt[k] for k in slots])
    texts, images = tile.shape[0], img.shape[0]
    rows = texts // len(order)
    lane = lax.broadcasted_iota(jnp.int32, (1, texts), 1)
    ids = lane
    for j, k in enumerate(order):
        shift_by = (place[0] * line + (column[0] ^ (2 * k))) * rows - j * rows
        ids = jnp.where(lane // rows == j, lane + shift_by, ids)
    paired = jnp.broadcast_to(perm[...], (128, images)).T[:, :1]
    products = lax.dot_general(
        img[...], tile, (((1,), (1,)), ((), ())), preferred_element_type=F32
    )
    positive = (paired == ids).astype(F32)
    weights = (jax.nn.sigmoid(scale[0] * products + shift[0]) - positive).astype(BF16)
    kept[...] = weights
    out[...] = jnp.dot(weights, tile, preferred_element_type=F32).astype(BF16)


def own_body(slots, order, line, place, column, scale, shift, perm, img, img_other, kept, *refs):
    *txt, own_sum, own_txt, txt_sums = refs
    tile = joined([txt[k] for k in slots])
    weights = weights_of(tile, order, line, place, column, scale, shift, perm[...], img[...])
    own_sum[...] = to_images(weights, tile)
    sums = to_texts(weights, img[...]) + to_images(kept[...], img_other[...])
    rows = own_txt.shape[0]
    own_txt[...] = sums[:rows]
    txt_sums[...] = sums[rows:].astype(BF16)


def split_body(count, blocks, place, own, other, txt_sums, *refs):
    txt_out, (keep, *send) = refs[:blocks], refs[blocks:]
    rows = txt_out[0].shape[0]
    for k, out in enumerate(txt_out):
        out[...] = txt_sums[k * rows : (k + 1) * rows, :]
    rows = keep.shape[0]
    for k in range(count):
        start = pl.multiple_of((place[0] ^ k) * rows, rows)
        part = own[pl.ds(start, rows), :] + other[pl.ds(start, rows), :].astype(F32)
        if k == 0:
            keep[...] = part
        else:
            send[k - 1][...] = part.astype(BF16)


def total_of(own, parts):
    total = own[...]
    for part in parts:
        total = total + part[...].astype(F32)
    return total


def backward_unit(unit, inverse, upstream):
    along = jnp.sum(unit * upstream, axis=1, keepdims=True)
    return inverse[:, :1] * (upstream - unit * along)


def finish_img_body(scale, unit, inverse, own, *refs):
    *parts, out = refs
    out[...] = backward_unit(
        unit[...], inverse[...], scale[0] * total_of(own, parts)
    ).astype(BF16)


def quarter_copies(partners, place, parts, img_out, img_held, sems):
    rows = parts[0].shape[0]
    copies = []
    for k, (partner, part) in enumerate(zip(partners, parts)):
        img_held[k * rows : (k + 1) * rows, :] = part[...].astype(F32)
        start = pl.multiple_of((place[0] ^ partner) * rows, rows)
        copies.append(
            pltpu.make_async_copy(
                img_held.at[pl.ds(k * rows, rows), :],
                img_out.at[pl.ds(start, rows), :],
                sems.at[k],
            )
        )
        copies[-1].start()
    return copies


def first_body(partners, place, scale, unit, inverse, own, *refs):
    count = len(partners)
    parts = refs[:count]
    *back, img_out, txt_out, img_held, txt_held, sems = refs[count:]
    copies = quarter_copies(partners, place, parts, img_out, img_held, sems)
    txt_held[...] = backward_unit(unit[...], inverse[...], scale[0] * total_of(own, back))
    copies.append(pltpu.make_async_copy(txt_held, txt_out, sems.at[count]))
    copies[-1].start()
    for copy in copies:
        copy.wait()


def last_body(partners, place, begun, *refs):
    del begun
    *parts, img_out, img_held, sems = refs
    for copy in quarter_copies(partners, place, parts, img_out, img_held, sems):
        copy.wait()


def swapped(value, axis, step):
    count = lax.axis_size(axis)
    return lax.ppermute(value, axis, [(s, s ^ step) for s in range(count)])


def local(images, texts, perm, scale, shift):
    rows, width = images.shape
    txt_rows = texts.shape[0]
    line = lax.axis_size("txt")
    blocks = line // 2
    count = lax.axis_size("img")
    part = rows // count
    column = lax.axis_index("txt").reshape(1).astype(jnp.int32)
    place = lax.axis_index("img").reshape(1).astype(jnp.int32)
    perm_row = perm.reshape(1, rows)

    perm_other = swapped(perm_row, "txt", 1)
    raw_other = swapped(images, "txt", 1)
    first = txt_rows // 2
    txt_bf, head, tail, txt_unit, txt_inv = call(
        unit_txt_body,
        [struct(size, width, BF16) for size in (txt_rows, first, txt_rows - first)]
        + [struct(txt_rows, width, F32), struct(txt_rows, 128, F32)],
        [in_hbm(texts)],
        [ANY],
        16 << 20,
        4 * txt_rows * width,
        [pltpu.VMEM((txt_rows, width), F32), pltpu.SemaphoreType.DMA],
    )
    half = blocks // 2
    order = list(range(0, blocks, 2)) + list(range(1, blocks, 2))
    far = [swapped(piece, "txt", 4 * k) for k in range(1, half) for piece in (head, tail)]
    near = [swapped(txt_bf, "txt", 2)]
    for k in range(1, half):
        near += [swapped(far[2 * k - 2], "txt", 2), swapped(tail, "txt", 4 * k + 2)]
    ranks = [0, *(1, 5) * (half - 1), 2, *(3, 4) * (half - 1)]
    stand = sorted(range(len(ranks)), key=lambda k: ranks[k])
    tiles = [([txt_bf] + far + near)[k] for k in stand]
    slots = [stand.index(k) for k in range(len(stand))]
    img_bf, img_other, img_unit, img_inv = call(
        unit_img_body,
        [struct(rows, width, BF16)] * 2 + [struct(part, width, F32), struct(part, 128, F32)],
        [place, raw_other, in_hbm(images)],
        [SMEM, VMEM, ANY],
        24 << 20,
        8 * rows * width,
        [pltpu.VMEM((rows, width), F32), pltpu.SemaphoreType.DMA],
    )
    scalars = [place, column, scale, shift]
    pairs = 2 * rows * blocks * txt_rows * width
    kept, other_img = call(
        functools.partial(other_body, slots, order, line),
        [struct(rows, blocks * txt_rows, BF16), struct(rows, width, BF16)],
        [*scalars, perm_other, img_other, *tiles],
        [SMEM] * 4 + [VMEM] * (2 + len(tiles)),
        40 << 20,
        2 * pairs,
    )
    from_other = swapped(other_img, "txt", 1)
    own_img, own_txt, txt_sums = call(
        functools.partial(own_body, slots, order, line),
        [
            struct(rows, width, F32),
            struct(txt_rows, width, F32),
            struct((blocks - 1) * txt_rows, width, BF16),
        ],
        [*scalars, perm_row, img_bf, img_other, kept, *tiles],
        [SMEM] * 4 + [VMEM] * (4 + len(tiles)),
        40 << 20,
        4 * pairs,
    )
    outs = call(
        functools.partial(split_body, count, blocks - 1),
        [struct(txt_rows, width, BF16)] * (blocks - 1)
        + [struct(part, width, F32)]
        + [struct(part, width, BF16)] * (count - 1),
        [place, own_img, from_other, txt_sums],
        [SMEM] + [VMEM] * 3,
        24 << 20,
        rows * width,
    )
    send_txt, (keep, *send) = outs[: blocks - 1], outs[blocks - 1 :]
    got = [swapped(send[k - 1], "img", k) for k in range(1, count)]
    homes = sorted(zip(order[1:], send_txt), key=lambda pair: pair[0])
    back = [swapped(block, "txt", 2 * k) for k, block in homes]
    (grad_part,) = call(
        finish_img_body,
        [struct(part, width, BF16)],
        [scale, img_unit, img_inv, keep, *got],
        [SMEM] + [VMEM] * (2 + count),
        24 << 20,
        10 * part * width,
    )
    partners = [2, *range(count - 1, 2, -1), 1]
    grads = [grad_part] + [swapped(grad_part, "img", k) for k in partners]
    partners = [0, *partners]
    early = 2
    begun, grad_texts = pl.pallas_call(
        functools.partial(first_body, partners[:early]),
        out_shape=[struct(rows, width, F32), struct(txt_rows, width, F32)],
        in_specs=[SMEM] * 2 + [VMEM] * (2 + early + blocks),
        out_specs=[ANY] * 2,
        scratch_shapes=[
            pltpu.VMEM((early * part, width), F32),
            pltpu.VMEM((txt_rows, width), F32),
            pltpu.SemaphoreType.DMA((early + 1,)),
        ],
        compiler_params=pltpu.CompilerParams(vmem_limit_bytes=24 << 20),
        cost_estimate=pl.CostEstimate(
            flops=10 * txt_rows * width, bytes_accessed=8 * rows * width, transcendentals=0
        ),
    )(place, scale, txt_unit, txt_inv, own_txt, *grads[:early], *back)
    grad_images = pl.pallas_call(
        functools.partial(last_body, partners[early:]),
        out_shape=struct(rows, width, F32),
        in_specs=[SMEM, ANY] + [VMEM] * (count - early),
        out_specs=ANY,
        scratch_shapes=[
            pltpu.VMEM(((count - early) * part, width), F32),
            pltpu.SemaphoreType.DMA((count - early,)),
        ],
        input_output_aliases={1: 0},
        compiler_params=pltpu.CompilerParams(vmem_limit_bytes=24 << 20),
        cost_estimate=pl.CostEstimate(
            flops=rows * width, bytes_accessed=8 * rows * width, transcendentals=0
        ),
    )(place, begun, *grads[early:])
    return (grad_images, grad_texts)


def solution(mesh):
    placed = (P("txt", None), P(("img", "txt"), None), P("txt"), P(), P())
    return jax.shard_map(
        local,
        mesh=mesh,
        in_specs=placed,
        out_specs=(P("txt", None), P(("img", "txt"), None)),
        check_vma=False,
    )
```

```python
import functools

import jax
import jax.numpy as jnp
from jax import lax
from jax.experimental import pallas as pl
from jax.experimental.pallas import tpu as pltpu
from jax.sharding import PartitionSpec as P

EPSILON = 1e-06
F32 = jnp.float32
BF16 = jnp.bfloat16
VMEM = pl.BlockSpec(memory_space=pltpu.VMEM)
ANY = pl.BlockSpec(memory_space=pl.ANY)
SMEM = pl.BlockSpec(memory_space=pltpu.SMEM)


def in_hbm(value):
    return pltpu.with_memory_space_constraint(value, pltpu.HBM)


def call(body, outs, args, specs, limit, flops, scratch=()):
    size = sum(a.size * a.dtype.itemsize for a in args)
    size += sum(o.size * o.dtype.itemsize for o in outs)
    return pl.pallas_call(
        body,
        out_shape=outs,
        in_specs=specs,
        out_specs=[VMEM] * len(outs),
        scratch_shapes=scratch,
        compiler_params=pltpu.CompilerParams(vmem_limit_bytes=limit),
        cost_estimate=pl.CostEstimate(flops=flops, bytes_accessed=size, transcendentals=0),
    )(*args)


def struct(rows, cols, dtype):
    return jax.ShapeDtypeStruct((rows, cols), dtype)


def inverse_norm(values):
    return lax.rsqrt(jnp.sum(values * values, axis=1, keepdims=True) + EPSILON)


def unit_txt_body(source, bf, head, tail, unit_out, inv, held, sem):
    copy = pltpu.make_async_copy(source, held, sem)
    copy.start()
    copy.wait()
    values = held[...]
    inverse = inverse_norm(values)
    unit = values * inverse
    rounded = unit.astype(BF16)
    bf[...] = rounded
    head[...] = rounded[: head.shape[0]]
    tail[...] = rounded[head.shape[0] :]
    unit_out[...] = unit
    inv[...] = jnp.broadcast_to(inverse, inv.shape)


def unit_img_body(place, other, source, bf, other_bf, unit_out, inv, held, sem):
    copy = pltpu.make_async_copy(source, held, sem)
    copy.start()
    values = other[...]
    other_bf[...] = (values * inverse_norm(values)).astype(BF16)
    copy.wait()
    values = held[...]
    bf[...] = (values * inverse_norm(values)).astype(BF16)
    rows = unit_out.shape[0]
    values = held[pl.ds(pl.multiple_of(place[0] * rows, rows), rows), :]
    inverse = inverse_norm(values)
    unit_out[...] = values * inverse
    inv[...] = jnp.broadcast_to(inverse, inv.shape)


def weights_of(tile, order, line, place, column, scale, shift, perm, img):
    rows = tile.shape[0] // len(order)
    row = lax.broadcasted_iota(jnp.int32, (rows, 1), 0)
    ids = jnp.concatenate(
        [row + (place[0] * line + (column[0] ^ (2 * k))) * rows for k in order], axis=0
    )
    products = lax.dot_general(tile, img, (((1,), (1,)), ((), ())), preferred_element_type=F32)
    positive = (ids == perm).astype(F32)
    return (jax.nn.sigmoid(scale[0] * products + shift[0]) - positive).astype(BF16)


def to_images(weights, tile):
    return lax.dot_general(weights, tile, (((0,), (0,)), ((), ())), preferred_element_type=F32)


def to_texts(weights, img):
    return jnp.dot(weights, img, preferred_element_type=F32)


def joined(tiles):
    return jnp.concatenate([t[...] for t in tiles], axis=0)


def other_body(slots, order, line, place, column, scale, shift, perm, img, *refs):
    *txt, kept, out = refs
    tile = joined([txt[k] for k in slots])
    texts, images = tile.shape[0], img.shape[0]
    rows = texts // len(order)
    lane = lax.broadcasted_iota(jnp.int32, (1, texts), 1)
    ids = lane
    for j, k in enumerate(order):
        shift_by = (place[0] * line + (column[0] ^ (2 * k))) * rows - j * rows
        ids = jnp.where(lane // rows == j, lane + shift_by, ids)
    paired = jnp.broadcast_to(perm[...], (128, images)).T[:, :1]
    products = lax.dot_general(
        img[...], tile, (((1,), (1,)), ((), ())), preferred_element_type=F32
    )
    positive = (paired == ids).astype(F32)
    weights = (jax.nn.sigmoid(scale[0] * products + shift[0]) - positive).astype(BF16)
    kept[...] = weights
    out[...] = jnp.dot(weights, tile, preferred_element_type=F32).astype(BF16)


def own_body(slots, order, line, place, column, scale, shift, perm, img, img_other, kept, *refs):
    *txt, own_sum, own_txt, txt_sums = refs
    tile = joined([txt[k] for k in slots])
    weights = weights_of(tile, order, line, place, column, scale, shift, perm[...], img[...])
    own_sum[...] = to_images(weights, tile)
    sums = to_texts(weights, img[...]) + to_images(kept[...], img_other[...])
    rows = own_txt.shape[0]
    own_txt[...] = sums[:rows]
    txt_sums[...] = sums[rows:].astype(BF16)


def split_body(count, blocks, place, own, other, txt_sums, *refs):
    txt_out, (keep, *send) = refs[:blocks], refs[blocks:]
    rows = txt_out[0].shape[0]
    for k, out in enumerate(txt_out):
        out[...] = txt_sums[k * rows : (k + 1) * rows, :]
    rows = keep.shape[0]
    for k in range(count):
        start = pl.multiple_of((place[0] ^ k) * rows, rows)
        part = own[pl.ds(start, rows), :] + other[pl.ds(start, rows), :].astype(F32)
        if k == 0:
            keep[...] = part
        else:
            send[k - 1][...] = part.astype(BF16)


def total_of(own, parts):
    total = own[...]
    for part in parts:
        total = total + part[...].astype(F32)
    return total


def backward_unit(unit, inverse, upstream):
    along = jnp.sum(unit * upstream, axis=1, keepdims=True)
    return inverse[:, :1] * (upstream - unit * along)


def finish_img_body(scale, unit, inverse, own, *refs):
    *parts, out = refs
    out[...] = backward_unit(
        unit[...], inverse[...], scale[0] * total_of(own, parts)
    ).astype(BF16)


def quarter_copies(partners, place, parts, img_out, img_held, sems):
    rows = parts[0].shape[0]
    copies = []
    for k, (partner, part) in enumerate(zip(partners, parts)):
        img_held[k * rows : (k + 1) * rows, :] = part[...].astype(F32)
        start = pl.multiple_of((place[0] ^ partner) * rows, rows)
        copies.append(
            pltpu.make_async_copy(
                img_held.at[pl.ds(k * rows, rows), :],
                img_out.at[pl.ds(start, rows), :],
                sems.at[k],
            )
        )
        copies[-1].start()
    return copies


def first_body(partners, place, scale, unit, inverse, own, *refs):
    count = len(partners)
    parts = refs[:count]
    *back, img_out, txt_out, img_held, txt_held, sems = refs[count:]
    copies = quarter_copies(partners, place, parts, img_out, img_held, sems)
    txt_held[...] = backward_unit(unit[...], inverse[...], scale[0] * total_of(own, back))
    copies.append(pltpu.make_async_copy(txt_held, txt_out, sems.at[count]))
    copies[-1].start()
    for copy in copies:
        copy.wait()


def last_body(partners, place, begun, *refs):
    del begun
    *parts, img_out, img_held, sems = refs
    for copy in quarter_copies(partners, place, parts, img_out, img_held, sems):
        copy.wait()


def swapped(value, axis, step):
    count = lax.axis_size(axis)
    return lax.ppermute(value, axis, [(s, s ^ step) for s in range(count)])


def local(images, texts, perm, scale, shift):
    rows, width = images.shape
    txt_rows = texts.shape[0]
    line = lax.axis_size("txt")
    blocks = line // 2
    count = lax.axis_size("img")
    part = rows // count
    column = lax.axis_index("txt").reshape(1).astype(jnp.int32)
    place = lax.axis_index("img").reshape(1).astype(jnp.int32)
    perm_row = perm.reshape(1, rows)

    perm_other = swapped(perm_row, "txt", 1)
    raw_other = swapped(images, "txt", 1)
    first = txt_rows // 2
    txt_bf, head, tail, txt_unit, txt_inv = call(
        unit_txt_body,
        [struct(size, width, BF16) for size in (txt_rows, first, txt_rows - first)]
        + [struct(txt_rows, width, F32), struct(txt_rows, 128, F32)],
        [in_hbm(texts)],
        [ANY],
        16 << 20,
        4 * txt_rows * width,
        [pltpu.VMEM((txt_rows, width), F32), pltpu.SemaphoreType.DMA],
    )
    half = blocks // 2
    order = list(range(0, blocks, 2)) + list(range(1, blocks, 2))
    far = [swapped(piece, "txt", 4 * k) for k in range(1, half) for piece in (head, tail)]
    near = [swapped(txt_bf, "txt", 2)]
    for k in range(1, half):
        near += [swapped(far[2 * k - 2], "txt", 2), swapped(tail, "txt", 4 * k + 2)]
    ranks = [0, *(1, 5) * (half - 1), 2, *(3, 4) * (half - 1)]
    stand = sorted(range(len(ranks)), key=lambda k: ranks[k])
    tiles = [([txt_bf] + far + near)[k] for k in stand]
    slots = [stand.index(k) for k in range(len(stand))]
    img_bf, img_other, img_unit, img_inv = call(
        unit_img_body,
        [struct(rows, width, BF16)] * 2 + [struct(part, width, F32), struct(part, 128, F32)],
        [place, raw_other, in_hbm(images)],
        [SMEM, VMEM, ANY],
        24 << 20,
        8 * rows * width,
        [pltpu.VMEM((rows, width), F32), pltpu.SemaphoreType.DMA],
    )
    scalars = [place, column, scale, shift]
    pairs = 2 * rows * blocks * txt_rows * width
    kept, other_img = call(
        functools.partial(other_body, slots, order, line),
        [struct(rows, blocks * txt_rows, BF16), struct(rows, width, BF16)],
        [*scalars, perm_other, img_other, *tiles],
        [SMEM] * 4 + [VMEM] * (2 + len(tiles)),
        40 << 20,
        2 * pairs,
    )
    from_other = swapped(other_img, "txt", 1)
    own_img, own_txt, txt_sums = call(
        functools.partial(own_body, slots, order, line),
        [
            struct(rows, width, F32),
            struct(txt_rows, width, F32),
            struct((blocks - 1) * txt_rows, width, BF16),
        ],
        [*scalars, perm_row, img_bf, img_other, kept, *tiles],
        [SMEM] * 4 + [VMEM] * (4 + len(tiles)),
        40 << 20,
        4 * pairs,
    )
    outs = call(
        functools.partial(split_body, count, blocks - 1),
        [struct(txt_rows, width, BF16)] * (blocks - 1)
        + [struct(part, width, F32)]
        + [struct(part, width, BF16)] * (count - 1),
        [place, own_img, from_other, txt_sums],
        [SMEM] + [VMEM] * 3,
        24 << 20,
        rows * width,
    )
    send_txt, (keep, *send) = outs[: blocks - 1], outs[blocks - 1 :]
    got = [swapped(send[k - 1], "img", k) for k in range(1, count)]
    homes = sorted(zip(order[1:], send_txt), key=lambda pair: (pair[0] % 2 == 0, pair[0]))
    back = [swapped(block, "txt", 2 * k) for k, block in homes]
    (grad_part,) = call(
        finish_img_body,
        [struct(part, width, BF16)],
        [scale, img_unit, img_inv, keep, *got],
        [SMEM] + [VMEM] * (2 + count),
        24 << 20,
        10 * part * width,
    )
    partners = [1, *range(count - 1, 1, -1)]
    grads = [grad_part] + [swapped(grad_part, "img", k) for k in partners]
    partners = [0, *partners]
    early = 2
    begun, grad_texts = pl.pallas_call(
        functools.partial(first_body, partners[:early]),
        out_shape=[struct(rows, width, F32), struct(txt_rows, width, F32)],
        in_specs=[SMEM] * 2 + [VMEM] * (2 + early + blocks),
        out_specs=[ANY] * 2,
        scratch_shapes=[
            pltpu.VMEM((early * part, width), F32),
            pltpu.VMEM((txt_rows, width), F32),
            pltpu.SemaphoreType.DMA((early + 1,)),
        ],
        compiler_params=pltpu.CompilerParams(vmem_limit_bytes=24 << 20),
        cost_estimate=pl.CostEstimate(
            flops=10 * txt_rows * width, bytes_accessed=8 * rows * width, transcendentals=0
        ),
    )(place, scale, txt_unit, txt_inv, own_txt, *grads[:early], *back)
    grad_images = pl.pallas_call(
        functools.partial(last_body, partners[early:]),
        out_shape=struct(rows, width, F32),
        in_specs=[SMEM, ANY] + [VMEM] * (count - early),
        out_specs=ANY,
        scratch_shapes=[
            pltpu.VMEM(((count - early) * part, width), F32),
            pltpu.SemaphoreType.DMA((count - early,)),
        ],
        input_output_aliases={1: 0},
        compiler_params=pltpu.CompilerParams(vmem_limit_bytes=24 << 20),
        cost_estimate=pl.CostEstimate(
            flops=rows * width, bytes_accessed=8 * rows * width, transcendentals=0
        ),
    )(place, begun, *grads[early:])
    return (grad_images, grad_texts)


def solution(mesh):
    placed = (P("txt", None), P(("img", "txt"), None), P("txt"), P(), P())
    return jax.shard_map(
        local,
        mesh=mesh,
        in_specs=placed,
        out_specs=(P("txt", None), P(("img", "txt"), None)),
        check_vma=False,
    )
```

```python
import functools

import jax
import jax.numpy as jnp
from jax import lax
from jax.experimental import pallas as pl
from jax.experimental.pallas import tpu as pltpu
from jax.sharding import PartitionSpec as P

EPSILON = 1e-06
F32 = jnp.float32
BF16 = jnp.bfloat16
VMEM = pl.BlockSpec(memory_space=pltpu.VMEM)
ANY = pl.BlockSpec(memory_space=pl.ANY)
SMEM = pl.BlockSpec(memory_space=pltpu.SMEM)


def in_hbm(value):
    return pltpu.with_memory_space_constraint(value, pltpu.HBM)


def call(body, outs, args, specs, limit, flops, scratch=()):
    size = sum(a.size * a.dtype.itemsize for a in args)
    size += sum(o.size * o.dtype.itemsize for o in outs)
    return pl.pallas_call(
        body,
        out_shape=outs,
        in_specs=specs,
        out_specs=[VMEM] * len(outs),
        scratch_shapes=scratch,
        compiler_params=pltpu.CompilerParams(vmem_limit_bytes=limit),
        cost_estimate=pl.CostEstimate(flops=flops, bytes_accessed=size, transcendentals=0),
    )(*args)


def struct(rows, cols, dtype):
    return jax.ShapeDtypeStruct((rows, cols), dtype)


def inverse_norm(values):
    return lax.rsqrt(jnp.sum(values * values, axis=1, keepdims=True) + EPSILON)


def unit_txt_body(source, bf, head, tail, unit_out, inv, held, sem):
    copy = pltpu.make_async_copy(source, held, sem)
    copy.start()
    copy.wait()
    values = held[...]
    inverse = inverse_norm(values)
    unit = values * inverse
    rounded = unit.astype(BF16)
    bf[...] = rounded
    head[...] = rounded[: head.shape[0]]
    tail[...] = rounded[head.shape[0] :]
    unit_out[...] = unit
    inv[...] = jnp.broadcast_to(inverse, inv.shape)


def unit_img_body(place, other, source, bf, other_bf, unit_out, inv, held, sem):
    copy = pltpu.make_async_copy(source, held, sem)
    copy.start()
    values = other[...]
    other_bf[...] = (values * inverse_norm(values)).astype(BF16)
    copy.wait()
    values = held[...]
    bf[...] = (values * inverse_norm(values)).astype(BF16)
    rows = unit_out.shape[0]
    values = held[pl.ds(pl.multiple_of(place[0] * rows, rows), rows), :]
    inverse = inverse_norm(values)
    unit_out[...] = values * inverse
    inv[...] = jnp.broadcast_to(inverse, inv.shape)


def weights_of(tile, order, line, place, column, scale, shift, perm, img):
    rows = tile.shape[0] // len(order)
    row = lax.broadcasted_iota(jnp.int32, (rows, 1), 0)
    ids = jnp.concatenate(
        [row + (place[0] * line + (column[0] ^ (2 * k))) * rows for k in order], axis=0
    )
    products = lax.dot_general(tile, img, (((1,), (1,)), ((), ())), preferred_element_type=F32)
    positive = (ids == perm).astype(F32)
    return (jax.nn.sigmoid(scale[0] * products + shift[0]) - positive).astype(BF16)


def to_images(weights, tile):
    return lax.dot_general(weights, tile, (((0,), (0,)), ((), ())), preferred_element_type=F32)


def to_texts(weights, img):
    return jnp.dot(weights, img, preferred_element_type=F32)


def joined(tiles):
    return jnp.concatenate([t[...] for t in tiles], axis=0)


def other_body(slots, order, line, place, column, scale, shift, perm, img, *refs):
    *txt, kept, out = refs
    tile = joined([txt[k] for k in slots])
    texts, images = tile.shape[0], img.shape[0]
    rows = texts // len(order)
    lane = lax.broadcasted_iota(jnp.int32, (1, texts), 1)
    ids = lane
    for j, k in enumerate(order):
        shift_by = (place[0] * line + (column[0] ^ (2 * k))) * rows - j * rows
        ids = jnp.where(lane // rows == j, lane + shift_by, ids)
    paired = jnp.broadcast_to(perm[...], (128, images)).T[:, :1]
    products = lax.dot_general(
        img[...], tile, (((1,), (1,)), ((), ())), preferred_element_type=F32
    )
    positive = (paired == ids).astype(F32)
    weights = (jax.nn.sigmoid(scale[0] * products + shift[0]) - positive).astype(BF16)
    kept[...] = weights
    out[...] = jnp.dot(weights, tile, preferred_element_type=F32).astype(BF16)


def own_body(slots, order, line, place, column, scale, shift, perm, img, img_other, kept, *refs):
    *txt, own_sum, own_txt, txt_sums = refs
    tile = joined([txt[k] for k in slots])
    weights = weights_of(tile, order, line, place, column, scale, shift, perm[...], img[...])
    own_sum[...] = to_images(weights, tile)
    sums = to_texts(weights, img[...]) + to_images(kept[...], img_other[...])
    rows = own_txt.shape[0]
    own_txt[...] = sums[:rows]
    txt_sums[...] = sums[rows:].astype(BF16)


def split_body(count, blocks, place, own, other, txt_sums, *refs):
    txt_out, (keep, *send) = refs[:blocks], refs[blocks:]
    rows = txt_out[0].shape[0]
    for k, out in enumerate(txt_out):
        out[...] = txt_sums[k * rows : (k + 1) * rows, :]
    rows = keep.shape[0]
    for k in range(count):
        start = pl.multiple_of((place[0] ^ k) * rows, rows)
        part = own[pl.ds(start, rows), :] + other[pl.ds(start, rows), :].astype(F32)
        if k == 0:
            keep[...] = part
        else:
            send[k - 1][...] = part.astype(BF16)


def total_of(own, parts):
    total = own[...]
    for part in parts:
        total = total + part[...].astype(F32)
    return total


def backward_unit(unit, inverse, upstream):
    along = jnp.sum(unit * upstream, axis=1, keepdims=True)
    return inverse[:, :1] * (upstream - unit * along)


def finish_img_body(scale, unit, inverse, own, *refs):
    *parts, out = refs
    out[...] = backward_unit(
        unit[...], inverse[...], scale[0] * total_of(own, parts)
    ).astype(BF16)


def quarter_copies(partners, place, column, parts, img_out, img_held, sems):
    rows = parts[0].shape[0]
    core = column[0] & 1
    copies = []
    for k, ((even, odd), part) in enumerate(zip(partners, parts)):
        img_held[k * rows : (k + 1) * rows, :] = part[...].astype(F32)
        start = pl.multiple_of((place[0] ^ (even + core * (odd - even))) * rows, rows)
        copies.append(
            pltpu.make_async_copy(
                img_held.at[pl.ds(k * rows, rows), :],
                img_out.at[pl.ds(start, rows), :],
                sems.at[k],
            )
        )
        copies[-1].start()
    return copies


def first_body(partners, place, column, scale, unit, inverse, own, *refs):
    count = len(partners)
    parts = refs[:count]
    *back, img_out, txt_out, img_held, txt_held, sems = refs[count:]
    copies = quarter_copies(partners, place, column, parts, img_out, img_held, sems)
    txt_held[...] = backward_unit(unit[...], inverse[...], scale[0] * total_of(own, back))
    copies.append(pltpu.make_async_copy(txt_held, txt_out, sems.at[count]))
    copies[-1].start()
    for copy in copies:
        copy.wait()


def last_body(partners, place, column, begun, *refs):
    del begun
    *parts, img_out, img_held, sems = refs
    for copy in quarter_copies(partners, place, column, parts, img_out, img_held, sems):
        copy.wait()


def swapped(value, axis, step):
    count = lax.axis_size(axis)
    return lax.ppermute(value, axis, [(s, s ^ step) for s in range(count)])


def plane_swapped(value, even, odd):
    count, line = lax.axis_size("img"), lax.axis_size("txt")
    pairs = [
        (i * line + t, (i ^ (odd if t % 2 else even)) * line + t)
        for i in range(count)
        for t in range(line)
    ]
    return lax.ppermute(value, ("img", "txt"), pairs)


def local(images, texts, perm, scale, shift):
    rows, width = images.shape
    txt_rows = texts.shape[0]
    line = lax.axis_size("txt")
    blocks = line // 2
    count = lax.axis_size("img")
    part = rows // count
    column = lax.axis_index("txt").reshape(1).astype(jnp.int32)
    place = lax.axis_index("img").reshape(1).astype(jnp.int32)
    perm_row = perm.reshape(1, rows)

    perm_other = swapped(perm_row, "txt", 1)
    raw_other = swapped(images, "txt", 1)
    first = txt_rows // 2
    txt_bf, head, tail, txt_unit, txt_inv = call(
        unit_txt_body,
        [struct(size, width, BF16) for size in (txt_rows, first, txt_rows - first)]
        + [struct(txt_rows, width, F32), struct(txt_rows, 128, F32)],
        [in_hbm(texts)],
        [ANY],
        16 << 20,
        4 * txt_rows * width,
        [pltpu.VMEM((txt_rows, width), F32), pltpu.SemaphoreType.DMA],
    )
    half = blocks // 2
    order = list(range(0, blocks, 2)) + list(range(1, blocks, 2))
    far = [swapped(piece, "txt", 4 * k) for k in range(1, half) for piece in (head, tail)]
    near = [swapped(txt_bf, "txt", 2)]
    for k in range(1, half):
        near += [swapped(far[2 * k - 2], "txt", 2), swapped(tail, "txt", 4 * k + 2)]
    ranks = [0, *(1, 5) * (half - 1), 2, *(3, 4) * (half - 1)]
    stand = sorted(range(len(ranks)), key=lambda k: ranks[k])
    tiles = [([txt_bf] + far + near)[k] for k in stand]
    slots = [stand.index(k) for k in range(len(stand))]
    img_bf, img_other, img_unit, img_inv = call(
        unit_img_body,
        [struct(rows, width, BF16)] * 2 + [struct(part, width, F32), struct(part, 128, F32)],
        [place, raw_other, in_hbm(images)],
        [SMEM, VMEM, ANY],
        24 << 20,
        8 * rows * width,
        [pltpu.VMEM((rows, width), F32), pltpu.SemaphoreType.DMA],
    )
    scalars = [place, column, scale, shift]
    pairs = 2 * rows * blocks * txt_rows * width
    kept, other_img = call(
        functools.partial(other_body, slots, order, line),
        [struct(rows, blocks * txt_rows, BF16), struct(rows, width, BF16)],
        [*scalars, perm_other, img_other, *tiles],
        [SMEM] * 4 + [VMEM] * (2 + len(tiles)),
        40 << 20,
        2 * pairs,
    )
    from_other = swapped(other_img, "txt", 1)
    own_img, own_txt, txt_sums = call(
        functools.partial(own_body, slots, order, line),
        [
            struct(rows, width, F32),
            struct(txt_rows, width, F32),
            struct((blocks - 1) * txt_rows, width, BF16),
        ],
        [*scalars, perm_row, img_bf, img_other, kept, *tiles],
        [SMEM] * 4 + [VMEM] * (4 + len(tiles)),
        40 << 20,
        4 * pairs,
    )
    outs = call(
        functools.partial(split_body, count, blocks - 1),
        [struct(txt_rows, width, BF16)] * (blocks - 1)
        + [struct(part, width, F32)]
        + [struct(part, width, BF16)] * (count - 1),
        [place, own_img, from_other, txt_sums],
        [SMEM] + [VMEM] * 3,
        24 << 20,
        rows * width,
    )
    send_txt, (keep, *send) = outs[: blocks - 1], outs[blocks - 1 :]
    got = [swapped(send[k - 1], "img", k) for k in range(1, count)]
    homes = sorted(zip(order[1:], send_txt), key=lambda pair: pair[0])
    back = [swapped(block, "txt", 2 * k) for k, block in homes]
    (grad_part,) = call(
        finish_img_body,
        [struct(part, width, BF16)],
        [scale, img_unit, img_inv, keep, *got],
        [SMEM] + [VMEM] * (2 + count),
        24 << 20,
        10 * part * width,
    )
    partners = [(1, 2), *[(k, k) for k in range(count - 1, 2, -1)], (2, 1)]
    grads = [grad_part] + [plane_swapped(grad_part, *pair) for pair in partners]
    partners = [(0, 0), *partners]
    early = 2
    begun, grad_texts = pl.pallas_call(
        functools.partial(first_body, partners[:early]),
        out_shape=[struct(rows, width, F32), struct(txt_rows, width, F32)],
        in_specs=[SMEM] * 3 + [VMEM] * (2 + early + blocks),
        out_specs=[ANY] * 2,
        scratch_shapes=[
            pltpu.VMEM((early * part, width), F32),
            pltpu.VMEM((txt_rows, width), F32),
            pltpu.SemaphoreType.DMA((early + 1,)),
        ],
        compiler_params=pltpu.CompilerParams(vmem_limit_bytes=24 << 20),
        cost_estimate=pl.CostEstimate(
            flops=10 * txt_rows * width, bytes_accessed=8 * rows * width, transcendentals=0
        ),
    )(place, column, scale, txt_unit, txt_inv, own_txt, *grads[:early], *back)
    grad_images = pl.pallas_call(
        functools.partial(last_body, partners[early:]),
        out_shape=struct(rows, width, F32),
        in_specs=[SMEM] * 2 + [ANY] + [VMEM] * (count - early),
        out_specs=ANY,
        scratch_shapes=[
            pltpu.VMEM(((count - early) * part, width), F32),
            pltpu.SemaphoreType.DMA((count - early,)),
        ],
        input_output_aliases={2: 0},
        compiler_params=pltpu.CompilerParams(vmem_limit_bytes=24 << 20),
        cost_estimate=pl.CostEstimate(
            flops=rows * width, bytes_accessed=8 * rows * width, transcendentals=0
        ),
    )(place, column, begun, *grads[early:])
    return (grad_images, grad_texts)


def solution(mesh):
    placed = (P("txt", None), P(("img", "txt"), None), P("txt"), P(), P())
    return jax.shard_map(
        local,
        mesh=mesh,
        in_specs=placed,
        out_specs=(P("txt", None), P(("img", "txt"), None)),
        check_vma=False,
    )
```

```python
import functools

import jax
import jax.numpy as jnp
from jax import lax
from jax.experimental import pallas as pl
from jax.experimental.pallas import tpu as pltpu
from jax.sharding import PartitionSpec as P

EPSILON = 1e-06
F32 = jnp.float32
BF16 = jnp.bfloat16
VMEM = pl.BlockSpec(memory_space=pltpu.VMEM)
ANY = pl.BlockSpec(memory_space=pl.ANY)
SMEM = pl.BlockSpec(memory_space=pltpu.SMEM)


def in_hbm(value):
    return pltpu.with_memory_space_constraint(value, pltpu.HBM)


def call(body, outs, args, specs, limit, flops, scratch=()):
    size = sum(a.size * a.dtype.itemsize for a in args)
    size += sum(o.size * o.dtype.itemsize for o in outs)
    return pl.pallas_call(
        body,
        out_shape=outs,
        in_specs=specs,
        out_specs=[VMEM] * len(outs),
        scratch_shapes=scratch,
        compiler_params=pltpu.CompilerParams(vmem_limit_bytes=limit),
        cost_estimate=pl.CostEstimate(flops=flops, bytes_accessed=size, transcendentals=0),
    )(*args)


def struct(rows, cols, dtype):
    return jax.ShapeDtypeStruct((rows, cols), dtype)


def inverse_norm(values):
    return lax.rsqrt(jnp.sum(values * values, axis=1, keepdims=True) + EPSILON)


def unit_txt_body(source, bf, head, tail, unit_out, inv, held, sem):
    copy = pltpu.make_async_copy(source, held, sem)
    copy.start()
    copy.wait()
    values = held[...]
    inverse = inverse_norm(values)
    unit = values * inverse
    rounded = unit.astype(BF16)
    bf[...] = rounded
    head[...] = rounded[: head.shape[0]]
    tail[...] = rounded[head.shape[0] :]
    unit_out[...] = unit
    inv[...] = jnp.broadcast_to(inverse, inv.shape)


def unit_img_body(place, other, source, bf, other_bf, unit_out, inv, held, sem):
    copy = pltpu.make_async_copy(source, held, sem)
    copy.start()
    values = other[...]
    other_bf[...] = (values * inverse_norm(values)).astype(BF16)
    copy.wait()
    values = held[...]
    bf[...] = (values * inverse_norm(values)).astype(BF16)
    rows = unit_out.shape[0]
    values = held[pl.ds(pl.multiple_of(place[0] * rows, rows), rows), :]
    inverse = inverse_norm(values)
    unit_out[...] = values * inverse
    inv[...] = jnp.broadcast_to(inverse, inv.shape)


def weights_of(tile, order, line, place, column, scale, shift, perm, img):
    rows = tile.shape[0] // len(order)
    row = lax.broadcasted_iota(jnp.int32, (rows, 1), 0)
    ids = jnp.concatenate(
        [row + (place[0] * line + (column[0] ^ (2 * k))) * rows for k in order], axis=0
    )
    products = lax.dot_general(tile, img, (((1,), (1,)), ((), ())), preferred_element_type=F32)
    positive = (ids == perm).astype(F32)
    return (jax.nn.sigmoid(scale[0] * products + shift[0]) - positive).astype(BF16)


def to_images(weights, tile):
    return lax.dot_general(weights, tile, (((0,), (0,)), ((), ())), preferred_element_type=F32)


def to_texts(weights, img):
    return jnp.dot(weights, img, preferred_element_type=F32)


def joined(tiles):
    return jnp.concatenate([t[...] for t in tiles], axis=0)


def other_body(slots, order, line, place, column, scale, shift, perm, img, *refs):
    *txt, kept, out = refs
    tile = joined([txt[k] for k in slots])
    texts, images = tile.shape[0], img.shape[0]
    rows = texts // len(order)
    lane = lax.broadcasted_iota(jnp.int32, (1, texts), 1)
    ids = lane
    for j, k in enumerate(order):
        shift_by = (place[0] * line + (column[0] ^ (2 * k))) * rows - j * rows
        ids = jnp.where(lane // rows == j, lane + shift_by, ids)
    paired = jnp.broadcast_to(perm[...], (128, images)).T[:, :1]
    products = lax.dot_general(
        img[...], tile, (((1,), (1,)), ((), ())), preferred_element_type=F32
    )
    positive = (paired == ids).astype(F32)
    weights = (jax.nn.sigmoid(scale[0] * products + shift[0]) - positive).astype(BF16)
    kept[...] = weights
    out[...] = jnp.dot(weights, tile, preferred_element_type=F32).astype(BF16)


def own_body(slots, order, line, place, column, scale, shift, perm, img, img_other, kept, *refs):
    *txt, own_sum, own_txt, txt_sums = refs
    tile = joined([txt[k] for k in slots])
    weights = weights_of(tile, order, line, place, column, scale, shift, perm[...], img[...])
    own_sum[...] = to_images(weights, tile)
    sums = to_texts(weights, img[...]) + to_images(kept[...], img_other[...])
    rows = own_txt.shape[0]
    own_txt[...] = sums[:rows]
    txt_sums[...] = sums[rows:].astype(BF16)


def split_body(count, blocks, place, own, other, txt_sums, *refs):
    txt_out, (keep, *send) = refs[:blocks], refs[blocks:]
    rows = txt_out[0].shape[0]
    for k, out in enumerate(txt_out):
        out[...] = txt_sums[k * rows : (k + 1) * rows, :]
    rows = keep.shape[0]
    for k in range(count):
        start = pl.multiple_of((place[0] ^ k) * rows, rows)
        part = own[pl.ds(start, rows), :] + other[pl.ds(start, rows), :].astype(F32)
        if k == 0:
            keep[...] = part
        else:
            send[k - 1][...] = part.astype(BF16)


def total_of(own, parts):
    total = own[...]
    for part in parts:
        total = total + part[...].astype(F32)
    return total


def backward_unit(unit, inverse, upstream):
    along = jnp.sum(unit * upstream, axis=1, keepdims=True)
    return inverse[:, :1] * (upstream - unit * along)


def finish_img_body(scale, unit, inverse, own, *refs):
    *parts, out = refs
    out[...] = backward_unit(
        unit[...], inverse[...], scale[0] * total_of(own, parts)
    ).astype(BF16)


def quarter_copies(partners, place, parts, img_out, img_held, sems):
    rows = parts[0].shape[0]
    copies = []
    for k, (partner, part) in enumerate(zip(partners, parts)):
        img_held[k * rows : (k + 1) * rows, :] = part[...].astype(F32)
        start = pl.multiple_of((place[0] ^ partner) * rows, rows)
        copies.append(
            pltpu.make_async_copy(
                img_held.at[pl.ds(k * rows, rows), :],
                img_out.at[pl.ds(start, rows), :],
                sems.at[k],
            )
        )
        copies[-1].start()
    return copies


def first_body(count, scale, unit, inverse, own, *refs):
    parts = refs[:count]
    *back, img_out, txt_out = refs[count:]
    rows = parts[0].shape[0]
    for k, part in enumerate(parts):
        img_out[k * rows : (k + 1) * rows, :] = part[...].astype(F32)
    txt_out[...] = backward_unit(unit[...], inverse[...], scale[0] * total_of(own, back))


def last_body(early, partners, place, ready, grad_txt, *refs):
    *parts, img_out, txt_out, img_held, sems = refs
    rows = parts[0].shape[0]
    copies = [pltpu.make_async_copy(grad_txt, txt_out, sems.at[len(parts)])]
    for k, partner in enumerate(early):
        start = pl.multiple_of((place[0] ^ partner) * rows, rows)
        copies.append(
            pltpu.make_async_copy(
                ready.at[pl.ds(k * rows, rows), :],
                img_out.at[pl.ds(start, rows), :],
                sems.at[len(parts) + 1 + k],
            )
        )
    for copy in copies:
        copy.start()
    copies += quarter_copies(partners, place, parts, img_out, img_held, sems)
    for copy in copies:
        copy.wait()


def swapped(value, axis, step):
    count = lax.axis_size(axis)
    return lax.ppermute(value, axis, [(s, s ^ step) for s in range(count)])


def local(images, texts, perm, scale, shift):
    rows, width = images.shape
    txt_rows = texts.shape[0]
    line = lax.axis_size("txt")
    blocks = line // 2
    count = lax.axis_size("img")
    part = rows // count
    column = lax.axis_index("txt").reshape(1).astype(jnp.int32)
    place = lax.axis_index("img").reshape(1).astype(jnp.int32)
    perm_row = perm.reshape(1, rows)

    perm_other = swapped(perm_row, "txt", 1)
    raw_other = swapped(images, "txt", 1)
    first = txt_rows // 2
    txt_bf, head, tail, txt_unit, txt_inv = call(
        unit_txt_body,
        [struct(size, width, BF16) for size in (txt_rows, first, txt_rows - first)]
        + [struct(txt_rows, width, F32), struct(txt_rows, 128, F32)],
        [in_hbm(texts)],
        [ANY],
        16 << 20,
        4 * txt_rows * width,
        [pltpu.VMEM((txt_rows, width), F32), pltpu.SemaphoreType.DMA],
    )
    half = blocks // 2
    order = list(range(0, blocks, 2)) + list(range(1, blocks, 2))
    far = [swapped(piece, "txt", 4 * k) for k in range(1, half) for piece in (head, tail)]
    near = [swapped(txt_bf, "txt", 2)]
    for k in range(1, half):
        near += [swapped(far[2 * k - 2], "txt", 2), swapped(tail, "txt", 4 * k + 2)]
    ranks = [0, *(1, 5) * (half - 1), 2, *(3, 4) * (half - 1)]
    stand = sorted(range(len(ranks)), key=lambda k: ranks[k])
    tiles = [([txt_bf] + far + near)[k] for k in stand]
    slots = [stand.index(k) for k in range(len(stand))]
    img_bf, img_other, img_unit, img_inv = call(
        unit_img_body,
        [struct(rows, width, BF16)] * 2 + [struct(part, width, F32), struct(part, 128, F32)],
        [place, raw_other, in_hbm(images)],
        [SMEM, VMEM, ANY],
        24 << 20,
        8 * rows * width,
        [pltpu.VMEM((rows, width), F32), pltpu.SemaphoreType.DMA],
    )
    scalars = [place, column, scale, shift]
    pairs = 2 * rows * blocks * txt_rows * width
    kept, other_img = call(
        functools.partial(other_body, slots, order, line),
        [struct(rows, blocks * txt_rows, BF16), struct(rows, width, BF16)],
        [*scalars, perm_other, img_other, *tiles],
        [SMEM] * 4 + [VMEM] * (2 + len(tiles)),
        40 << 20,
        2 * pairs,
    )
    from_other = swapped(other_img, "txt", 1)
    own_img, own_txt, txt_sums = call(
        functools.partial(own_body, slots, order, line),
        [
            struct(rows, width, F32),
            struct(txt_rows, width, F32),
            struct((blocks - 1) * txt_rows, width, BF16),
        ],
        [*scalars, perm_row, img_bf, img_other, kept, *tiles],
        [SMEM] * 4 + [VMEM] * (4 + len(tiles)),
        40 << 20,
        4 * pairs,
    )
    outs = call(
        functools.partial(split_body, count, blocks - 1),
        [struct(txt_rows, width, BF16)] * (blocks - 1)
        + [struct(part, width, F32)]
        + [struct(part, width, BF16)] * (count - 1),
        [place, own_img, from_other, txt_sums],
        [SMEM] + [VMEM] * 3,
        24 << 20,
        rows * width,
    )
    send_txt, (keep, *send) = outs[: blocks - 1], outs[blocks - 1 :]
    got = [swapped(send[k - 1], "img", k) for k in range(1, count)]
    homes = sorted(zip(order[1:], send_txt), key=lambda pair: pair[0])
    back = [swapped(block, "txt", 2 * k) for k, block in homes]
    (grad_part,) = call(
        finish_img_body,
        [struct(part, width, BF16)],
        [scale, img_unit, img_inv, keep, *got],
        [SMEM] + [VMEM] * (2 + count),
        24 << 20,
        10 * part * width,
    )
    partners = [1, *range(count - 1, 1, -1)]
    grads = [grad_part] + [swapped(grad_part, "img", k) for k in partners]
    partners = [0, *partners]
    early = 2
    ready, grad_txt = call(
        functools.partial(first_body, early),
        [struct(early * part, width, F32), struct(txt_rows, width, F32)],
        [scale, txt_unit, txt_inv, own_txt, *grads[:early], *back],
        [SMEM] + [VMEM] * (2 + early + blocks),
        24 << 20,
        10 * txt_rows * width,
    )
    return pl.pallas_call(
        functools.partial(last_body, partners[:early], partners[early:]),
        out_shape=[struct(rows, width, F32), struct(txt_rows, width, F32)],
        in_specs=[SMEM] + [VMEM] * (2 + count - early),
        out_specs=[ANY] * 2,
        scratch_shapes=[
            pltpu.VMEM(((count - early) * part, width), F32),
            pltpu.SemaphoreType.DMA((count + 1,)),
        ],
        compiler_params=pltpu.CompilerParams(vmem_limit_bytes=24 << 20),
        cost_estimate=pl.CostEstimate(
            flops=rows * width, bytes_accessed=8 * rows * width, transcendentals=0
        ),
    )(place, ready, grad_txt, *grads[early:])


def solution(mesh):
    placed = (P("txt", None), P(("img", "txt"), None), P("txt"), P(), P())
    return jax.shard_map(
        local,
        mesh=mesh,
        in_specs=placed,
        out_specs=(P("txt", None), P(("img", "txt"), None)),
        check_vma=False,
    )
```

```python
import functools

import jax
import jax.numpy as jnp
from jax import lax
from jax.experimental import pallas as pl
from jax.experimental.pallas import tpu as pltpu
from jax.sharding import PartitionSpec as P

EPSILON = 1e-06
F32 = jnp.float32
BF16 = jnp.bfloat16
VMEM = pl.BlockSpec(memory_space=pltpu.VMEM)
ANY = pl.BlockSpec(memory_space=pl.ANY)
SMEM = pl.BlockSpec(memory_space=pltpu.SMEM)


def in_hbm(value):
    return pltpu.with_memory_space_constraint(value, pltpu.HBM)


def call(body, outs, args, specs, limit, flops, scratch=()):
    size = sum(a.size * a.dtype.itemsize for a in args)
    size += sum(o.size * o.dtype.itemsize for o in outs)
    return pl.pallas_call(
        body,
        out_shape=outs,
        in_specs=specs,
        out_specs=[VMEM] * len(outs),
        scratch_shapes=scratch,
        compiler_params=pltpu.CompilerParams(vmem_limit_bytes=limit),
        cost_estimate=pl.CostEstimate(flops=flops, bytes_accessed=size, transcendentals=0),
    )(*args)


def struct(rows, cols, dtype):
    return jax.ShapeDtypeStruct((rows, cols), dtype)


def inverse_norm(values):
    return lax.rsqrt(jnp.sum(values * values, axis=1, keepdims=True) + EPSILON)


def unit_txt_body(source, bf, head, tail, unit_out, inv, held, sem):
    copy = pltpu.make_async_copy(source, held, sem)
    copy.start()
    copy.wait()
    values = held[...]
    inverse = inverse_norm(values)
    unit = values * inverse
    rounded = unit.astype(BF16)
    bf[...] = rounded
    head[...] = rounded[: head.shape[0]]
    tail[...] = rounded[head.shape[0] :]
    unit_out[...] = unit
    inv[...] = jnp.broadcast_to(inverse, inv.shape)


def unit_img_body(place, other, source, bf, other_bf, unit_out, inv, held, sem):
    copy = pltpu.make_async_copy(source, held, sem)
    copy.start()
    values = other[...]
    other_bf[...] = (values * inverse_norm(values)).astype(BF16)
    copy.wait()
    values = held[...]
    bf[...] = (values * inverse_norm(values)).astype(BF16)
    rows = unit_out.shape[0]
    values = held[pl.ds(pl.multiple_of(place[0] * rows, rows), rows), :]
    inverse = inverse_norm(values)
    unit_out[...] = values * inverse
    inv[...] = jnp.broadcast_to(inverse, inv.shape)


def weights_of(tile, order, line, place, column, scale, shift, perm, img):
    rows = tile.shape[0] // len(order)
    row = lax.broadcasted_iota(jnp.int32, (rows, 1), 0)
    ids = jnp.concatenate(
        [row + (place[0] * line + (column[0] ^ (2 * k))) * rows for k in order], axis=0
    )
    products = lax.dot_general(tile, img, (((1,), (1,)), ((), ())), preferred_element_type=F32)
    positive = (ids == perm).astype(F32)
    return (jax.nn.sigmoid(scale[0] * products + shift[0]) - positive).astype(BF16)


def to_images(weights, tile):
    return lax.dot_general(weights, tile, (((0,), (0,)), ((), ())), preferred_element_type=F32)


def to_texts(weights, img):
    return jnp.dot(weights, img, preferred_element_type=F32)


def joined(tiles):
    return jnp.concatenate([t[...] for t in tiles], axis=0)


def other_body(slots, order, line, place, column, scale, shift, perm, img, *refs):
    *txt, kept, out = refs
    tile = joined([txt[k] for k in slots])
    texts, images = tile.shape[0], img.shape[0]
    rows = texts // len(order)
    lane = lax.broadcasted_iota(jnp.int32, (1, texts), 1)
    ids = lane
    for j, k in enumerate(order):
        shift_by = (place[0] * line + (column[0] ^ (2 * k))) * rows - j * rows
        ids = jnp.where(lane // rows == j, lane + shift_by, ids)
    paired = jnp.broadcast_to(perm[...], (128, images)).T[:, :1]
    products = lax.dot_general(
        img[...], tile, (((1,), (1,)), ((), ())), preferred_element_type=F32
    )
    positive = (paired == ids).astype(F32)
    weights = (jax.nn.sigmoid(scale[0] * products + shift[0]) - positive).astype(BF16)
    kept[...] = weights
    out[...] = jnp.dot(weights, tile, preferred_element_type=F32).astype(BF16)


def own_body(slots, order, line, place, column, scale, shift, perm, img, img_other, kept, *refs):
    *txt, own_sum, own_txt, txt_sums = refs
    tile = joined([txt[k] for k in slots])
    weights = weights_of(tile, order, line, place, column, scale, shift, perm[...], img[...])
    own_sum[...] = to_images(weights, tile)
    sums = to_texts(weights, img[...]) + to_images(kept[...], img_other[...])
    rows = own_txt.shape[0]
    own_txt[...] = sums[:rows]
    txt_sums[...] = sums[rows:].astype(BF16)


def split_body(count, blocks, place, own, other, txt_sums, *refs):
    txt_out, (keep, *send) = refs[:blocks], refs[blocks:]
    rows = txt_out[0].shape[0]
    for k, out in enumerate(txt_out):
        out[...] = txt_sums[k * rows : (k + 1) * rows, :]
    rows = keep.shape[0]
    for k in range(count):
        start = pl.multiple_of((place[0] ^ k) * rows, rows)
        part = own[pl.ds(start, rows), :] + other[pl.ds(start, rows), :].astype(F32)
        if k == 0:
            keep[...] = part
        else:
            send[k - 1][...] = part.astype(BF16)


def total_of(own, parts):
    total = own[...]
    for part in parts:
        total = total + part[...].astype(F32)
    return total


def backward_unit(unit, inverse, upstream):
    along = jnp.sum(unit * upstream, axis=1, keepdims=True)
    return inverse[:, :1] * (upstream - unit * along)


def finish_img_body(scale, unit, inverse, own, *refs):
    *parts, out = refs
    out[...] = backward_unit(
        unit[...], inverse[...], scale[0] * total_of(own, parts)
    ).astype(BF16)


def quarter_copies(partners, place, parts, img_out, img_held, sems):
    rows = parts[0].shape[0]
    copies = []
    for k, (partner, part) in enumerate(zip(partners, parts)):
        img_held[k * rows : (k + 1) * rows, :] = part[...].astype(F32)
        start = pl.multiple_of((place[0] ^ partner) * rows, rows)
        copies.append(
            pltpu.make_async_copy(
                img_held.at[pl.ds(k * rows, rows), :],
                img_out.at[pl.ds(start, rows), :],
                sems.at[k],
            )
        )
        copies[-1].start()
    return copies


def first_body(count, scale, unit, inverse, own, *refs):
    parts = refs[:count]
    *back, img_out, txt_out = refs[count:]
    rows = parts[0].shape[0]
    for k, part in enumerate(parts):
        img_out[k * rows : (k + 1) * rows, :] = part[...].astype(F32)
    txt_out[...] = backward_unit(unit[...], inverse[...], scale[0] * total_of(own, back))


def last_body(early, partners, place, ready, grad_txt, *refs):
    *parts, img_out, txt_out, img_held, sems = refs
    rows = parts[0].shape[0]
    copies = [pltpu.make_async_copy(grad_txt, txt_out, sems.at[len(parts)])]
    for k, partner in enumerate(early):
        start = pl.multiple_of((place[0] ^ partner) * rows, rows)
        copies.append(
            pltpu.make_async_copy(
                ready.at[pl.ds(k * rows, rows), :],
                img_out.at[pl.ds(start, rows), :],
                sems.at[len(parts) + 1 + k],
            )
        )
    for copy in copies:
        copy.start()
    copies += quarter_copies(partners, place, parts, img_out, img_held, sems)
    for copy in copies:
        copy.wait()


def swapped(value, axis, step):
    count = lax.axis_size(axis)
    return lax.ppermute(value, axis, [(s, s ^ step) for s in range(count)])


def local(images, texts, perm, scale, shift):
    rows, width = images.shape
    txt_rows = texts.shape[0]
    line = lax.axis_size("txt")
    blocks = line // 2
    count = lax.axis_size("img")
    part = rows // count
    column = lax.axis_index("txt").reshape(1).astype(jnp.int32)
    place = lax.axis_index("img").reshape(1).astype(jnp.int32)
    perm_row = perm.reshape(1, rows)

    perm_other = swapped(perm_row, "txt", 1)
    raw_other = swapped(images, "txt", 1)
    first = txt_rows // 2
    txt_bf, head, tail, txt_unit, txt_inv = call(
        unit_txt_body,
        [struct(size, width, BF16) for size in (txt_rows, first, txt_rows - first)]
        + [struct(txt_rows, width, F32), struct(txt_rows, 128, F32)],
        [in_hbm(texts)],
        [ANY],
        16 << 20,
        4 * txt_rows * width,
        [pltpu.VMEM((txt_rows, width), F32), pltpu.SemaphoreType.DMA],
    )
    half = blocks // 2
    order = list(range(0, blocks, 2)) + list(range(1, blocks, 2))
    far = [swapped(piece, "txt", 4 * k) for k in range(1, half) for piece in (head, tail)]
    near = [swapped(txt_bf, "txt", 2)]
    for k in range(1, half):
        near += [swapped(far[2 * k - 2], "txt", 2), swapped(tail, "txt", 4 * k + 2)]
    ranks = [0, *(1, 5) * (half - 1), 2, *(3, 4) * (half - 1)]
    stand = sorted(range(len(ranks)), key=lambda k: ranks[k])
    tiles = [([txt_bf] + far + near)[k] for k in stand]
    slots = [stand.index(k) for k in range(len(stand))]
    img_bf, img_other, img_unit, img_inv = call(
        unit_img_body,
        [struct(rows, width, BF16)] * 2 + [struct(part, width, F32), struct(part, 128, F32)],
        [place, raw_other, in_hbm(images)],
        [SMEM, VMEM, ANY],
        24 << 20,
        8 * rows * width,
        [pltpu.VMEM((rows, width), F32), pltpu.SemaphoreType.DMA],
    )
    scalars = [place, column, scale, shift]
    pairs = 2 * rows * blocks * txt_rows * width
    kept, other_img = call(
        functools.partial(other_body, slots, order, line),
        [struct(rows, blocks * txt_rows, BF16), struct(rows, width, BF16)],
        [*scalars, perm_other, img_other, *tiles],
        [SMEM] * 4 + [VMEM] * (2 + len(tiles)),
        40 << 20,
        2 * pairs,
    )
    from_other = swapped(other_img, "txt", 1)
    own_img, own_txt, txt_sums = call(
        functools.partial(own_body, slots, order, line),
        [
            struct(rows, width, F32),
            struct(txt_rows, width, F32),
            struct((blocks - 1) * txt_rows, width, BF16),
        ],
        [*scalars, perm_row, img_bf, img_other, kept, *tiles],
        [SMEM] * 4 + [VMEM] * (4 + len(tiles)),
        40 << 20,
        4 * pairs,
    )
    outs = call(
        functools.partial(split_body, count, blocks - 1),
        [struct(txt_rows, width, BF16)] * (blocks - 1)
        + [struct(part, width, F32)]
        + [struct(part, width, BF16)] * (count - 1),
        [place, own_img, from_other, txt_sums],
        [SMEM] + [VMEM] * 3,
        24 << 20,
        rows * width,
    )
    send_txt, (keep, *send) = outs[: blocks - 1], outs[blocks - 1 :]
    got = [swapped(send[k - 1], "img", k) for k in range(1, count)]
    homes = sorted(zip(order[1:], send_txt), key=lambda pair: pair[0])
    back = [swapped(block, "txt", 2 * k) for k, block in homes]
    (grad_part,) = call(
        finish_img_body,
        [struct(part, width, BF16)],
        [scale, img_unit, img_inv, keep, *got],
        [SMEM] + [VMEM] * (2 + count),
        24 << 20,
        10 * part * width,
    )
    partners = list(range(count - 1, 0, -1))
    grads = [grad_part] + [swapped(grad_part, "img", k) for k in partners]
    partners = [0, *partners]
    early = 2
    ready, grad_txt = call(
        functools.partial(first_body, early),
        [struct(early * part, width, F32), struct(txt_rows, width, F32)],
        [scale, txt_unit, txt_inv, own_txt, *grads[:early], *back],
        [SMEM] + [VMEM] * (2 + early + blocks),
        24 << 20,
        10 * txt_rows * width,
    )
    return pl.pallas_call(
        functools.partial(last_body, partners[:early], partners[early:]),
        out_shape=[struct(rows, width, F32), struct(txt_rows, width, F32)],
        in_specs=[SMEM] + [VMEM] * (2 + count - early),
        out_specs=[ANY] * 2,
        scratch_shapes=[
            pltpu.VMEM(((count - early) * part, width), F32),
            pltpu.SemaphoreType.DMA((count + 1,)),
        ],
        compiler_params=pltpu.CompilerParams(vmem_limit_bytes=24 << 20),
        cost_estimate=pl.CostEstimate(
            flops=rows * width, bytes_accessed=8 * rows * width, transcendentals=0
        ),
    )(place, ready, grad_txt, *grads[early:])


def solution(mesh):
    placed = (P("txt", None), P(("img", "txt"), None), P("txt"), P(), P())
    return jax.shard_map(
        local,
        mesh=mesh,
        in_specs=placed,
        out_specs=(P("txt", None), P(("img", "txt"), None)),
        check_vma=False,
    )
```
